32 devices in a mesh: dp: 8 (over y, x, core), tensor: 4 (over z).
Axes of the slice: x: 2, y: 2, z: 4, core: 2. Of those that a mesh axis runs over, the one named last changes fastest.
Arguments:
- images: bfloat16 [24, 196, 768], P('dp'), may hold values from -6 to 6
- cotangent: bfloat16 [24, 196, 768], P('dp'), may hold values from -6 to 6
- norm_gains: bfloat16 [2, 768], P(None, 'dp'), may hold values from 0.099609375 to 1.8984375
- norm_shifts: bfloat16 [2, 768], P(None, 'dp'), may hold values from -1.5 to 1.5
- tok_in: bfloat16 [196, 384], P(None, 'dp'), may hold values from -0.4375 to 0.4375
- tok_out_t: bfloat16 [196, 384], P(None, 'dp'), may hold values from -0.3125 to 0.3125
- tok_bias_in: bfloat16 [1, 384], P(None, 'dp'), may hold values from -1.5 to 1.5
- tok_bias_out: bfloat16 [196], replicated, may hold values from -1.5 to 1.5
- w_in: bfloat16 [768, 3072], P(None, 'tensor'), may hold values from -0.21875 to 0.21875
- bias_in: bfloat16 [3072], P('tensor'), may hold values from -1.5 to 1.5
- w_out: bfloat16 [3072, 768], P('tensor'), may hold values from -0.109375 to 0.109375
- bias_out: bfloat16 [768], replicated, may hold values from -1.5 to 1.5
Outputs:
- activations: bfloat16 [24, 196, 768], P('dp')
- input_grad: bfloat16 [24, 196, 768], P('dp')
- grad_norm_gains: float32 [2, 768], P(None, 'dp')
- grad_norm_shifts: float32 [2, 768], P(None, 'dp')
- grad_tok_in: float32 [196, 384], P(None, 'dp')
- grad_tok_out_t: float32 [196, 384], P(None, 'dp')
- grad_tok_bias_in: float32 [1, 384], P(None, 'dp')
- grad_tok_bias_out: float32 [196], replicated
- grad_w_in: float32 [768, 3072], P('dp', 'tensor')
- grad_bias_in: float32 [3072], P(('tensor', 'dp'))
- grad_w_out: float32 [3072, 768], P('tensor', 'dp')
- grad_bias_out: float32 [768], P('dp')
- sqnorms: float32 [24], P('dp')
- influence: float32 [8, 16], P(None, 'dp')
The draws below stay inside these ranges and needn't reach their ends.
All inputs are finite; a program needn't handle non-finite values.
Results may differ from the reference program's by a relative error of at most 0.0073.
Values may be sent and summed in bfloat16 or wider, within the bound.
A program may use at most 512 MiB of HBM per device.

```python
import jax
import jax.numpy as jnp
import numpy as np
from jax import lax

D = 768
FF = 3072
PATCHES = 196
TOK_HID = 384
QRY_DEV = 1
IMG_DEV = 3
IMAGES = 24
N_DP = 8


def strengthened(entries, key, source, target, blocks, factor):
    def block_of(dim):
        return (jnp.arange(entries.shape[dim]) // (entries.shape[dim] // blocks)).reshape((-1,) + (1,) * (entries.ndim - 1 - dim))

    one_side = jax.random.permutation(key, blocks)[block_of(target)]
    far = (block_of(target) + blocks // 2) % blocks
    return jnp.where((block_of(source) == one_side) | (block_of(source) == far), factor * entries, entries)


def steps_of(stream_key, extent, pieces, smallest, largest):
    level = 1.0
    for axis_at, parts in pieces:
        draws = jax.random.uniform(jax.random.fold_in(jax.random.fold_in(stream_key, 6), axis_at), (parts,), jnp.float32, smallest / len(pieces), largest / len(pieces))
        level = level * jnp.repeat(jnp.exp(draws), extent[axis_at] // parts).reshape((-1,) + (1,) * (len(extent) - 1 - axis_at))
    return level


def centred(rng, extent, deviation, limit, cuts=(), kind=jnp.bfloat16):
    array = deviation * jax.random.normal(rng, extent, jnp.float32)
    if cuts:
        array = array * steps_of(rng, extent, cuts, -0.22, 0.18)
    return jnp.clip(array, -limit, limit).astype(kind)


def heavy_noise(rng, dims, deviation, most, pieces, heavy, kind=jnp.bfloat16):
    values = deviation * jax.random.normal(rng, dims, jnp.float32)
    if pieces:
        values = values * steps_of(rng, dims, pieces, -0.22, 0.18)
    return jnp.clip(strengthened(values, jax.random.fold_in(rng, 3), *heavy), -most, most).astype(kind)


def setup_inputs(seed: int = 0) -> dict:
    keys = jax.random.split(jax.random.key(seed), 13)
    return {
        "images": centred(keys[0], (IMAGES, PATCHES, D), 1.0, 6.0, ((0, 8),)),
        "cotangent": heavy_noise(keys[1], (IMAGES, PATCHES, D), 1.0, 6.0, ((0, 8),), (0, 2, 8, 2.0)),
        "norm_gains": jnp.clip(1.0 + 0.18 * jax.random.normal(keys[2], (2, D), jnp.float32), 0.099609375, 1.8984375).astype(jnp.bfloat16),
        "norm_shifts": centred(keys[3], (2, D), 0.3, 1.5, ((1, 8),)),
        "tok_in": centred(keys[4], (PATCHES, TOK_HID), PATCHES ** -0.5, 0.4375, ((1, 8),)),
        "tok_out_t": centred(keys[5], (PATCHES, TOK_HID), TOK_HID ** -0.5, 0.3125, ((1, 8),)),
        "tok_bias_in": centred(keys[6], (1, TOK_HID), 0.3, 1.5, ((1, 8),)),
        "tok_bias_out": centred(keys[7], (PATCHES,), 0.3, 1.5),
        "w_in": centred(keys[8], (D, FF), D ** -0.5, 0.21875, ((1, 4),)),
        "bias_in": centred(keys[9], (FF,), 0.3, 1.5, ((0, 4),)),
        "w_out": centred(keys[10], (FF, D), FF ** -0.5, 0.109375, ((0, 4),)),
        "bias_out": centred(keys[11], (D,), 0.3, 1.5),
    }


@jax.custom_vjp
def low(v):
    return lax.optimization_barrier(v.astype(jnp.bfloat16)).astype(jnp.float32)

@jax.custom_vjp
def low_back(v):
    return v

def low_keep(v):
    return (low(v), None)

def low_pass(kept, grad):
    return (grad,)

def back_keep(v):
    return (v, None)

def back_low(kept, grad):
    return (low(grad),)
low.defvjp(low_keep, low_pass)
low_back.defvjp(back_keep, back_low)
HIGH = lax.Precision.HIGHEST

def layer_norm(values, gain, shift):
    center = values - lax.optimization_barrier(jnp.mean(values, axis=-1, keepdims=True))
    spread = lax.optimization_barrier(jnp.mean(center * center, axis=-1, keepdims=True))
    return center * lax.rsqrt(spread + 1e-06) * gain + shift

def smooth(values):
    return jax.nn.gelu(values, approximate=True)

def forward(image, gains, shifts, tok_in, tok_out_t, tok_bias_in, tok_bias_out, w_in, bias_in, w_out, bias_out):
    normed_one = low(layer_norm(image, gains[0], shifts[0]))
    tok_pre = low_back(jnp.einsum('sk,sd->kd', tok_in, normed_one, precision=HIGH) + tok_bias_in[0][:, None])
    tok_hidden = low(smooth(tok_pre))
    tok_mixed = low_back(jnp.einsum('sk,kd->sd', tok_out_t, tok_hidden, precision=HIGH) + tok_bias_out[:, None])
    resid = image + tok_mixed
    chan_in = low(layer_norm(resid, gains[1], shifts[1]))
    chan_pre = low_back(jnp.dot(chan_in, w_in, precision=HIGH, preferred_element_type=jnp.float32) + bias_in)
    hidden = low(smooth(chan_pre))
    return resid + jnp.dot(hidden, w_out, precision=HIGH, preferred_element_type=jnp.float32) + bias_out

def reference(images, cotangent, norm_gains, norm_shifts, tok_in, tok_out_t, tok_bias_in, tok_bias_out, w_in, bias_in, w_out, bias_out):
    params = tuple((p.astype(jnp.float32) for p in (norm_gains, norm_shifts, tok_in, tok_out_t, tok_bias_in, tok_bias_out, w_in, bias_in, w_out, bias_out)))
    inputs = images.astype(jnp.float32)
    douts = cotangent.astype(jnp.float32)

    def single(image, dout):
        result, back = jax.vjp(forward, image, *params)
        return (result, back(dout))

    def step(totals, item):
        result, grads = single(item[0], item[1])
        squares = jnp.sum(grads[7] * grads[7]) + jnp.sum(grads[9] * grads[9])
        totals = tuple((a + b for a, b in zip(totals, grads[1:])))
        return (totals, (result, grads[0], squares))
    zeros = tuple((jnp.zeros_like(p) for p in params))
    totals, (results, dinputs, squares) = lax.scan(step, zeros, (inputs, douts))
    order = np.arange(N_DP * IMG_DEV).reshape(N_DP, IMG_DEV)
    query_rows = order[:, :QRY_DEV].reshape(-1)
    train_rows = order[:, QRY_DEV:].reshape(-1)

    def weight_grads(item):
        result, grads = single(item[0], item[1])
        return (grads[7], grads[9])
    query_in, query_out = lax.map(weight_grads, (inputs[query_rows], douts[query_rows]))

    def against(item):
        grad_in, grad_out = weight_grads(item)
        return lax.optimization_barrier(jnp.sum(grad_in[None] * query_in, axis=(1, 2))) + lax.optimization_barrier(jnp.sum(grad_out[None] * query_out, axis=(1, 2)))
    scores = lax.map(against, (inputs[train_rows], douts[train_rows]))
    sqnorms = squares / (2.0 * D * FF)
    influence = scores.T * (2.0 * D * FF) ** (-0.5)
    return (results.astype(jnp.bfloat16), dinputs.astype(jnp.bfloat16), totals[0], totals[1], totals[2], totals[3], totals[4], totals[5], totals[6], totals[7], totals[8], totals[9], sqnorms, influence)
```

```python
import functools

import jax
import jax.numpy as jnp
from jax import lax
from jax.experimental import pallas as pl
from jax.experimental.pallas import tpu as pltpu
from jax.sharding import PartitionSpec as P

D = 768
FF = 3072
QRY_DEV = 1
HIGH = lax.Precision.HIGHEST
MESH = pl.DeviceIdType.MESH
F32 = jnp.float32
BF16 = jnp.bfloat16

ROWS = 208
CHUNK = 48
LAG = 2
C1 = 0.7978845608028654
C2 = 0.044715


def dot_nn(a, b):
    return lax.dot_general(a, b, (((1,), (0,)), ((), ())), preferred_element_type=F32)


def dot_nt(a, b):
    return lax.dot_general(a, b, (((1,), (1,)), ((), ())), preferred_element_type=F32)


def dot_tn(a, b):
    return lax.dot_general(a, b, (((0,), (0,)), ((), ())), preferred_element_type=F32)


def gelu_pair(v):
    u = v * v
    th = jnp.tanh(v * (C1 + (C1 * C2) * u))
    hp = 0.5 + 0.5 * th
    value = v * hp
    slope = hp + (0.5 * v) * (1.0 - th * th) * (C1 + (3.0 * C1 * C2) * u)
    return value, slope


def fold(v):
    out = v[0:8]
    for s in range(8, v.shape[0], 8):
        out = out + v[s : s + 8]
    return out


def mega(
    n_dp,
    count,
    patches,
    toks,
    images,
    cotangent,
    w_in_h,
    w_out_h,
    gains_r,
    shifts_r,
    tok_in_r,
    tok_out_r,
    tok_bias_r,
    tok_bias_out_r,
    bias_in_r,
    bias_out_r,
    act_o,
    ing_o,
    gwi_o,
    gwo_o,
    gti_o,
    gto_o,
    vec_o,
    tbo_o,
    sm_o,
    x_raw,
    d_raw,
    w_in,
    w_out,
    act_s,
    ing_s,
    pb,
    aug,
    misc,
    toki_t,
    toko_t,
    toki,
    toko,
    gs,
    dout,
    dhid,
    xf,
    xh1,
    rs1,
    xh2,
    rs2,
    normed,
    th,
    tgp,
    chan,
    hid,
    dpre,
    tmp,
    dq,
    cq,
    hq,
    pq,
    infl,
    sqs,
    dmix,
    dtok,
    dnorm,
    zpart,
    zrx,
    zpair,
    zrxp,
    ztot,
    gw,
    wsib_s,
    wsib_r,
    wch_s,
    wch_r,
    gtok,
    tsib_s,
    tsib_r,
    tch_s,
    tch_r,
    acc,
    vec,
    vsib_r,
    vch,
    zsm,
    in_sem,
    out_sem,
    pb_c,
    pb_x,
    dq_c,
    dq_x,
    cq_c,
    cq_x,
    ze,
    zm,
    zt,
    w_sem,
    t_sem,
    v_sem,
    s_sem,
):
    me = lax.axis_index("dp")
    t = lax.axis_index("tensor")
    core = me % 2
    chip = me // 2
    sib = chip * 2 + 1 - core
    nc = n_dp // 2
    mid = (t == 1) | (t == 2)
    end = (t == 0) | (t == 3)
    end_peer = jnp.where(t < 2, 1, 2)
    mid_end = jnp.where(t < 2, 0, 3)
    mid_peer = 3 - t
    shard = D // n_dp
    ks = toks // n_dp
    kb = -(-ks // 16) * 16
    K = n_dp * kb
    KA = K + 16
    R = count * ROWS
    half = R // CHUNK
    steps = 2 * half
    nblk = ROWS // 16
    last = ROWS - 16
    tail = patches - last

    def peer(k):
        return ((chip + k) % nc) * 2 + core

    def src(k):
        return ((chip - k + nc) % nc) * 2 + core

    def src_sib(k):
        return ((chip - k + nc) % nc) * 2 + 1 - core

    def rcopy(a, b, ss, rs, dev):
        return pltpu.make_async_remote_copy(
            src_ref=a, dst_ref=b, send_sem=ss, recv_sem=rs, device_id=dev, device_id_type=MESH
        )

    class Gather:
        def __init__(self, buf, c, x):
            self.buf, self.c, self.x = buf, c, x

        def chip_copy(self, k):
            return rcopy(
                self.buf.at[me], self.buf.at[me], self.c.at[0, k - 1], self.c.at[1, k - 1], (peer(k), t)
            )

        def sib_copy(self, k):
            s = src(k)
            return rcopy(self.buf.at[s], self.buf.at[s], self.x.at[0, k], self.x.at[1, k], (sib, t))

        def start(self):
            for k in range(1, nc):
                self.chip_copy(k).start()
            self.sib_copy(0).start()

        def relay(self, k):
            s = src(k)
            rcopy(
                self.buf.at[s], self.buf.at[s], self.c.at[0, k - 1], self.c.at[1, k - 1], (sib, t)
            ).wait_recv()
            self.sib_copy(k).start()

        def from_sib(self, k):
            s = src_sib(k)
            rcopy(
                self.buf.at[s], self.buf.at[s], self.x.at[0, k], self.x.at[1, k], (sib, t)
            ).wait_recv()

        def drain(self):
            for k in range(1, nc):
                self.chip_copy(k).wait_send()
            for k in range(nc):
                self.sib_copy(k).wait_send()

    params = Gather(pb, pb_c, pb_x)
    dqs = Gather(dq, dq_c, dq_x)
    cqs = Gather(cq, cq_c, cq_x)

    loads = [
        pltpu.make_async_copy(cotangent, d_raw, in_sem.at[0]),
        pltpu.make_async_copy(w_out_h, w_out, in_sem.at[1]),
        pltpu.make_async_copy(images, x_raw, in_sem.at[2]),
        pltpu.make_async_copy(w_in_h, w_in, in_sem.at[3]),
    ]
    for c in loads:
        c.start()

    barrier = pltpu.get_barrier_semaphore()
    others = [(sib, t)] + [(peer(k), t) for k in range(1, nc)] + [(me, (t + k) % 4) for k in (1, 2, 3)]
    for dev in others:
        pl.semaphore_signal(barrier, inc=1, device_id=dev, device_id_type=MESH)

    pb[me] = jnp.zeros(pb.shape[1:], BF16)
    eye = (
        lax.broadcasted_iota(jnp.int32, (kb, 128), 0) == lax.broadcasted_iota(jnp.int32, (kb, 128), 1)
    ).astype(BF16)
    aug[...] = jnp.zeros(aug.shape, F32)
    aug[0:patches, 0:ks] = tok_in_r[...].astype(F32)
    aug[patches : patches + 1, 0:ks] = tok_bias_r[...].astype(F32)
    pb[me, 0:kb, 0:ROWS] = dot_nt(eye, aug[...].astype(BF16)).astype(BF16)
    aug[0:patches, 0:ks] = tok_out_r[...].astype(F32)
    aug[patches : patches + 1, 0:ks] = jnp.zeros((1, ks), F32)
    pb[me, kb : 2 * kb, 0:ROWS] = dot_nt(eye, aug[...].astype(BF16)).astype(BF16)
    misc[...] = jnp.zeros(misc.shape, F32)
    misc[0:2, 0:shard] = gains_r[...].astype(F32)
    misc[2:4, 0:shard] = shifts_r[...].astype(F32)
    pb[me, 2 * kb : 2 * kb + 16, :] = misc[...].astype(BF16)

    pl.semaphore_wait(barrier, len(others))
    params.start()

    loads[0].wait()
    misc[...] = jnp.zeros(misc.shape, F32)
    acc[...] = jnp.zeros(acc.shape, F32)

    def pad_dout(i, carry):
        base = pl.multiple_of(i * ROWS, 16)
        dout[pl.ds(base, last), :] = d_raw[i, 0:last, :]
        for c in range(0, D, 256):
            misc[0:tail, :] = d_raw[i, last:patches, c : c + 256].astype(F32)
            dout[pl.ds(base + last, 16), c : c + 256] = misc[...].astype(BF16)
        a = jnp.zeros((8, D), F32)
        for b in range(nblk):
            a = a + fold(dout[pl.ds(base + 16 * b, 16), :].astype(F32))
        acc[4] += a
        return carry

    lax.fori_loop(0, count, pad_dout, 0)
    dq[me] = dout[0:ROWS, :]
    dqs.start()

    loads[1].wait()

    def hidden_grad(i, carry):
        r = pl.ds(pl.multiple_of(i * ROWS, 16), ROWS)
        for c in range(0, D, 256):
            dhid[r, c : c + 256] = dot_nt(dout[r, :], w_out[c : c + 256, :])
        return carry

    lax.fori_loop(0, count, hidden_grad, 0)

    loads[2].wait()

    def first_norm(i, carry):
        base = pl.multiple_of(i * ROWS, 16)
        xf[pl.ds(base + last, 16), :] = jnp.zeros((16, D), F32)
        xf[pl.ds(base, last), :] = x_raw[i, 0:last, :].astype(F32)
        xf[pl.ds(base + last, tail), :] = x_raw[i, last:patches, :].astype(F32)
        for b in range(nblk):
            r = pl.ds(base + 16 * b, 16)
            v = xf[r, :]
            center = v - jnp.mean(v, axis=-1, keepdims=True)
            inv = lax.rsqrt(jnp.mean(center * center, axis=-1, keepdims=True) + 1e-06)
            xh1[r, :] = center * inv
            rs1[r, :] = jnp.broadcast_to(inv, (16, 128))
        return carry

    lax.fori_loop(0, count, first_norm, 0)

    for k in range(1, nc):
        params.relay(k)
    for k in range(nc):
        params.from_sib(k)
    full = jnp.zeros((16, D), F32)
    for d in range(n_dp):
        toki_t[d * kb : (d + 1) * kb, :] = pb[d, 0:kb, :]
        toko_t[d * kb : (d + 1) * kb, :] = pb[d, kb : 2 * kb, :]
        part = pb[d, 2 * kb : 2 * kb + 16, 0:128].astype(F32)
        part = jnp.concatenate([part, jnp.zeros((16, D - 128), F32)], axis=1)
        full = full + (pltpu.roll(part, d * shard, 1) if d else part)
    gs[...] = full
    misc[...] = jnp.zeros(misc.shape, F32)
    misc[0:1, 0:patches] = tok_bias_out_r[...].astype(F32)
    toko_t[K:KA, :] = misc[...].astype(BF16)
    ri = lax.broadcasted_iota(jnp.int32, (ROWS, ROWS), 0)
    ci = lax.broadcasted_iota(jnp.int32, (ROWS, ROWS), 1)
    eye_rows = ((ri == ci) & (ri < patches)).astype(BF16)
    toki[:, 0:K] = dot_nt(eye_rows, toki_t[:, 0:ROWS]).astype(BF16)
    toko[:, 0:KA] = dot_nt(eye_rows, toko_t[:, 0:ROWS]).astype(BF16)
    loads[3].wait()

    def zrows(c):
        return pl.ds(pl.multiple_of(c * CHUNK, 16), CHUNK)

    def up_copy(c):
        return rcopy(zpart.at[zrows(c)], zrx.at[zrows(c)], ze.at[0, c], ze.at[1, c], (me, end_peer))

    def mid_copy(c):
        return rcopy(zpair.at[zrows(c)], zrxp.at[zrows(c)], zm.at[0, c], zm.at[1, c], (me, mid_peer))

    def down_copy(c):
        return rcopy(ztot.at[zrows(c)], ztot.at[zrows(c)], zt.at[0, c], zt.at[1, c], (me, mid_end))

    def start_up(first, extra, more):
        @pl.when(end)
        def _():
            for j in range(4):
                up_copy(first + j).start()

            @pl.when(more)
            def _():
                for j in range(4, 4 + extra):
                    up_copy(first + j).start()

    def zpair_step(c):
        up_copy(c).wait_recv()
        r = zrows(c)
        zpair[r, :] = (zpart[r, :].astype(F32) + zrx[r, :].astype(F32)).astype(BF16)
        mid_copy(c).start()

    def ztot_step(c):
        mid_copy(c).wait_recv()
        r = zrows(c)
        ztot[r, :] = (zpair[r, :].astype(F32) + zrxp[r, :].astype(F32)).astype(BF16)
        down_copy(c).start()

    def zslot(s):
        @pl.when(mid)
        def _():
            if isinstance(s, int):
                if s < steps:
                    zpair_step(s)
                if 0 <= s - LAG < steps:
                    ztot_step(s - LAG)
            else:
                zpair_step(s)
                ztot_step(s - LAG)

    def zfin(first, number):
        @pl.when(end)
        def _():
            for j in range(number):
                down_copy(first + j).wait_recv()

    def forward(i, carry):
        base = pl.multiple_of(i * ROWS, 16)
        r = pl.ds(base, ROWS)
        for b in range(nblk):
            rb = pl.ds(base + 16 * b, 16)
            v = xh1[rb, :] * gs[0:1, :] + gs[2:3, :]
            if 16 * (b + 1) > patches:
                row = lax.broadcasted_iota(jnp.int32, (16, D), 0) + 16 * b
                v = jnp.where(row < patches, v, jnp.where(row == patches, 1.0, 0.0))
            normed[rb, :] = v.astype(BF16)
        th[i, K:KA, :] = (lax.broadcasted_iota(jnp.int32, (16, D), 0) == 0).astype(F32).astype(BF16)
        for c in range(0, D, 256):
            tmp[0:K, :] = dot_nn(toki_t[:, 0:ROWS], normed[r, c : c + 256])
            for b in range(0, K, 16):
                value, slope = gelu_pair(tmp[b : b + 16, :])
                th[i, b : b + 16, c : c + 256] = value.astype(BF16)
                tgp[i, b : b + 16, c : c + 256] = slope
            xf[r, c : c + 256] += dot_nn(toko[:, 0:KA], th[i, :, c : c + 256])
        for b in range(nblk):
            rb = pl.ds(base + 16 * b, 16)
            v = xf[rb, :]
            center = v - jnp.mean(v, axis=-1, keepdims=True)
            inv = lax.rsqrt(jnp.mean(center * center, axis=-1, keepdims=True) + 1e-06)
            xhat = center * inv
            xh2[rb, :] = xhat
            rs2[rb, :] = jnp.broadcast_to(inv, (16, 128))
            chan[rb, :] = (xhat * gs[1:2, :] + gs[3:4, :]).astype(BF16)

        @pl.when(i == 0)
        def _():
            cq[me] = chan[0:ROWS, :]
            cqs.start()

        for c in range(0, D, 256):
            tmp[0:ROWS, :] = dot_nn(chan[r, :], w_in[:, c : c + 256])
            a = jnp.zeros((8, 256), F32)
            for b in range(nblk):
                rb = pl.ds(base + 16 * b, 16)
                value, slope = gelu_pair(tmp[16 * b : 16 * b + 16, :] + bias_in_r[:, c : c + 256])
                hid[rb, c : c + 256] = value.astype(BF16)
                low = (slope * dhid[rb, c : c + 256]).astype(BF16)
                dpre[rb, c : c + 256] = low
                a = a + fold(low.astype(F32))
            acc[5, :, c : c + 256] += a
        for c in range(0, D, 256):
            zpart[r, c : c + 256] = dot_nt(dpre[r, :], w_in[c : c + 256, :]).astype(BF16)
        start_up(4 * i, half - 4 * count, i == count - 1)
        return carry

    lax.fori_loop(0, count, forward, 0)

    def partial_out(i, carry):
        r = pl.ds(pl.multiple_of(i * ROWS, 16), ROWS)
        ro = pl.ds(pl.multiple_of(R + i * ROWS, 16), ROWS)
        for c in range(0, D, 256):
            zpart[ro, c : c + 256] = dot_nn(hid[r, :], w_out[:, c : c + 256]).astype(BF16)
        start_up(half + 4 * i, half - 4 * count, i == count - 1)
        return carry

    lax.fori_loop(0, count, partial_out, 0)
    zslot(0)
    zslot(1)

    def weight_grad(j, carry):
        cols = pl.ds(pl.multiple_of(j * 256, 256), 256)
        gw[0, cols, :] = dot_tn(chan[:, cols], dpre[...])
        gw[1, cols, :] = dot_tn(dout[:, cols], hid[...])
        return carry

    lax.fori_loop(0, D // 256, weight_grad, 0)
    for c in range(nc):
        rows = pl.ds(pl.multiple_of((2 * c + 1 - core) * shard, 8), shard)
        for m in range(2):
            wsib_s[c, m] = gw[m, rows, :].astype(BF16)
    w_sib = rcopy(wsib_s, wsib_r, w_sem.at[0, 0], w_sem.at[1, 0], (sib, t))
    w_sib.start()
    zslot(2)

    sqs[...] = jnp.zeros(sqs.shape, F32)

    def square(i, carry):
        r = pl.ds(pl.multiple_of(i * ROWS, 16), ROWS)
        g1 = dot_nt(chan[r, :], chan[r, :]) * dot_nt(dpre[r, :], dpre[r, :])
        g2 = dot_nt(dout[r, :], dout[r, :]) * dot_nt(hid[r, :], hid[r, :])
        sqs[pl.ds(i, 1), 0:ROWS] = jnp.sum(g1 + g2, axis=0, keepdims=True)
        return carry

    lax.fori_loop(0, count, square, 0)
    zslot(3)

    w_sib.wait_recv()

    def w_chip(k):
        return rcopy(
            wch_s.at[k - 1], wch_r.at[k - 1], w_sem.at[0, k], w_sem.at[1, k], (peer(k), t)
        )

    for k in range(1, nc):
        dest = (chip + k) % nc
        rows = pl.ds(pl.multiple_of((2 * dest + core) * shard, 8), shard)
        for m in range(2):
            wch_s[k - 1, m] = (gw[m, rows, :] + wsib_r[dest, m].astype(F32)).astype(BF16)
        w_chip(k).start()
    zslot(4)

    infl[...] = jnp.zeros(infl.shape, F32)

    def query(j, carry):
        k = j // 2
        own = j % 2 == 0
        slot = jnp.where(own, src(k), src_sib(k))

        @pl.when(own & (k > 0))
        def _():
            dqs.relay(k)
            cqs.relay(k)

        @pl.when(jnp.logical_not(own))
        def _():
            dqs.from_sib(k)
            cqs.from_sib(k)

        @pl.when(j + 5 < half)
        def _():
            zslot(j + 5)

        for c in range(0, D, 256):
            tmp[0:ROWS, :] = dot_nn(cq[slot], w_in[:, c : c + 256])
            tmp[ROWS : 2 * ROWS, :] = dot_nt(dq[slot], w_out[c : c + 256, :])
            for b in range(0, ROWS, 16):
                value, slope = gelu_pair(tmp[b : b + 16, :] + bias_in_r[:, c : c + 256])
                hq[b : b + 16, c : c + 256] = value.astype(BF16)
                pq[b : b + 16, c : c + 256] = (slope * tmp[ROWS + b : ROWS + b + 16, :]).astype(BF16)
        for q in range(count - QRY_DEV):
            r = slice((QRY_DEV + q) * ROWS, (QRY_DEV + q + 1) * ROWS)
            g1 = dot_nt(cq[slot], chan[r, :]) * dot_nt(pq[...], dpre[r, :])
            g2 = dot_nt(dq[slot], dout[r, :]) * dot_nt(hq[...], hid[r, :])
            infl[q, pl.ds(slot, 1), 0:ROWS] = jnp.sum(g1 + g2, axis=0, keepdims=True)
        return carry

    lax.fori_loop(0, n_dp, query, 0)
    for s in range(min(n_dp + 5, half), half + LAG):
        zslot(s)

    lane = lax.broadcasted_iota(jnp.int32, (n_dp, 128), 1)
    sm = jnp.zeros((n_dp, 128), F32)
    for q in range(count - QRY_DEV):
        sm = jnp.where(lane == q, jnp.sum(infl[q], axis=1, keepdims=True), sm)
    zsm[t, 0:n_dp, :] = sm * (2.0 * D * FF) ** (-0.5)
    zsm[t, n_dp : n_dp + 8, :] = jnp.broadcast_to(
        jnp.sum(sqs[...], axis=1, keepdims=True) / (2.0 * D * FF), (8, 128)
    )

    def sm_copy(k):
        return rcopy(
            zsm.at[t], zsm.at[t], s_sem.at[0, k - 1], s_sem.at[1, k - 1], (me, (t + k) % 4)
        )

    for k in (1, 2, 3):
        sm_copy(k).start()

    gtok[...] = jnp.zeros(gtok.shape, F32)

    def ing_copy(i):
        return pltpu.make_async_copy(ing_s.at[i], ing_o.at[i], out_sem.at[0, i])

    def backward(i, carry):
        @pl.when(i == 0)
        def _():
            zfin(0, 1)

        zfin(4 * i + 1, 4)
        base = pl.multiple_of(i * ROWS, 16)
        r = pl.ds(base, ROWS)
        a1 = jnp.zeros((8, D), F32)
        a3 = jnp.zeros((8, D), F32)
        for b in range(nblk):
            rb = pl.ds(base + 16 * b, 16)
            e = ztot[rb, :].astype(F32)
            xhat = xh2[rb, :]
            a1 = a1 + fold(e * xhat)
            a3 = a3 + fold(e)
            eg = e * gs[1:2, :]
            m1 = jnp.mean(eg, axis=-1, keepdims=True)
            m2 = jnp.mean(eg * xhat, axis=-1, keepdims=True)
            d = dout[rb, :].astype(F32) + rs2[rb, 0:1] * (eg - m1 - xhat * m2)
            dhid[rb, :] = d
            dmix[16 * b : 16 * b + 16, :] = d.astype(BF16)
        acc[1] += a1
        acc[3] += a3
        for c in range(0, D, 256):
            tmp[0:K, :] = dot_nn(toko_t[0:K, 0:ROWS], dmix[:, c : c + 256])
            for b in range(0, K, 16):
                dtok[b : b + 16, c : c + 256] = (
                    tmp[b : b + 16, :] * tgp[i, b : b + 16, c : c + 256]
                ).astype(BF16)
        gtok[0, 0:K, 0:ROWS] += dot_nt(dtok[...], normed[r, :])
        gtok[1, :, 0:ROWS] += dot_nt(th[i], dmix[...])
        for c in range(0, D, 256):
            dnorm[:, c : c + 256] = dot_nn(toki[:, 0:K], dtok[:, c : c + 256])
        a0 = jnp.zeros((8, D), F32)
        a2 = jnp.zeros((8, D), F32)
        for b in range(nblk):
            rb = pl.ds(base + 16 * b, 16)
            e = dnorm[16 * b : 16 * b + 16, :]
            xhat = xh1[rb, :]
            a0 = a0 + fold(e * xhat)
            a2 = a2 + fold(e)
            eg = e * gs[0:1, :]
            m1 = jnp.mean(eg, axis=-1, keepdims=True)
            m2 = jnp.mean(eg * xhat, axis=-1, keepdims=True)
            d = (dhid[rb, :] + rs1[rb, 0:1] * (eg - m1 - xhat * m2)).astype(BF16)
            n = min(16, patches - 16 * b)
            ing_s[i, 16 * b : 16 * b + n, :] = d[0:n]
        acc[0] += a0
        acc[2] += a2
        ing_copy(i).start()
        zslot(half + LAG + i)
        return carry

    lax.fori_loop(0, count, backward, 0)
    done = half + LAG + count

    for c in range(nc):
        rows = pl.ds(pl.multiple_of((2 * c + 1 - core) * kb, 8), kb)
        for m in range(2):
            tsib_s[c, m] = gtok[m, rows, :]
    t_sib = rcopy(tsib_s, tsib_r, t_sem.at[0, 0], t_sem.at[1, 0], (sib, t))
    t_sib.start()
    vec[...] = jnp.zeros(vec.shape, F32)
    for q in range(6):
        vec[q : q + 1, :] = jnp.sum(acc[q], axis=0, keepdims=True)
    vec[6:7, 0:256] = gtok[1, K : K + 1, :]
    v_sib = rcopy(vec, vsib_r, v_sem.at[0, 0], v_sem.at[1, 0], (sib, t))
    v_sib.start()
    zslot(done)
    v_sib.wait_recv()

    def v_chip(k):
        return rcopy(
            vch.at[chip], vch.at[chip], v_sem.at[0, k], v_sem.at[1, k], (peer(k), t)
        )

    vch[chip] = vec[...] + vsib_r[...]
    for k in range(1, nc):
        v_chip(k).start()
    t_sib.wait_recv()

    def t_chip(k):
        return rcopy(
            tch_s.at[k - 1], tch_r.at[k - 1], t_sem.at[0, k], t_sem.at[1, k], (peer(k), t)
        )

    for k in range(1, nc):
        dest = (chip + k) % nc
        rows = pl.ds(pl.multiple_of((2 * dest + core) * kb, 8), kb)
        for m in range(2):
            tch_s[k - 1, m] = gtok[m, rows, :] + tsib_r[dest, m]
        t_chip(k).start()
    zslot(done + 1)

    rows = pl.ds(pl.multiple_of(me * shard, 8), shard)
    for m, out in enumerate((gwi_o, gwo_o)):
        out[...] = gw[m, rows, :] + wsib_r[chip, m].astype(F32)
    for k in range(1, nc):
        w_chip(k).wait_recv()
        for m, out in enumerate((gwi_o, gwo_o)):
            out[...] += wch_r[k - 1, m].astype(F32)
    zslot(done + 2)
    zslot(done + 3)
    for k in (1, 2, 3):
        sm_copy(k).wait_recv()
    sm_o[...] = (zsm[0] + zsm[1]) + (zsm[2] + zsm[3])
    rows = pl.ds(pl.multiple_of(me * kb, 8), kb)
    for m, out in enumerate((gti_o, gto_o)):
        out[...] = gtok[m, rows, :] + tsib_r[chip, m]
    for k in range(1, nc):
        t_chip(k).wait_recv()
        for m, out in enumerate((gti_o, gto_o)):
            out[...] += tch_r[k - 1, m]
    for k in range(1, nc):
        v_chip(k).wait_recv()
    total = vch[0]
    for c in range(1, nc):
        total = total + vch[c]
    tbo_o[...] = total[:, 0:256]
    vec_o[...] = pltpu.roll(total, (D - me * shard) % D, 1)[:, 0:128]

    def act_copy(i):
        return pltpu.make_async_copy(act_s.at[i], act_o.at[i], out_sem.at[1, i])

    at = done + 4
    for i in range(count):
        need = -(-((i + 1) * ROWS) // CHUNK) + half
        while at < min(need + LAG, steps + LAG):
            zslot(at)
            at += 1
        first = half if i == 0 else -(-(i * ROWS) // CHUNK) + half
        zfin(first, need - first)
        for b in range(nblk):
            n = min(16, patches - 16 * b)
            rb = slice(i * ROWS + 16 * b, i * ROWS + 16 * b + 16)
            ro = slice(R + i * ROWS + 16 * b, R + i * ROWS + 16 * b + 16)
            a = (xf[rb, :] + ztot[ro, :].astype(F32) + bias_out_r[...]).astype(BF16)
            act_s[i, 16 * b : 16 * b + n, :] = a[0:n]
        act_copy(i).start()

    params.drain()
    dqs.drain()
    cqs.drain()

    def drain_end(c, carry):
        up_copy(c).wait_send()
        return carry

    def drain_mid(c, carry):
        mid_copy(c).wait_send()
        down_copy(c).wait_send()
        return carry

    @pl.when(end)
    def _():
        lax.fori_loop(0, steps, drain_end, 0)

    @pl.when(mid)
    def _():
        lax.fori_loop(0, steps, drain_mid, 0)

    w_sib.wait_send()
    t_sib.wait_send()
    v_sib.wait_send()
    for k in range(1, nc):
        w_chip(k).wait_send()
        t_chip(k).wait_send()
        v_chip(k).wait_send()
    for k in (1, 2, 3):
        sm_copy(k).wait_send()
    for i in range(count):
        ing_copy(i).wait()
        act_copy(i).wait()


def fused(
    n_dp,
    images,
    cotangent,
    norm_gains,
    norm_shifts,
    tok_in,
    tok_out_t,
    tok_bias_in,
    tok_bias_out,
    w_in,
    bias_in,
    w_out,
    bias_out,
):
    count, patches, width = images.shape
    nc = n_dp // 2
    ks = tok_in.shape[1]
    toks = ks * n_dp
    kb = -(-ks // 16) * 16
    K = n_dp * kb
    KA = K + 16
    KL = -(-KA // 128) * 128
    R = count * ROWS
    steps = 2 * (R // CHUNK)
    shard = width // n_dp
    hidden = w_in.shape[1]
    anyspace = pl.BlockSpec(memory_space=pl.ANY)
    vm = pl.BlockSpec(memory_space=pltpu.VMEM)
    V = pltpu.VMEM
    dma = lambda *s: pltpu.SemaphoreType.DMA(s)
    smr = n_dp + 8
    scratch = dict(
        x_raw=V((count, patches, D), BF16),
        d_raw=V((count, patches, D), BF16),
        w_in=V((D, hidden), BF16),
        w_out=V((hidden, D), BF16),
        act_s=V((count, patches, D), BF16),
        ing_s=V((count, patches, D), BF16),
        pb=V((n_dp, 2 * kb + 16, 256), BF16),
        aug=V((ROWS, 128), F32),
        misc=V((16, 256), F32),
        toki_t=V((K, 256), BF16),
        toko_t=V((KA, 256), BF16),
        toki=V((ROWS, KL), BF16),
        toko=V((ROWS, KL), BF16),
        gs=V((16, D), F32),
        dout=V((R, D), BF16),
        dhid=V((R, hidden), F32),
        xf=V((R, D), F32),
        xh1=V((R, D), F32),
        rs1=V((R, 128), F32),
        xh2=V((R, D), F32),
        rs2=V((R, 128), F32),
        normed=V((R, D), BF16),
        th=V((count, KA, D), BF16),
        tgp=V((count, K, D), F32),
        chan=V((R, D), BF16),
        hid=V((R, hidden), BF16),
        dpre=V((R, hidden), BF16),
        tmp=V((max(K, 2 * ROWS), 256), F32),
        dq=V((n_dp, ROWS, D), BF16),
        cq=V((n_dp, ROWS, D), BF16),
        hq=V((ROWS, hidden), BF16),
        pq=V((ROWS, hidden), BF16),
        infl=V((count - QRY_DEV, n_dp, 256), F32),
        sqs=V((8, 256), F32),
        dmix=V((ROWS, D), BF16),
        dtok=V((K, D), BF16),
        dnorm=V((ROWS, D), F32),
        zpart=V((2 * R, D), BF16),
        zrx=V((2 * R, D), BF16),
        zpair=V((2 * R, D), BF16),
        zrxp=V((2 * R, D), BF16),
        ztot=V((2 * R, D), BF16),
        gw=V((2, D, hidden), F32),
        wsib_s=V((nc, 2, shard, hidden), BF16),
        wsib_r=V((nc, 2, shard, hidden), BF16),
        wch_s=V((nc - 1, 2, shard, hidden), BF16),
        wch_r=V((nc - 1, 2, shard, hidden), BF16),
        gtok=V((2, KA, 256), F32),
        tsib_s=V((nc, 2, kb, 256), F32),
        tsib_r=V((nc, 2, kb, 256), F32),
        tch_s=V((nc - 1, 2, kb, 256), F32),
        tch_r=V((nc - 1, 2, kb, 256), F32),
        acc=V((6, 8, D), F32),
        vec=V((8, D), F32),
        vsib_r=V((8, D), F32),
        vch=V((nc, 8, D), F32),
        zsm=V((4, smr, 128), F32),
        in_sem=dma(4),
        out_sem=dma(2, count),
        pb_c=dma(2, nc - 1),
        pb_x=dma(2, nc),
        dq_c=dma(2, nc - 1),
        dq_x=dma(2, nc),
        cq_c=dma(2, nc - 1),
        cq_x=dma(2, nc),
        ze=dma(2, steps),
        zm=dma(2, steps),
        zt=dma(2, steps),
        w_sem=dma(2, nc),
        t_sem=dma(2, nc),
        v_sem=dma(2, nc),
        s_sem=dma(2, 3),
    )
    outs = [
        (images.shape, BF16, anyspace),
        (images.shape, BF16, anyspace),
        ((shard, hidden), F32, vm),
        ((shard, hidden), F32, vm),
        ((kb, 256), F32, vm),
        ((kb, 256), F32, vm),
        ((8, 128), F32, vm),
        ((8, 256), F32, vm),
        ((smr, 128), F32, vm),
    ]
    names = list(scratch)
    n_in, n_out = 12, len(outs)

    def body(*refs):
        mega(n_dp, count, patches, toks, *refs[: n_in + n_out], **dict(zip(names, refs[n_in + n_out :])))

    act, ing, gwi, gwo, gti, gto, vec, tbo, sm = pl.pallas_call(
        body,
        out_shape=[jax.ShapeDtypeStruct(s, d) for s, d, _ in outs],
        in_specs=[anyspace] * 4 + [vm] * 8,
        out_specs=[o[2] for o in outs],
        scratch_shapes=list(scratch.values()),
        compiler_params=pltpu.CompilerParams(
            collective_id=0, has_side_effects=True, vmem_limit_bytes=60 * 2**20
        ),
        name="mixer",
    )(
        images,
        cotangent,
        w_in,
        w_out,
        norm_gains,
        norm_shifts,
        tok_in,
        tok_out_t,
        tok_bias_in,
        tok_bias_out.reshape(1, -1),
        bias_in.astype(F32).reshape(1, -1),
        bias_out.astype(F32).reshape(1, -1),
    )
    return (
        act,
        ing,
        vec[0:2, 0:shard],
        vec[2:4, 0:shard],
        gti[0:ks, 0:patches].T,
        gto[0:ks, 0:patches].T,
        gti[0:ks, patches].reshape(1, ks),
        tbo[6, 0:patches],
        gwi,
        vec[5, 0:shard],
        gwo.T,
        vec[4, 0:shard],
        sm[n_dp : n_dp + count, 0],
        sm[0:n_dp, 0 : count - QRY_DEV],
    )


def layer_norm(values, gain, shift):
    center = values - jnp.mean(values, axis=-1, keepdims=True)
    spread = jnp.mean(center * center, axis=-1, keepdims=True)
    return center * lax.rsqrt(spread + 1e-06) * gain + shift


def smooth(values):
    return jax.nn.gelu(values, approximate=True)


def contract(left, right, left_dim, right_dim):
    return lax.dot_general(
        left, right, (((left_dim,), (right_dim,)), ((), ())), preferred_element_type=jnp.float32
    )


def per_device(
    images,
    cotangent,
    norm_gains,
    norm_shifts,
    tok_in,
    tok_out_t,
    tok_bias_in,
    tok_bias_out,
    w_in,
    bias_in,
    w_out,
    bias_out,
):
    gains, shifts, tok_first, tok_second, tok_bias = (
        lax.all_gather(norm_gains, "dp", axis=1, tiled=True),
        lax.all_gather(norm_shifts, "dp", axis=1, tiled=True),
        lax.all_gather(tok_in, "dp", axis=1, tiled=True),
        lax.all_gather(tok_out_t, "dp", axis=1, tiled=True),
        lax.all_gather(tok_bias_in, "dp", axis=1, tiled=True),
    )
    gains = gains.astype(jnp.float32)
    shifts = shifts.astype(jnp.float32)
    count, patches, width = images.shape
    rows = count * patches
    inputs = images.astype(jnp.float32)
    normed_one, first_back = jax.vjp(layer_norm, inputs, gains[0], shifts[0])
    normed_low = normed_one.astype(jnp.bfloat16)
    tok_pre = (
        jnp.einsum("sk,nsd->nkd", tok_first, normed_low, preferred_element_type=jnp.float32)
        + tok_bias[0].astype(jnp.float32)[None, :, None]
    )
    tok_hidden = smooth(tok_pre).astype(jnp.bfloat16)
    tok_mixed = (
        jnp.einsum("sk,nkd->nsd", tok_second, tok_hidden, preferred_element_type=jnp.float32)
        + tok_bias_out.astype(jnp.float32)[None, :, None]
    )
    resid = inputs + tok_mixed
    normed_two, second_back = jax.vjp(layer_norm, resid, gains[1], shifts[1])
    chan_in = normed_two.astype(jnp.bfloat16).reshape(rows, width)
    chan_pre = jnp.dot(chan_in, w_in, preferred_element_type=jnp.float32) + bias_in.astype(
        jnp.float32
    )
    hidden = smooth(chan_pre).astype(jnp.bfloat16)
    partial_out = jnp.dot(hidden, w_out, preferred_element_type=jnp.float32)
    mixed = lax.psum(partial_out, "tensor")
    activations = (
        resid + mixed.reshape(count, patches, width) + bias_out.astype(jnp.float32)
    ).astype(jnp.bfloat16)
    dout_rows = cotangent.reshape(rows, width)
    d_hidden = contract(dout_rows, w_out, 1, 1)
    smooth_value, smooth_back = jax.vjp(smooth, chan_pre)
    d_pre = smooth_back(d_hidden)[0].astype(jnp.bfloat16)
    d_chan_part = contract(d_pre, w_in, 1, 1)
    d_chan = lax.psum(d_chan_part, "tensor")
    d_resid_norm, d_gain_two, d_shift_two = second_back(d_chan.reshape(count, patches, width))
    d_resid = cotangent.astype(jnp.float32) + d_resid_norm
    d_mixed = d_resid.astype(jnp.bfloat16)
    d_tokhid = jnp.einsum("sk,nsd->nkd", tok_second, d_mixed, preferred_element_type=jnp.float32)
    tok_value, tok_back = jax.vjp(smooth, tok_pre)
    d_tokpre = tok_back(d_tokhid)[0].astype(jnp.bfloat16)
    grad_second = jnp.einsum("nsd,nkd->sk", d_mixed, tok_hidden, preferred_element_type=jnp.float32)
    grad_first = jnp.einsum("nsd,nkd->sk", normed_low, d_tokpre, preferred_element_type=jnp.float32)
    grad_tbias = jnp.sum(d_tokpre, axis=(0, 2), dtype=jnp.float32)[None, :]
    grad_tbias_out = jnp.sum(d_mixed, axis=(0, 2), dtype=jnp.float32)
    d_normed = jnp.einsum("sk,nkd->nsd", tok_first, d_tokpre, preferred_element_type=jnp.float32)
    d_input_norm, d_gain_one, d_shift_one = first_back(d_normed)
    input_grad = (d_resid + d_input_norm).astype(jnp.bfloat16)
    grad_win = contract(chan_in, d_pre, 0, 0)
    grad_wout_t = contract(dout_rows, hidden, 0, 0)
    grad_bin = jnp.sum(d_pre, axis=0, dtype=jnp.float32)
    grad_bout = jnp.sum(dout_rows, axis=0, dtype=jnp.float32)
    share_win, share_wout_t, share_bin, share_bout = (
        lax.psum_scatter(grad_win, "dp", scatter_dimension=0, tiled=True),
        lax.psum_scatter(grad_wout_t, "dp", scatter_dimension=0, tiled=True),
        lax.psum_scatter(grad_bin, "dp", scatter_dimension=0, tiled=True),
        lax.psum_scatter(grad_bout, "dp", scatter_dimension=0, tiled=True),
    )
    share_gains, share_shifts, share_first, share_second, share_tbias = (
        lax.psum_scatter(
            jnp.stack([d_gain_one, d_gain_two]), "dp", scatter_dimension=1, tiled=True
        ),
        lax.psum_scatter(
            jnp.stack([d_shift_one, d_shift_two]), "dp", scatter_dimension=1, tiled=True
        ),
        lax.psum_scatter(grad_first, "dp", scatter_dimension=1, tiled=True),
        lax.psum_scatter(grad_second, "dp", scatter_dimension=1, tiled=True),
        lax.psum_scatter(grad_tbias, "dp", scatter_dimension=1, tiled=True),
    )
    total_tbias_out = lax.psum(grad_tbias_out, "dp")
    chan_cube = chan_in.reshape(count, patches, width)
    pre_cube = d_pre.reshape(count, patches, -1)
    hidden_cube = hidden.reshape(count, patches, -1)
    def against(chan, pre, dout, low):
        grams = [
            jnp.einsum("sd,npd->nsp", a, b, preferred_element_type=jnp.float32)
            for a, b in ((chan, chan_cube), (pre, pre_cube), (dout, cotangent), (low, hidden_cube))
        ]
        return jnp.sum(grams[0] * grams[1] + grams[2] * grams[3], axis=(1, 2))

    own = lax.map(lambda a: against(*a), (chan_cube, pre_cube, cotangent, hidden_cube))
    squares = jnp.diagonal(own)
    queries = tuple(
        lax.all_gather(a[:QRY_DEV], "dp", axis=0, tiled=True)
        for a in (chan_cube, pre_cube, cotangent, hidden_cube)
    )
    influence = lax.map(lambda a: against(*a), queries)[:, QRY_DEV:]
    influence, squares = lax.psum((influence, squares), "tensor")
    sqnorms = squares / (2.0 * D * FF)
    influence = influence * (2.0 * D * FF) ** (-0.5)
    return (
        activations,
        input_grad,
        share_gains,
        share_shifts,
        share_first,
        share_second,
        share_tbias,
        total_tbias_out,
        share_win,
        share_bin,
        share_wout_t.T,
        share_bout,
        sqnorms,
        influence,
    )


def solution(mesh):
    placed = (
        P("dp", None, None),
        P("dp", None, None),
        P(None, "dp"),
        P(None, "dp"),
        P(None, "dp"),
        P(None, "dp"),
        P(None, "dp"),
        P(),
        P(None, "tensor"),
        P("tensor"),
        P("tensor", None),
        P(),
    )
    n_dp = mesh.shape["dp"]
    fits = n_dp % 2 == 0 and n_dp <= 8 and mesh.shape["tensor"] == 4
    device = functools.partial(fused, n_dp) if fits else per_device
    return jax.shard_map(
        device,
        mesh=mesh,
        in_specs=placed,
        out_specs=(
            P("dp", None, None),
            P("dp", None, None),
            P(None, "dp"),
            P(None, "dp"),
            P(None, "dp"),
            P(None, "dp"),
            P(None, "dp"),
            P(),
            P("dp", "tensor"),
            P(("tensor", "dp")),
            P("tensor", "dp"),
            P("dp"),
            P("dp"),
            P(None, "dp"),
        ),
        check_vma=False,
    )
```

```python
import functools

import jax
import jax.numpy as jnp
from jax import lax
from jax.experimental import pallas as pl
from jax.experimental.pallas import tpu as pltpu
from jax.sharding import PartitionSpec as P

D = 768
FF = 3072
QRY_DEV = 1
HIGH = lax.Precision.HIGHEST
MESH = pl.DeviceIdType.MESH
F32 = jnp.float32
BF16 = jnp.bfloat16

ROWS = 208
CHUNK = 48
LAG = 2
C1 = 0.7978845608028654
C2 = 0.044715


def dot_nn(a, b):
    return lax.dot_general(a, b, (((1,), (0,)), ((), ())), preferred_element_type=F32)


def dot_nt(a, b):
    return lax.dot_general(a, b, (((1,), (1,)), ((), ())), preferred_element_type=F32)


def dot_tn(a, b):
    return lax.dot_general(a, b, (((0,), (0,)), ((), ())), preferred_element_type=F32)


def gelu_pair(v):
    u = v * v
    th = jnp.tanh(v * (C1 + (C1 * C2) * u))
    hp = 0.5 + 0.5 * th
    value = v * hp
    slope = hp + (0.5 * v) * (1.0 - th * th) * (C1 + (3.0 * C1 * C2) * u)
    return value, slope


def fold(v):
    out = v[0:8]
    for s in range(8, v.shape[0], 8):
        out = out + v[s : s + 8]
    return out


def mega(
    n_dp,
    count,
    patches,
    toks,
    images,
    cotangent,
    w_in_h,
    w_out_h,
    gains_r,
    shifts_r,
    tok_in_r,
    tok_out_r,
    tok_bias_r,
    tok_bias_out_r,
    bias_in_r,
    bias_out_r,
    act_o,
    ing_o,
    gwi_o,
    gwo_o,
    gti_o,
    gto_o,
    vec_o,
    tbo_o,
    sm_o,
    x_raw,
    d_raw,
    w_in,
    w_out,
    act_s,
    ing_s,
    pb,
    aug,
    misc,
    toki_t,
    toko_t,
    toki,
    toko,
    gs,
    bs,
    dout,
    dhid,
    xf,
    xh1,
    rs1,
    xh2,
    rs2,
    normed,
    th,
    tgp,
    chan,
    hid,
    dpre,
    tmp,
    dq,
    cq,
    hq,
    pq,
    infl,
    sqs,
    dmix,
    dtok,
    dnorm,
    zpart,
    zrx,
    zpair,
    zrxp,
    ztot,
    gw,
    wsib_s,
    wsib_r,
    wch_s,
    wch_r,
    gtok,
    tsib_s,
    tsib_r,
    tch_s,
    tch_r,
    acc,
    vec,
    vsib_r,
    vch,
    zsm,
    in_sem,
    out_sem,
    pb_c,
    pb_x,
    dq_c,
    dq_x,
    cq_c,
    cq_x,
    ze,
    zm,
    zt,
    w_sem,
    t_sem,
    v_sem,
    s_sem,
):
    me = lax.axis_index("dp")
    t = lax.axis_index("tensor")
    core = me % 2
    chip = me // 2
    sib = chip * 2 + 1 - core
    nc = n_dp // 2
    mid = (t == 1) | (t == 2)
    end = (t == 0) | (t == 3)
    end_peer = jnp.where(t < 2, 1, 2)
    mid_end = jnp.where(t < 2, 0, 3)
    mid_peer = 3 - t
    shard = D // n_dp
    ks = toks // n_dp
    kb = -(-ks // 16) * 16
    K = n_dp * kb
    KA = K + 16
    R = count * ROWS
    half = R // CHUNK
    steps = 2 * half
    nblk = ROWS // 16
    last = ROWS - 16
    tail = patches - last

    def peer(k):
        return (chip ^ k) * 2 + core

    def peer_sib(k):
        return (chip ^ k) * 2 + 1 - core

    def rcopy(a, b, ss, rs, dev):
        return pltpu.make_async_remote_copy(
            src_ref=a, dst_ref=b, send_sem=ss, recv_sem=rs, device_id=dev, device_id_type=MESH
        )

    class Gather:
        def __init__(self, buf, c, x):
            self.buf, self.c, self.x = buf, c, x

        def chip_copy(self, block, k, n):
            b = self.buf.at[block]
            return rcopy(b, b, self.c.at[0, n], self.c.at[1, n], (peer(k), t))

        def sib_copy(self, k):
            b = self.buf.at[peer(k)]
            return rcopy(b, b, self.x.at[0, k], self.x.at[1, k], (sib, t))

        def start(self, across=False):
            for k in (1, 2, 3) if across else (1, 2):
                self.chip_copy(me, k, k - 1).start()
            self.sib_copy(0).start()

        def relay(self, k, across=False):
            self.chip_copy(peer(k), k, k - 1).wait_recv()
            if k < 3 and not across:

                @pl.when(core == k - 1)
                def _():
                    self.chip_copy(peer(k), 3 - k, 2).start()

            self.sib_copy(k).start()

        def from_sib(self, k):
            b = self.buf.at[peer_sib(k)]
            rcopy(b, b, self.x.at[0, k], self.x.at[1, k], (sib, t)).wait_recv()

        def drain(self):
            for n in range(3):
                self.chip_copy(me, n + 1, n).wait_send()
            for k in range(4):
                self.sib_copy(k).wait_send()

    params = Gather(pb, pb_c, pb_x)
    dqs = Gather(dq, dq_c, dq_x)
    cqs = Gather(cq, cq_c, cq_x)

    loads = [
        pltpu.make_async_copy(cotangent, d_raw, in_sem.at[0]),
        pltpu.make_async_copy(w_out_h, w_out, in_sem.at[1]),
        pltpu.make_async_copy(images, x_raw, in_sem.at[2]),
        pltpu.make_async_copy(w_in_h, w_in, in_sem.at[3]),
    ]
    for c in loads:
        c.start()

    barrier = pltpu.get_barrier_semaphore()
    others = [(sib, t)] + [(peer(k), t) for k in range(1, nc)] + [(me, (t + k) % 4) for k in (1, 2, 3)]
    for dev in others:
        pl.semaphore_signal(barrier, inc=1, device_id=dev, device_id_type=MESH)

    pb[me] = jnp.zeros(pb.shape[1:], BF16)
    eye = (
        lax.broadcasted_iota(jnp.int32, (kb, 128), 0) == lax.broadcasted_iota(jnp.int32, (kb, 128), 1)
    ).astype(BF16)
    aug[...] = jnp.zeros(aug.shape, F32)
    aug[patches : patches + 1, 0:ks] = tok_bias_r[...].astype(F32)
    pb[me, 0:kb, 0:ROWS] = dot_nt(eye, aug[...].astype(BF16)).astype(BF16)
    pb[me, 0:ks, 0:patches] = tok_in_r[...]
    pb[me, kb : kb + ks, 0:patches] = tok_out_r[...]
    misc[...] = jnp.zeros(misc.shape, F32)
    misc[0:2, 0:shard] = gains_r[...].astype(F32)
    misc[2:4, 0:shard] = shifts_r[...].astype(F32)
    pb[me, 2 * kb : 2 * kb + 16, :] = misc[...].astype(BF16)

    pl.semaphore_wait(barrier, len(others))
    params.start(across=True)

    loads[0].wait()
    misc[...] = jnp.zeros(misc.shape, F32)
    acc[...] = jnp.zeros(acc.shape, F32)

    def pad_dout(i, carry):
        base = pl.multiple_of(i * ROWS, 16)
        dout[pl.ds(base, last), :] = d_raw[i, 0:last, :]
        for c in range(0, D, 256):
            misc[0:tail, :] = d_raw[i, last:patches, c : c + 256].astype(F32)
            dout[pl.ds(base + last, 16), c : c + 256] = misc[...].astype(BF16)
        a = jnp.zeros((8, D), F32)
        for b in range(nblk):
            a = a + fold(dout[pl.ds(base + 16 * b, 16), :].astype(F32))
        acc[4] += a
        return carry

    lax.fori_loop(0, count, pad_dout, 0)
    dq[me] = dout[0:ROWS, :]
    dqs.start()

    loads[1].wait()

    def hidden_grad(i, carry):
        r = pl.ds(pl.multiple_of(i * ROWS, 16), ROWS)
        for c in range(0, D, 256):
            dhid[r, c : c + 256] = dot_nt(dout[r, :], w_out[c : c + 256, :])
        return carry

    lax.fori_loop(0, count, hidden_grad, 0)

    loads[2].wait()

    def first_norm(i, carry):
        base = pl.multiple_of(i * ROWS, 16)
        xf[pl.ds(base + last, 16), :] = jnp.zeros((16, D), F32)
        xf[pl.ds(base, last), :] = x_raw[i, 0:last, :].astype(F32)
        xf[pl.ds(base + last, tail), :] = x_raw[i, last:patches, :].astype(F32)
        for b in range(nblk):
            r = pl.ds(base + 16 * b, 16)
            v = xf[r, :]
            center = v - jnp.mean(v, axis=-1, keepdims=True)
            inv = lax.rsqrt(jnp.mean(center * center, axis=-1, keepdims=True) + 1e-06)
            xh1[r, :] = center * inv
            rs1[r, :] = jnp.broadcast_to(inv, (16, 128))
        return carry

    lax.fori_loop(0, count, first_norm, 0)

    for k in (1, 2, 3):
        params.relay(k, across=True)
    for k in range(nc):
        params.from_sib(k)
    full = jnp.zeros((16, D), F32)
    for d in range(n_dp):
        toki_t[d * kb : (d + 1) * kb, :] = pb[d, 0:kb, :]
        toko_t[d * kb : (d + 1) * kb, :] = pb[d, kb : 2 * kb, :]
        part = pb[d, 2 * kb : 2 * kb + 16, 0:128].astype(F32)
        part = jnp.concatenate([part, jnp.zeros((16, D - 128), F32)], axis=1)
        full = full + (pltpu.roll(part, d * shard, 1) if d else part)
    gs[...] = full
    misc[...] = jnp.zeros(misc.shape, F32)
    misc[0:1, 0:patches] = tok_bias_out_r[...].astype(F32).reshape(1, patches)
    bs[0:1, :] = bias_in_r[...].astype(F32).reshape(1, D)
    bs[1:2, :] = bias_out_r[...].astype(F32).reshape(1, D)
    toko_t[K:KA, :] = misc[...].astype(BF16)
    ri = lax.broadcasted_iota(jnp.int32, (ROWS, ROWS), 0)
    ci = lax.broadcasted_iota(jnp.int32, (ROWS, ROWS), 1)
    eye_rows = ((ri == ci) & (ri < patches)).astype(BF16)
    toki[:, 0:K] = dot_nt(eye_rows, toki_t[:, 0:ROWS]).astype(BF16)
    toko[:, 0:KA] = dot_nt(eye_rows, toko_t[:, 0:ROWS]).astype(BF16)
    loads[3].wait()

    def zrows(c):
        return pl.ds(pl.multiple_of(c * CHUNK, 16), CHUNK)

    def up_copy(c):
        return rcopy(zpart.at[zrows(c)], zrx.at[zrows(c)], ze.at[0, c], ze.at[1, c], (me, end_peer))

    def mid_copy(c):
        return rcopy(zpair.at[zrows(c)], zrxp.at[zrows(c)], zm.at[0, c], zm.at[1, c], (me, mid_peer))

    def down_copy(c):
        return rcopy(ztot.at[zrows(c)], ztot.at[zrows(c)], zt.at[0, c], zt.at[1, c], (me, mid_end))

    def start_up(first, extra, more):
        @pl.when(end)
        def _():
            for j in range(4):
                up_copy(first + j).start()

            @pl.when(more)
            def _():
                for j in range(4, 4 + extra):
                    up_copy(first + j).start()

    def zpair_step(c):
        up_copy(c).wait_recv()
        r = zrows(c)
        zpair[r, :] = (zpart[r, :].astype(F32) + zrx[r, :].astype(F32)).astype(BF16)
        mid_copy(c).start()

    def ztot_step(c):
        mid_copy(c).wait_recv()
        r = zrows(c)
        ztot[r, :] = (zpair[r, :].astype(F32) + zrxp[r, :].astype(F32)).astype(BF16)
        down_copy(c).start()

    def zslot(s, pair=True, total=True):
        if isinstance(s, int):
            pair, total = s < steps, 0 <= s - LAG < steps

        @pl.when(mid)
        def _():
            if pair:
                zpair_step(s)
            if total:
                ztot_step(s - LAG)

    def zfin(first, number):
        @pl.when(end)
        def _():
            for j in range(number):
                down_copy(first + j).wait_recv()

    def forward(i, carry):
        base = pl.multiple_of(i * ROWS, 16)
        r = pl.ds(base, ROWS)
        for b in range(nblk):
            rb = pl.ds(base + 16 * b, 16)
            v = xh1[rb, :] * gs[0:1, :] + gs[2:3, :]
            if 16 * (b + 1) > patches:
                row = lax.broadcasted_iota(jnp.int32, (16, D), 0) + 16 * b
                v = jnp.where(row < patches, v, jnp.where(row == patches, 1.0, 0.0))
            normed[rb, :] = v.astype(BF16)
        th[i, K:KA, :] = (lax.broadcasted_iota(jnp.int32, (16, D), 0) == 0).astype(F32).astype(BF16)
        for c in range(0, D, 256):
            tmp[0:K, :] = dot_nn(toki_t[:, 0:ROWS], normed[r, c : c + 256])
            for b in range(0, K, 16):
                value, slope = gelu_pair(tmp[b : b + 16, :])
                th[i, b : b + 16, c : c + 256] = value.astype(BF16)
                tgp[i, b : b + 16, c : c + 256] = slope
            xf[r, c : c + 256] += dot_nn(toko[:, 0:KA], th[i, :, c : c + 256])
        for b in range(nblk):
            rb = pl.ds(base + 16 * b, 16)
            v = xf[rb, :]
            center = v - jnp.mean(v, axis=-1, keepdims=True)
            inv = lax.rsqrt(jnp.mean(center * center, axis=-1, keepdims=True) + 1e-06)
            xhat = center * inv
            xh2[rb, :] = xhat
            rs2[rb, :] = jnp.broadcast_to(inv, (16, 128))
            chan[rb, :] = (xhat * gs[1:2, :] + gs[3:4, :]).astype(BF16)

        @pl.when(i == 0)
        def _():
            cq[me] = chan[0:ROWS, :]
            cqs.start()

        for c in range(0, D, 256):
            tmp[0:ROWS, :] = dot_nn(chan[r, :], w_in[:, c : c + 256])
            a = jnp.zeros((8, 256), F32)
            for b in range(nblk):
                rb = pl.ds(base + 16 * b, 16)
                value, slope = gelu_pair(tmp[16 * b : 16 * b + 16, :] + bs[0:1, c : c + 256])
                hid[rb, c : c + 256] = value.astype(BF16)
                low = (slope * dhid[rb, c : c + 256]).astype(BF16)
                dpre[rb, c : c + 256] = low
                a = a + fold(low.astype(F32))
            acc[5, :, c : c + 256] += a
        for c in range(0, D, 256):
            zpart[r, c : c + 256] = dot_nt(dpre[r, :], w_in[c : c + 256, :]).astype(BF16)
        start_up(4 * i, half - 4 * count, i == count - 1)

        @pl.when(i > 0)
        def _():
            zslot(i - 1, total=False)

        return carry

    lax.fori_loop(0, count, forward, 0)

    def partial_out(i, carry):
        r = pl.ds(pl.multiple_of(i * ROWS, 16), ROWS)
        ro = pl.ds(pl.multiple_of(R + i * ROWS, 16), ROWS)
        for c in range(0, D, 256):
            zpart[ro, c : c + 256] = dot_nn(hid[r, :], w_out[:, c : c + 256]).astype(BF16)
        start_up(half + 4 * i, half - 4 * count, i == count - 1)
        return carry

    lax.fori_loop(0, count, partial_out, 0)
    zslot(2)

    def weight_grad(j, carry):
        cols = pl.ds(pl.multiple_of(j * 256, 256), 256)
        gw[0, cols, :] = dot_tn(chan[:, cols], dpre[...])
        gw[1, cols, :] = dot_tn(dout[:, cols], hid[...])
        return carry

    lax.fori_loop(0, D // 256, weight_grad, 0)
    for c in range(nc):
        rows = pl.ds(pl.multiple_of((2 * c + 1 - core) * shard, 8), shard)
        for m in range(2):
            wsib_s[c, m] = gw[m, rows, :].astype(BF16)
    w_sib = rcopy(wsib_s, wsib_r, w_sem.at[0, 0], w_sem.at[1, 0], (sib, t))
    w_sib.start()
    zslot(3)

    sqs[...] = jnp.zeros(sqs.shape, F32)

    def square(i, carry):
        r = pl.ds(pl.multiple_of(i * ROWS, 16), ROWS)
        g1 = dot_nt(chan[r, :], chan[r, :]) * dot_nt(dpre[r, :], dpre[r, :])
        g2 = dot_nt(dout[r, :], dout[r, :]) * dot_nt(hid[r, :], hid[r, :])
        sqs[pl.ds(i, 1), 0:ROWS] = jnp.sum(g1 + g2, axis=0, keepdims=True)
        return carry

    lax.fori_loop(0, count, square, 0)
    zslot(4)

    w_sib.wait_recv()

    def w_chip(n, k):
        return rcopy(wch_s.at[n], wch_r.at[n], w_sem.at[0, n + 1], w_sem.at[1, n + 1], (peer(k), t))

    def w_share(dest, m):
        rows = pl.ds(pl.multiple_of((2 * dest + core) * shard, 8), shard)
        return gw[m, rows, :] + wsib_r[dest, m].astype(F32)

    first, second = 1 + core, 2 - core
    for n, dest in ((0, chip ^ 3), (1, chip ^ first)):
        for m in range(2):
            wch_s[n, m] = w_share(dest, m).astype(BF16)
        w_chip(n, first).start()

    infl[...] = jnp.zeros(infl.shape, F32)

    def query(j, carry):
        k = j // 2
        own = j % 2 == 0
        slot = jnp.where(own, peer(k), peer_sib(k))

        @pl.when(jnp.logical_not(own))
        def _():
            dqs.from_sib(k)
            cqs.from_sib(k)

        zslot(j + jnp.where(j < 2, 5, half + LAG + 2))
        for c in range(0, D, 256):
            tmp[0:ROWS, :] = dot_nn(cq[slot], w_in[:, c : c + 256])
            tmp[ROWS : 2 * ROWS, :] = dot_nt(dq[slot], w_out[c : c + 256, :])
            for b in range(0, ROWS, 16):
                value, slope = gelu_pair(tmp[b : b + 16, :] + bs[0:1, c : c + 256])
                hq[b : b + 16, c : c + 256] = value.astype(BF16)
                pq[b : b + 16, c : c + 256] = (slope * tmp[ROWS + b : ROWS + b + 16, :]).astype(BF16)
        for q in range(count - QRY_DEV):
            r = slice((QRY_DEV + q) * ROWS, (QRY_DEV + q + 1) * ROWS)
            g1 = dot_nt(cq[slot], chan[r, :]) * dot_nt(pq[...], dpre[r, :])
            g2 = dot_nt(dq[slot], dout[r, :]) * dot_nt(hq[...], hid[r, :])
            infl[q, pl.ds(slot, 1), 0:ROWS] = jnp.sum(g1 + g2, axis=0, keepdims=True)
        return carry

    lax.fori_loop(0, 2, query, 0)
    for s in range(7, half + LAG):
        zslot(s)
        if s == 7:
            for k in (1, 2):
                dqs.relay(k)
        if s == 9:
            dqs.relay(3)
            for k in (1, 2):
                cqs.relay(k)
        if s == 11:
            w_chip(0, first).wait_recv()
            for m in range(2):
                wch_s[2, m] = (w_share(chip ^ second, m) + wch_r[0, m].astype(F32)).astype(BF16)
            w_chip(2, second).start()

    gtok[...] = jnp.zeros(gtok.shape, F32)

    def ing_copy(i):
        return pltpu.make_async_copy(ing_s.at[i], ing_o.at[i], out_sem.at[0, i])

    def backward(i, carry):
        @pl.when(i == 0)
        def _():
            zfin(0, 1)

        zfin(4 * i + 1, 4)
        base = pl.multiple_of(i * ROWS, 16)
        r = pl.ds(base, ROWS)
        a1 = jnp.zeros((8, D), F32)
        a3 = jnp.zeros((8, D), F32)
        for b in range(nblk):
            rb = pl.ds(base + 16 * b, 16)
            e = ztot[rb, :].astype(F32)
            xhat = xh2[rb, :]
            a1 = a1 + fold(e * xhat)
            a3 = a3 + fold(e)
            eg = e * gs[1:2, :]
            m1 = jnp.mean(eg, axis=-1, keepdims=True)
            m2 = jnp.mean(eg * xhat, axis=-1, keepdims=True)
            d = dout[rb, :].astype(F32) + rs2[rb, 0:1] * (eg - m1 - xhat * m2)
            dhid[rb, :] = d
            dmix[16 * b : 16 * b + 16, :] = d.astype(BF16)
        acc[1] += a1
        acc[3] += a3
        for c in range(0, D, 256):
            tmp[0:K, :] = dot_nn(toko_t[0:K, 0:ROWS], dmix[:, c : c + 256])
            for b in range(0, K, 16):
                dtok[b : b + 16, c : c + 256] = (
                    tmp[b : b + 16, :] * tgp[i, b : b + 16, c : c + 256]
                ).astype(BF16)
        gtok[0, 0:K, 0:ROWS] += dot_nt(dtok[...], normed[r, :])
        gtok[1, :, 0:ROWS] += dot_nt(th[i], dmix[...])
        for c in range(0, D, 256):
            dnorm[:, c : c + 256] = dot_nn(toki[:, 0:K], dtok[:, c : c + 256])
        a0 = jnp.zeros((8, D), F32)
        a2 = jnp.zeros((8, D), F32)
        for b in range(nblk):
            rb = pl.ds(base + 16 * b, 16)
            e = dnorm[16 * b : 16 * b + 16, :]
            xhat = xh1[rb, :]
            a0 = a0 + fold(e * xhat)
            a2 = a2 + fold(e)
            eg = e * gs[0:1, :]
            m1 = jnp.mean(eg, axis=-1, keepdims=True)
            m2 = jnp.mean(eg * xhat, axis=-1, keepdims=True)
            d = (dhid[rb, :] + rs1[rb, 0:1] * (eg - m1 - xhat * m2)).astype(BF16)
            n = min(16, patches - 16 * b)
            ing_s[i, 16 * b : 16 * b + n, :] = d[0:n]
        acc[0] += a0
        acc[2] += a2
        ing_copy(i).start()
        zslot(half + LAG + i)
        return carry

    lax.fori_loop(0, count, backward, 0)

    for c in range(nc):
        rows = pl.ds(pl.multiple_of((2 * c + 1 - core) * kb, 8), kb)
        for m in range(2):
            tsib_s[c, m] = gtok[m, rows, :]
    t_sib = rcopy(tsib_s, tsib_r, t_sem.at[0, 0], t_sem.at[1, 0], (sib, t))
    t_sib.start()
    vec[...] = jnp.zeros(vec.shape, F32)
    for q in range(6):
        vec[q : q + 1, :] = jnp.sum(acc[q], axis=0, keepdims=True)
    vec[6:7, 0:256] = gtok[1, K : K + 1, :]
    v_sib = rcopy(vec, vsib_r, v_sem.at[0, 0], v_sem.at[1, 0], (sib, t))
    v_sib.start()
    zslot(half + LAG + count)
    v_sib.wait_recv()

    def v_chip(k):
        return rcopy(
            vch.at[chip], vch.at[chip], v_sem.at[0, k], v_sem.at[1, k], (peer(k), t)
        )

    vch[chip] = vec[...] + vsib_r[...]
    for k in range(1, nc):
        v_chip(k).start()
    t_sib.wait_recv()

    def t_chip(k):
        return rcopy(
            tch_s.at[k - 1], tch_r.at[k - 1], t_sem.at[0, k], t_sem.at[1, k], (peer(k), t)
        )

    for k in range(1, nc):
        dest = chip ^ k
        rows = pl.ds(pl.multiple_of((2 * dest + core) * kb, 8), kb)
        for m in range(2):
            tch_s[k - 1, m] = gtok[m, rows, :] + tsib_r[dest, m]
        t_chip(k).start()


    cqs.relay(3)
    lax.fori_loop(2, n_dp, query, 0)
    at = half + LAG + 2 + n_dp

    def as_row(values):
        totals = jnp.sum(values, axis=1, keepdims=True)
        at = lax.broadcasted_iota(jnp.int32, (values.shape[0], 128), 0)
        lane = lax.broadcasted_iota(jnp.int32, (values.shape[0], 128), 1)
        return jnp.sum(jnp.where(at == lane, totals, 0.0), axis=0, keepdims=True)

    zsm[t] = jnp.zeros((8, 128), F32)
    zsm[t, 0:1, :] = as_row(sqs[...]) / (2.0 * D * FF)
    for q in range(count - QRY_DEV):
        zsm[t, 1 + q : 2 + q, :] = as_row(infl[q]) * (2.0 * D * FF) ** (-0.5)

    def sm_copy(k):
        return rcopy(
            zsm.at[t], zsm.at[t], s_sem.at[0, k - 1], s_sem.at[1, k - 1], (me, (t + k) % 4)
        )

    for k in (1, 2, 3):
        sm_copy(k).start()

    for m, out in enumerate((gwi_o, gwo_o)):
        out[...] = w_share(chip, m)
    for n in (1, 2):
        w_chip(n, first).wait_recv()
        for m, out in enumerate((gwi_o, gwo_o)):
            out[...] += wch_r[n, m].astype(F32)
    zslot(at)
    for k in (1, 2, 3):
        sm_copy(k).wait_recv()
    sm_o[...] = (zsm[0] + zsm[1]) + (zsm[2] + zsm[3])
    rows = pl.ds(pl.multiple_of(me * kb, 8), kb)
    for m, out in enumerate((gti_o, gto_o)):
        out[...] = gtok[m, rows, :] + tsib_r[chip, m]
    for k in range(1, nc):
        t_chip(k).wait_recv()
        for m, out in enumerate((gti_o, gto_o)):
            out[...] += tch_r[k - 1, m]
    for k in range(1, nc):
        v_chip(k).wait_recv()
    total = vch[0]
    for c in range(1, nc):
        total = total + vch[c]
    tbo_o[...] = total[:, 0:256]
    vec_o[...] = pltpu.roll(total, (D - me * shard) % D, 1)[:, 0:128]


    def act_copy(i):
        return pltpu.make_async_copy(act_s.at[i], act_o.at[i], out_sem.at[1, i])

    at += 1
    for i in range(count):
        need = -(-((i + 1) * ROWS) // CHUNK) + half
        while at < min(need + LAG, steps + LAG):
            zslot(at)
            at += 1
        first = half if i == 0 else -(-(i * ROWS) // CHUNK) + half
        zfin(first, need - first)
        for b in range(nblk):
            n = min(16, patches - 16 * b)
            rb = slice(i * ROWS + 16 * b, i * ROWS + 16 * b + 16)
            ro = slice(R + i * ROWS + 16 * b, R + i * ROWS + 16 * b + 16)
            a = (xf[rb, :] + ztot[ro, :].astype(F32) + bs[1:2, :]).astype(BF16)
            act_s[i, 16 * b : 16 * b + n, :] = a[0:n]
        act_copy(i).start()

    params.drain()
    dqs.drain()
    cqs.drain()

    def drain_end(c, carry):
        up_copy(c).wait_send()
        return carry

    def drain_mid(c, carry):
        mid_copy(c).wait_send()
        down_copy(c).wait_send()
        return carry

    @pl.when(end)
    def _():
        lax.fori_loop(0, steps, drain_end, 0)

    @pl.when(mid)
    def _():
        lax.fori_loop(0, steps, drain_mid, 0)

    w_sib.wait_send()
    t_sib.wait_send()
    v_sib.wait_send()
    for k in range(1, nc):
        w_chip(k - 1, first).wait_send()
        t_chip(k).wait_send()
        v_chip(k).wait_send()
    for k in (1, 2, 3):
        sm_copy(k).wait_send()
    for i in range(count):
        ing_copy(i).wait()
        act_copy(i).wait()


def finish(shard, ks, patches, count, queries, act, ing, gwi, gwo, gti, gto, vec, tbo, sm, *refs):
    big, small, held, sem = refs[:4], refs[4:14], refs[14:18], refs[18]
    pieces = [(n, i) for n in (0, 1) for i in range(count)] + [(2, None), (3, None)]

    def part(ref, i):
        return ref if i is None else ref.at[i]

    loads, stores = [], []
    for at, (n, i) in enumerate(pieces):
        kept = part(held[n], i)
        loads.append(pltpu.make_async_copy(part((act, ing, gwi, gwo)[n], i), kept, sem.at[0, at]))
        stores.append(pltpu.make_async_copy(kept, part(big[n], i), sem.at[1, at]))
        loads[-1].start()
    gains, shifts, gti_o, gto_o, gtb_o, tbo_o, gbi_o, gbo_o, sq_o, infl_o = small
    gains[...] = vec[0:2, 0:shard]
    shifts[...] = vec[2:4, 0:shard]
    gbo_o[...] = vec[4:5, 0:shard]
    gbi_o[...] = vec[5:6, 0:shard]
    gti_o[...] = gti[0:ks, 0:patches]
    gto_o[...] = gto[0:ks, 0:patches]
    tbo_o[...] = tbo[6:7, 0:patches]
    column = gti[0:ks, patches : patches + 1]
    eye = lax.broadcasted_iota(jnp.int32, (ks, ks), 0) == lax.broadcasted_iota(jnp.int32, (ks, ks), 1)
    gtb_o[...] = jnp.sum(jnp.where(eye, column, 0.0), axis=0, keepdims=True)
    sq_o[...] = sm[0:1, 0:count]
    for t in range(infl_o.shape[0]):
        infl_o[t : t + 1, :] = sm[1 + t : 2 + t, 0:queries]
    for load, store in zip(loads, stores):
        load.wait()
        store.start()
    for store in stores:
        store.wait()


def fused(
    n_dp,
    images,
    cotangent,
    norm_gains,
    norm_shifts,
    tok_in,
    tok_out_t,
    tok_bias_in,
    tok_bias_out,
    w_in,
    bias_in,
    w_out,
    bias_out,
):
    count, patches, width = images.shape
    nc = n_dp // 2
    ks = tok_in.shape[1]
    toks = ks * n_dp
    kb = -(-ks // 16) * 16
    K = n_dp * kb
    KA = K + 16
    KL = -(-KA // 128) * 128
    R = count * ROWS
    steps = 2 * (R // CHUNK)
    shard = width // n_dp
    hidden = w_in.shape[1]
    anyspace = pl.BlockSpec(memory_space=pl.ANY)
    vm = pl.BlockSpec(memory_space=pltpu.VMEM)
    V = pltpu.VMEM
    dma = lambda *s: pltpu.SemaphoreType.DMA(s)
    scratch = dict(
        x_raw=V((count, patches, D), BF16),
        d_raw=V((count, patches, D), BF16),
        w_in=V((D, hidden), BF16),
        w_out=V((hidden, D), BF16),
        act_s=V((count, patches, D), BF16),
        ing_s=V((count, patches, D), BF16),
        pb=V((n_dp, 2 * kb + 16, 256), BF16),
        aug=V((ROWS, 128), F32),
        misc=V((16, 256), F32),
        toki_t=V((K, 256), BF16),
        toko_t=V((KA, 256), BF16),
        toki=V((ROWS, KL), BF16),
        toko=V((ROWS, KL), BF16),
        gs=V((16, D), F32),
        bs=V((8, D), F32),
        dout=V((R, D), BF16),
        dhid=V((R, hidden), F32),
        xf=V((R, D), F32),
        xh1=V((R, D), F32),
        rs1=V((R, 128), F32),
        xh2=V((R, D), F32),
        rs2=V((R, 128), F32),
        normed=V((R, D), BF16),
        th=V((count, KA, D), BF16),
        tgp=V((count, K, D), F32),
        chan=V((R, D), BF16),
        hid=V((R, hidden), BF16),
        dpre=V((R, hidden), BF16),
        tmp=V((max(K, 2 * ROWS), 256), F32),
        dq=V((n_dp, ROWS, D), BF16),
        cq=V((n_dp, ROWS, D), BF16),
        hq=V((ROWS, hidden), BF16),
        pq=V((ROWS, hidden), BF16),
        infl=V((count - QRY_DEV, n_dp, 256), F32),
        sqs=V((8, 256), F32),
        dmix=V((ROWS, D), BF16),
        dtok=V((K, D), BF16),
        dnorm=V((ROWS, D), F32),
        zpart=V((2 * R, D), BF16),
        zrx=V((2 * R, D), BF16),
        zpair=V((2 * R, D), BF16),
        zrxp=V((2 * R, D), BF16),
        ztot=V((2 * R, D), BF16),
        gw=V((2, D, hidden), F32),
        wsib_s=V((nc, 2, shard, hidden), BF16),
        wsib_r=V((nc, 2, shard, hidden), BF16),
        wch_s=V((nc - 1, 2, shard, hidden), BF16),
        wch_r=V((nc - 1, 2, shard, hidden), BF16),
        gtok=V((2, KA, 256), F32),
        tsib_s=V((nc, 2, kb, 256), F32),
        tsib_r=V((nc, 2, kb, 256), F32),
        tch_s=V((nc - 1, 2, kb, 256), F32),
        tch_r=V((nc - 1, 2, kb, 256), F32),
        acc=V((6, 8, D), F32),
        vec=V((8, D), F32),
        vsib_r=V((8, D), F32),
        vch=V((nc, 8, D), F32),
        zsm=V((4, 8, 128), F32),
        in_sem=dma(4),
        out_sem=dma(2, count),
        pb_c=dma(2, nc - 1),
        pb_x=dma(2, nc),
        dq_c=dma(2, nc - 1),
        dq_x=dma(2, nc),
        cq_c=dma(2, nc - 1),
        cq_x=dma(2, nc),
        ze=dma(2, steps),
        zm=dma(2, steps),
        zt=dma(2, steps),
        w_sem=dma(2, nc),
        t_sem=dma(2, nc),
        v_sem=dma(2, nc),
        s_sem=dma(2, 3),
    )
    outs = [
        (images.shape, BF16, anyspace),
        (images.shape, BF16, anyspace),
        ((shard, hidden), F32, vm),
        ((shard, hidden), F32, vm),
        ((kb, 256), F32, vm),
        ((kb, 256), F32, vm),
        ((8, 128), F32, vm),
        ((8, 256), F32, vm),
        ((8, 128), F32, vm),
    ]
    names = list(scratch)
    n_in, n_out = 12, len(outs)

    def body(*refs):
        mega(n_dp, count, patches, toks, *refs[: n_in + n_out], **dict(zip(names, refs[n_in + n_out :])))

    act, ing, gwi, gwo, gti, gto, vec, tbo, sm = pl.pallas_call(
        body,
        out_shape=[jax.ShapeDtypeStruct(s, d) for s, d, _ in outs],
        in_specs=[anyspace] * 4 + [vm] * 8,
        out_specs=[o[2] for o in outs],
        scratch_shapes=list(scratch.values()),
        compiler_params=pltpu.CompilerParams(
            collective_id=0, has_side_effects=True, vmem_limit_bytes=60 * 2**20
        ),
        name="mixer",
    )(
        images,
        cotangent,
        w_in,
        w_out,
        norm_gains,
        norm_shifts,
        tok_in.T,
        tok_out_t.T,
        tok_bias_in,
        tok_bias_out,
        bias_in,
        bias_out,
    )
    queries, trains = n_dp * QRY_DEV, count - QRY_DEV
    out = pl.pallas_call(
        functools.partial(finish, shard, ks, patches, count, queries),
        out_shape=[
            jax.ShapeDtypeStruct(s, d)
            for s, d in (
                (images.shape, BF16),
                (images.shape, BF16),
                ((shard, hidden), F32),
                ((shard, hidden), F32),
                ((2, shard), F32),
                ((2, shard), F32),
                ((ks, patches), F32),
                ((ks, patches), F32),
                ((1, ks), F32),
                ((1, patches), F32),
                ((1, shard), F32),
                ((1, shard), F32),
                ((1, count), F32),
                ((trains, queries), F32),
            )
        ],
        in_specs=[anyspace] * 4 + [vm] * 5,
        out_specs=[anyspace] * 4 + [vm] * 10,
        scratch_shapes=[
            V(images.shape, BF16),
            V(images.shape, BF16),
            V((shard, hidden), F32),
            V((shard, hidden), F32),
            dma(2, 2 * count + 2),
        ],
        name="finish",
    )(act, ing, gwi, gwo, gti, gto, vec, tbo, sm)
    act, ing, gwi, gwo, gains, shifts, gti, gto, gtb, tbo, gbi, gbo, squares, influence = out
    return (
        act,
        ing,
        gains,
        shifts,
        gti.T,
        gto.T,
        gtb,
        tbo.reshape(patches),
        gwi,
        gbi.reshape(shard),
        gwo.T,
        gbo.reshape(shard),
        squares.reshape(count),
        influence.T,
    )


def layer_norm(values, gain, shift):
    center = values - jnp.mean(values, axis=-1, keepdims=True)
    spread = jnp.mean(center * center, axis=-1, keepdims=True)
    return center * lax.rsqrt(spread + 1e-06) * gain + shift


def smooth(values):
    return jax.nn.gelu(values, approximate=True)


def contract(left, right, left_dim, right_dim):
    return lax.dot_general(
        left, right, (((left_dim,), (right_dim,)), ((), ())), preferred_element_type=jnp.float32
    )


def per_device(
    images,
    cotangent,
    norm_gains,
    norm_shifts,
    tok_in,
    tok_out_t,
    tok_bias_in,
    tok_bias_out,
    w_in,
    bias_in,
    w_out,
    bias_out,
):
    gains, shifts, tok_first, tok_second, tok_bias = (
        lax.all_gather(norm_gains, "dp", axis=1, tiled=True),
        lax.all_gather(norm_shifts, "dp", axis=1, tiled=True),
        lax.all_gather(tok_in, "dp", axis=1, tiled=True),
        lax.all_gather(tok_out_t, "dp", axis=1, tiled=True),
        lax.all_gather(tok_bias_in, "dp", axis=1, tiled=True),
    )
    gains = gains.astype(jnp.float32)
    shifts = shifts.astype(jnp.float32)
    count, patches, width = images.shape
    rows = count * patches
    inputs = images.astype(jnp.float32)
    normed_one, first_back = jax.vjp(layer_norm, inputs, gains[0], shifts[0])
    normed_low = normed_one.astype(jnp.bfloat16)
    tok_pre = (
        jnp.einsum("sk,nsd->nkd", tok_first, normed_low, preferred_element_type=jnp.float32)
        + tok_bias[0].astype(jnp.float32)[None, :, None]
    )
    tok_hidden = smooth(tok_pre).astype(jnp.bfloat16)
    tok_mixed = (
        jnp.einsum("sk,nkd->nsd", tok_second, tok_hidden, preferred_element_type=jnp.float32)
        + tok_bias_out.astype(jnp.float32)[None, :, None]
    )
    resid = inputs + tok_mixed
    normed_two, second_back = jax.vjp(layer_norm, resid, gains[1], shifts[1])
    chan_in = normed_two.astype(jnp.bfloat16).reshape(rows, width)
    chan_pre = jnp.dot(chan_in, w_in, preferred_element_type=jnp.float32) + bias_in.astype(
        jnp.float32
    )
    hidden = smooth(chan_pre).astype(jnp.bfloat16)
    partial_out = jnp.dot(hidden, w_out, preferred_element_type=jnp.float32)
    mixed = lax.psum(partial_out, "tensor")
    activations = (
        resid + mixed.reshape(count, patches, width) + bias_out.astype(jnp.float32)
    ).astype(jnp.bfloat16)
    dout_rows = cotangent.reshape(rows, width)
    d_hidden = contract(dout_rows, w_out, 1, 1)
    smooth_value, smooth_back = jax.vjp(smooth, chan_pre)
    d_pre = smooth_back(d_hidden)[0].astype(jnp.bfloat16)
    d_chan_part = contract(d_pre, w_in, 1, 1)
    d_chan = lax.psum(d_chan_part, "tensor")
    d_resid_norm, d_gain_two, d_shift_two = second_back(d_chan.reshape(count, patches, width))
    d_resid = cotangent.astype(jnp.float32) + d_resid_norm
    d_mixed = d_resid.astype(jnp.bfloat16)
    d_tokhid = jnp.einsum("sk,nsd->nkd", tok_second, d_mixed, preferred_element_type=jnp.float32)
    tok_value, tok_back = jax.vjp(smooth, tok_pre)
    d_tokpre = tok_back(d_tokhid)[0].astype(jnp.bfloat16)
    grad_second = jnp.einsum("nsd,nkd->sk", d_mixed, tok_hidden, preferred_element_type=jnp.float32)
    grad_first = jnp.einsum("nsd,nkd->sk", normed_low, d_tokpre, preferred_element_type=jnp.float32)
    grad_tbias = jnp.sum(d_tokpre, axis=(0, 2), dtype=jnp.float32)[None, :]
    grad_tbias_out = jnp.sum(d_mixed, axis=(0, 2), dtype=jnp.float32)
    d_normed = jnp.einsum("sk,nkd->nsd", tok_first, d_tokpre, preferred_element_type=jnp.float32)
    d_input_norm, d_gain_one, d_shift_one = first_back(d_normed)
    input_grad = (d_resid + d_input_norm).astype(jnp.bfloat16)
    grad_win = contract(chan_in, d_pre, 0, 0)
    grad_wout_t = contract(dout_rows, hidden, 0, 0)
    grad_bin = jnp.sum(d_pre, axis=0, dtype=jnp.float32)
    grad_bout = jnp.sum(dout_rows, axis=0, dtype=jnp.float32)
    share_win, share_wout_t, share_bin, share_bout = (
        lax.psum_scatter(grad_win, "dp", scatter_dimension=0, tiled=True),
        lax.psum_scatter(grad_wout_t, "dp", scatter_dimension=0, tiled=True),
        lax.psum_scatter(grad_bin, "dp", scatter_dimension=0, tiled=True),
        lax.psum_scatter(grad_bout, "dp", scatter_dimension=0, tiled=True),
    )
    share_gains, share_shifts, share_first, share_second, share_tbias = (
        lax.psum_scatter(
            jnp.stack([d_gain_one, d_gain_two]), "dp", scatter_dimension=1, tiled=True
        ),
        lax.psum_scatter(
            jnp.stack([d_shift_one, d_shift_two]), "dp", scatter_dimension=1, tiled=True
        ),
        lax.psum_scatter(grad_first, "dp", scatter_dimension=1, tiled=True),
        lax.psum_scatter(grad_second, "dp", scatter_dimension=1, tiled=True),
        lax.psum_scatter(grad_tbias, "dp", scatter_dimension=1, tiled=True),
    )
    total_tbias_out = lax.psum(grad_tbias_out, "dp")
    chan_cube = chan_in.reshape(count, patches, width)
    pre_cube = d_pre.reshape(count, patches, -1)
    hidden_cube = hidden.reshape(count, patches, -1)
    def against(chan, pre, dout, low):
        grams = [
            jnp.einsum("sd,npd->nsp", a, b, preferred_element_type=jnp.float32)
            for a, b in ((chan, chan_cube), (pre, pre_cube), (dout, cotangent), (low, hidden_cube))
        ]
        return jnp.sum(grams[0] * grams[1] + grams[2] * grams[3], axis=(1, 2))

    own = lax.map(lambda a: against(*a), (chan_cube, pre_cube, cotangent, hidden_cube))
    squares = jnp.diagonal(own)
    queries = tuple(
        lax.all_gather(a[:QRY_DEV], "dp", axis=0, tiled=True)
        for a in (chan_cube, pre_cube, cotangent, hidden_cube)
    )
    influence = lax.map(lambda a: against(*a), queries)[:, QRY_DEV:]
    influence, squares = lax.psum((influence, squares), "tensor")
    sqnorms = squares / (2.0 * D * FF)
    influence = influence * (2.0 * D * FF) ** (-0.5)
    return (
        activations,
        input_grad,
        share_gains,
        share_shifts,
        share_first,
        share_second,
        share_tbias,
        total_tbias_out,
        share_win,
        share_bin,
        share_wout_t.T,
        share_bout,
        sqnorms,
        influence,
    )


def solution(mesh):
    placed = (
        P("dp", None, None),
        P("dp", None, None),
        P(None, "dp"),
        P(None, "dp"),
        P(None, "dp"),
        P(None, "dp"),
        P(None, "dp"),
        P(),
        P(None, "tensor"),
        P("tensor"),
        P("tensor", None),
        P(),
    )
    n_dp = mesh.shape["dp"]
    fits = n_dp == 8 and mesh.shape["tensor"] == 4
    device = functools.partial(fused, n_dp) if fits else per_device
    return jax.shard_map(
        device,
        mesh=mesh,
        in_specs=placed,
        out_specs=(
            P("dp", None, None),
            P("dp", None, None),
            P(None, "dp"),
            P(None, "dp"),
            P(None, "dp"),
            P(None, "dp"),
            P(None, "dp"),
            P(),
            P("dp", "tensor"),
            P(("tensor", "dp")),
            P("tensor", "dp"),
            P("dp"),
            P("dp"),
            P(None, "dp"),
        ),
        check_vma=False,
    )
```

```python
import functools

import jax
import jax.numpy as jnp
from jax import lax
from jax.experimental import pallas as pl
from jax.experimental.pallas import tpu as pltpu
from jax.sharding import PartitionSpec as P

D = 768
FF = 3072
QRY_DEV = 1
HIGH = lax.Precision.HIGHEST
MESH = pl.DeviceIdType.MESH
F32 = jnp.float32
BF16 = jnp.bfloat16

ROWS = 208
C1 = 0.7978845608028654
C2 = 0.044715


def dot_nn(a, b):
    return lax.dot_general(a, b, (((1,), (0,)), ((), ())), preferred_element_type=F32)


def dot_nt(a, b):
    return lax.dot_general(a, b, (((1,), (1,)), ((), ())), preferred_element_type=F32)


def dot_tn(a, b):
    return lax.dot_general(a, b, (((0,), (0,)), ((), ())), preferred_element_type=F32)


def gelu_pair(v):
    u = v * v
    th = jnp.tanh(v * (C1 + (C1 * C2) * u))
    hp = 0.5 + 0.5 * th
    value = v * hp
    slope = hp + (0.5 * v) * (1.0 - th * th) * (C1 + (3.0 * C1 * C2) * u)
    return value, slope


def z_sizes(count):
    full = [64] * (3 * count)
    return full + [16, 16] + full


def fold(v):
    out = v[0:8]
    for s in range(8, v.shape[0], 8):
        out = out + v[s : s + 8]
    return out


def mega(
    n_dp,
    count,
    patches,
    toks,
    images,
    cotangent,
    w_in_h,
    w_out_h,
    gains_h,
    shifts_h,
    tok_in_h,
    tok_out_h,
    tok_bias_h,
    tok_bias_out_h,
    bias_in_h,
    bias_out_h,
    act_o,
    ing_o,
    gwi_o,
    gwo_o,
    gti_o,
    gto_o,
    vec_o,
    tbo_o,
    sm_o,
    gains_r,
    shifts_r,
    tok_in_r,
    tok_out_r,
    tok_bias_r,
    tok_bias_out_r,
    bias_in_r,
    bias_out_r,
    x_raw,
    d_raw,
    w_in,
    w_out,
    act_s,
    ing_s,
    pb,
    aug,
    misc,
    toki_t,
    toko_t,
    toki,
    toko,
    gs,
    bs,
    dout,
    dhid,
    xf,
    xh1,
    rs1,
    xh2,
    rs2,
    normed,
    th,
    tgp,
    chan,
    hid,
    dpre,
    tmp,
    dq,
    cq,
    hq,
    pq,
    infl,
    sqs,
    dmix,
    dtok,
    dnorm,
    tails,
    rests,
    zpart,
    zrx,
    zpair,
    zrxp,
    ztot,
    gw,
    wsib_s,
    wsib_r,
    wch_s,
    wch_r,
    gtok,
    tsib_s,
    tsib_r,
    tch_s,
    tch_r,
    acc,
    vec,
    vsib_r,
    vch,
    zsm,
    in_sem,
    out_sem,
    pb_sem,
    dq_sem,
    cq_sem,
    z_sem,
    z_sent,
    w_sem,
    t_sem,
    v_sem,
    s_sem,
):
    me = lax.axis_index("dp")
    t = lax.axis_index("tensor")
    core = me % 2
    chip = me // 2
    sib = chip * 2 + 1 - core
    nc = n_dp // 2
    mid = (t == 1) | (t == 2)
    end = (t == 0) | (t == 3)
    end_peer = jnp.where(t < 2, 1, 2)
    mid_end = jnp.where(t < 2, 0, 3)
    mid_peer = 3 - t
    shard = D // n_dp
    ks = toks // n_dp
    kb = -(-ks // 16) * 16
    K = n_dp * kb
    KA = K + 16
    R = count * ROWS
    nblk = ROWS // 16
    last = ROWS - 16
    tail = patches - last

    def peer(k):
        return (chip ^ k) * 2 + core

    def peer_sib(k):
        return (chip ^ k) * 2 + 1 - core

    def rcopy(a, b, ss, rs, dev):
        return pltpu.make_async_remote_copy(
            src_ref=a, dst_ref=b, send_sem=ss, recv_sem=rs, device_id=dev, device_id_type=MESH
        )

    class Gather:
        def __init__(self, buf, sem):
            self.buf, self.sem = buf, sem

        def chip_copy(self, block, k, n):
            b = self.buf.at[block]
            return rcopy(b, b, self.sem.at[0], self.sem.at[1 + n], (peer(k), t))

        def sib_copy(self, k):
            b = self.buf.at[peer(k)]
            return rcopy(b, b, self.sem.at[0], self.sem.at[4 + k], (sib, t))

        def start(self, across=False):
            for k in (1, 2, 3) if across else (1, 2):
                self.chip_copy(me, k, k - 1).start()
            self.sib_copy(0).start()

        def relay(self, k, across=False):
            self.chip_copy(peer(k), k, k - 1).wait_recv()
            if k < 3 and not across:

                @pl.when(core == k - 1)
                def _():
                    self.chip_copy(peer(k), 3 - k, 2).start()

            self.sib_copy(k).start()

        def from_sib(self, k):
            b = self.buf.at[peer_sib(k)]
            rcopy(b, b, self.sem.at[0], self.sem.at[4 + k], (sib, t)).wait_recv()

        def drain(self):
            b = self.buf.at[pl.ds(0, 7)]
            rcopy(b, b, self.sem.at[0], self.sem.at[1], (sib, t)).wait_send()

    params, dqs, cqs = Gather(pb, pb_sem), Gather(dq, dq_sem), Gather(cq, cq_sem)

    barrier = pltpu.get_barrier_semaphore()
    others = [(sib, t)] + [(peer(k), t) for k in range(1, nc)] + [(me, (t + k) % 4) for k in (1, 2, 3)]
    for dev in others:
        pl.semaphore_signal(barrier, inc=1, device_id=dev, device_id_type=MESH)

    pairs = [
        (gains_h, gains_r),
        (shifts_h, shifts_r),
        (tok_in_h, tok_in_r),
        (tok_out_h, tok_out_r),
        (tok_bias_h, tok_bias_r),
        (cotangent, d_raw),
        (w_out_h, w_out),
        (images, x_raw),
        (w_in_h, w_in),
        (tok_bias_out_h, tok_bias_out_r),
        (bias_in_h, bias_in_r),
        (bias_out_h, bias_out_r),
    ]
    loads = [pltpu.make_async_copy(a, b, in_sem.at[n]) for n, (a, b) in enumerate(pairs)]
    for c in loads:
        c.start()

    pb[me] = jnp.zeros(pb.shape[1:], BF16)
    eye = (
        lax.broadcasted_iota(jnp.int32, (kb, 128), 0) == lax.broadcasted_iota(jnp.int32, (kb, 128), 1)
    ).astype(BF16)
    aug[...] = jnp.zeros(aug.shape, F32)
    misc[...] = jnp.zeros(misc.shape, F32)
    for c in loads[:5]:
        c.wait()
    aug[patches : patches + 1, 0:ks] = tok_bias_r[...].astype(F32)
    pb[me, 0:kb, 0:ROWS] = dot_nt(eye, aug[...].astype(BF16)).astype(BF16)
    pb[me, 0:ks, 0:patches] = tok_in_r[...]
    pb[me, kb : kb + ks, 0:patches] = tok_out_r[...]
    misc[0:2, 0:shard] = gains_r[...].astype(F32)
    misc[2:4, 0:shard] = shifts_r[...].astype(F32)
    pb[me, 2 * kb : 2 * kb + 16, :] = misc[...].astype(BF16)

    pl.semaphore_wait(barrier, len(others))
    params.start(across=True)

    loads[5].wait()
    misc[...] = jnp.zeros(misc.shape, F32)
    acc[...] = jnp.zeros(acc.shape, F32)

    def pad_dout(i):
        base = i * ROWS
        dout[pl.ds(base, last), :] = d_raw[i, 0:last, :]
        for c in range(0, D, 256):
            misc[0:tail, :] = d_raw[i, last:patches, c : c + 256].astype(F32)
            dout[pl.ds(base + last, 16), c : c + 256] = misc[...].astype(BF16)
        a = jnp.zeros((8, D), F32)
        for b in range(nblk):
            a = a + fold(dout[pl.ds(base + 16 * b, 16), :].astype(F32))
        acc[4] += a

    for i in range(count):
        pad_dout(i)
    dq[me] = dout[0:ROWS, :]

    loads[6].wait()

    def hidden_grad(i):
        r = pl.ds(i * ROWS, ROWS)
        for c in range(0, D, 256):
            dhid[r, c : c + 256] = dot_nt(dout[r, :], w_out[c : c + 256, :])

    for i in range(count):
        hidden_grad(i)

    loads[7].wait()

    def first_norm(i):
        base = i * ROWS
        xf[pl.ds(base + last, 16), :] = jnp.zeros((16, D), F32)
        xf[pl.ds(base, last), :] = x_raw[i, 0:last, :].astype(F32)
        xf[pl.ds(base + last, tail), :] = x_raw[i, last:patches, :].astype(F32)
        for b in range(nblk):
            r = pl.ds(base + 16 * b, 16)
            v = xf[r, :]
            center = v - jnp.mean(v, axis=-1, keepdims=True)
            inv = lax.rsqrt(jnp.mean(center * center, axis=-1, keepdims=True) + 1e-06)
            xh1[r, :] = center * inv
            rs1[r, :] = jnp.broadcast_to(inv, (16, 128))

    for i in range(count):
        first_norm(i)

    for k in (1, 2, 3):
        params.relay(k, across=True)
    for k in range(nc):
        params.from_sib(k)
    dqs.start()
    for c in loads[8:]:
        c.wait()
    full = jnp.zeros((16, D), F32)
    for d in range(n_dp):
        toki_t[d * kb : (d + 1) * kb, :] = pb[d, 0:kb, :]
        toko_t[d * kb : (d + 1) * kb, :] = pb[d, kb : 2 * kb, :]
        part = pb[d, 2 * kb : 2 * kb + 16, 0:128].astype(F32)
        part = jnp.concatenate([part, jnp.zeros((16, D - 128), F32)], axis=1)
        full = full + (pltpu.roll(part, d * shard, 1) if d else part)
    gs[...] = full
    misc[...] = jnp.zeros(misc.shape, F32)
    misc[0:1, 0:patches] = tok_bias_out_r[...].astype(F32).reshape(1, patches)
    bs[0:1, :] = bias_in_r[...].astype(F32).reshape(1, D)
    bs[1:2, :] = bias_out_r[...].astype(F32).reshape(1, D)
    toko_t[K:KA, :] = misc[...].astype(BF16)
    ri = lax.broadcasted_iota(jnp.int32, (ROWS, ROWS), 0)
    ci = lax.broadcasted_iota(jnp.int32, (ROWS, ROWS), 1)
    eye_rows = ((ri == ci) & (ri < patches)).astype(BF16)
    toki[:, 0:K] = dot_nt(eye_rows, toki_t[:, 0:ROWS]).astype(BF16)
    toko[:, 0:KA] = dot_nt(eye_rows, toko_t[:, 0:ROWS]).astype(BF16)

    chunks = []
    at = 0
    for n in z_sizes(count):
        chunks.append((at, n))
        at += n
    steps = len(chunks)
    seam = [c for c in range(steps) if chunks[c][0] == count * last][0]
    d_rows, o_rows = 0, count * last + 32

    def zrows(c):
        return pl.ds(chunks[c][0], chunks[c][1])

    def chunks_of(start, i):
        return [c for c in range(steps) if start + i * last <= chunks[c][0] < start + (i + 1) * last]

    def up_copy(c, r):
        return rcopy(zpart.at[r], zrx.at[r], z_sent.at[0], z_sem.at[0, c], (me, end_peer))

    def mid_copy(c, r):
        return rcopy(zpair.at[r], zrxp.at[r], z_sent.at[1], z_sem.at[1, c], (me, mid_peer))

    def down_copy(c, r):
        return rcopy(ztot.at[r], ztot.at[r], z_sent.at[2], z_sem.at[2, c], (me, mid_end))

    def start_up(some):
        @pl.when(end)
        def _():
            for c in some:
                up_copy(c, zrows(c)).start()

    def zpair_step(c):
        r = zrows(c)
        up_copy(c, r).wait_recv()
        zpair[r, :] = (zpart[r, :].astype(F32) + zrx[r, :].astype(F32)).astype(BF16)
        mid_copy(c, r).start()

    def ztot_step(c):
        r = zrows(c)
        mid_copy(c, r).wait_recv()
        ztot[r, :] = (zpair[r, :].astype(F32) + zrxp[r, :].astype(F32)).astype(BF16)
        down_copy(c, r).start()

    slots = [[c] for c in range(seam)] + [[seam, seam + 1]] + [[c] for c in range(seam + 2, steps)]
    ticks = iter(range(len(slots) + 2))

    def tick(until=None):
        for n in ticks:
            ups = slots[n] if n < len(slots) else []
            downs = slots[n - 2] if n >= 2 else []

            @pl.when(mid)
            def _():
                for c in ups:
                    zpair_step(c)
                for c in downs:
                    ztot_step(c)

            if until is None or until in downs:
                return

    def zfin(some):
        @pl.when(end)
        def _():
            for c in some:
                down_copy(c, zrows(c)).wait_recv()

    def pack_tails():
        rows = [tails[i, 0:tail, :] for i in range(count)]
        rows.append(jnp.zeros((16 - count * tail, D), F32))
        return jnp.concatenate(rows, axis=0).astype(BF16)

    def forward(i):
        base = i * ROWS
        r = pl.ds(base, ROWS)
        for b in range(nblk):
            rb = pl.ds(base + 16 * b, 16)
            v = xh1[rb, :] * gs[0:1, :] + gs[2:3, :]
            if 16 * (b + 1) > patches:
                row = lax.broadcasted_iota(jnp.int32, (16, D), 0) + 16 * b
                v = jnp.where(row < patches, v, jnp.where(row == patches, 1.0, 0.0))
            normed[rb, :] = v.astype(BF16)
        th[i, K:KA, :] = (lax.broadcasted_iota(jnp.int32, (16, D), 0) == 0).astype(F32).astype(BF16)
        for c in range(0, D, 256):
            tmp[0:K, :] = dot_nn(toki_t[:, 0:ROWS], normed[r, c : c + 256])
            for b in range(0, K, 16):
                value, slope = gelu_pair(tmp[b : b + 16, :])
                th[i, b : b + 16, c : c + 256] = value.astype(BF16)
                tgp[i, b : b + 16, c : c + 256] = slope
            xf[r, c : c + 256] += dot_nn(toko[:, 0:KA], th[i, :, c : c + 256])
        for b in range(nblk):
            rb = pl.ds(base + 16 * b, 16)
            v = xf[rb, :]
            center = v - jnp.mean(v, axis=-1, keepdims=True)
            inv = lax.rsqrt(jnp.mean(center * center, axis=-1, keepdims=True) + 1e-06)
            xhat = center * inv
            xh2[rb, :] = xhat
            rs2[rb, :] = jnp.broadcast_to(inv, (16, 128))
            chan[rb, :] = (xhat * gs[1:2, :] + gs[3:4, :]).astype(BF16)

        if i == 0:
            cq[me] = chan[0:ROWS, :]
            cqs.start()

        for c in range(0, D, 256):
            tmp[0:ROWS, :] = dot_nn(chan[r, :], w_in[:, c : c + 256])
            a = jnp.zeros((8, 256), F32)
            for b in range(nblk):
                rb = pl.ds(base + 16 * b, 16)
                value, slope = gelu_pair(tmp[16 * b : 16 * b + 16, :] + bs[0:1, c : c + 256])
                hid[rb, c : c + 256] = value.astype(BF16)
                low = (slope * dhid[rb, c : c + 256]).astype(BF16)
                dpre[rb, c : c + 256] = low
                a = a + fold(low.astype(F32))
            acc[5, :, c : c + 256] += a
        for c in range(0, D, 256):
            part = dot_nt(dpre[r, :], w_in[c : c + 256, :])
            zpart[pl.ds(i * last, last), c : c + 256] = part[0:last].astype(BF16)
            tails[i, :, c : c + 256] = part[last : last + 8]
        start_up(chunks_of(d_rows, i))


    for i in range(count):
        forward(i)
    tick()

    zpart[zrows(seam), :] = pack_tails()
    start_up([seam])

    def partial_out(i):
        r = pl.ds(i * ROWS, ROWS)
        ro = pl.ds(o_rows + i * last, last)
        for c in range(0, D, 256):
            part = dot_nn(hid[r, :], w_out[:, c : c + 256])
            zpart[ro, c : c + 256] = part[0:last].astype(BF16)
            tails[i, :, c : c + 256] = part[last : last + 8]

    for i in range(count):
        partial_out(i)
    tick()
    zpart[zrows(seam + 1), :] = pack_tails()
    start_up(range(seam + 1, steps))

    def weight_grad(j):
        cols = pl.ds(j * 256, 256)
        gw[0, cols, :] = dot_tn(chan[:, cols], dpre[...])
        gw[1, cols, :] = dot_tn(dout[:, cols], hid[...])

    for j in range(D // 256):
        weight_grad(j)
    for c in range(nc):
        rows = pl.ds(pl.multiple_of((2 * c + 1 - core) * shard, 8), shard)
        for m in range(2):
            wsib_s[c, m] = gw[m, rows, :].astype(BF16)
    w_sib = rcopy(wsib_s, wsib_r, w_sem.at[0, 0], w_sem.at[1, 0], (sib, t))
    w_sib.start()
    tick()

    sqs[...] = jnp.zeros(sqs.shape, F32)

    def square(i):
        r = pl.ds(i * ROWS, ROWS)
        g1 = dot_nt(chan[r, :], chan[r, :]) * dot_nt(dpre[r, :], dpre[r, :])
        g2 = dot_nt(dout[r, :], dout[r, :]) * dot_nt(hid[r, :], hid[r, :])
        sqs[pl.ds(i, 1), 0:ROWS] = jnp.sum(g1 + g2, axis=0, keepdims=True)

    for i in range(count):
        square(i)
    tick()

    w_sib.wait_recv()

    def w_chip(n, k):
        return rcopy(wch_s.at[n], wch_r.at[n], w_sem.at[0, n + 1], w_sem.at[1, n + 1], (peer(k), t))

    def w_share(dest, m):
        rows = pl.ds(pl.multiple_of((2 * dest + core) * shard, 8), shard)
        return gw[m, rows, :] + wsib_r[dest, m].astype(F32)

    first, second = 1 + core, 2 - core

    infl[...] = jnp.zeros(infl.shape, F32)

    def query(j):
        k = j // 2
        if j == 0:
            slot, cin, din, hid_q, pre_q = me, chan, dout, hid, dpre
        else:
            slot = peer_sib(k) if j % 2 else peer(k)
            if j % 2:
                dqs.from_sib(k)
                cqs.from_sib(k)
            cin, din, hid_q, pre_q = cq.at[slot], dq.at[slot], hq, pq
            for c in range(0, D, 256):
                tmp[0:ROWS, :] = dot_nn(cin[...], w_in[:, c : c + 256])
                tmp[ROWS : 2 * ROWS, :] = dot_nt(din[...], w_out[c : c + 256, :])
                for b in range(0, ROWS, 16):
                    value, slope = gelu_pair(tmp[b : b + 16, :] + bs[0:1, c : c + 256])
                    hq[b : b + 16, c : c + 256] = value.astype(BF16)
                    pq[b : b + 16, c : c + 256] = (slope * tmp[ROWS + b : ROWS + b + 16, :]).astype(BF16)
        for q in range(count - QRY_DEV):
            r = slice((QRY_DEV + q) * ROWS, (QRY_DEV + q + 1) * ROWS)
            g1 = dot_nt(cin[0:ROWS, :], chan[r, :]) * dot_nt(pre_q[0:ROWS, :], dpre[r, :])
            g2 = dot_nt(din[0:ROWS, :], dout[r, :]) * dot_nt(hid_q[0:ROWS, :], hid[r, :])
            infl[q, pl.ds(slot, 1), 0:ROWS] = jnp.sum(g1 + g2, axis=0, keepdims=True)
        tick()

    dqs.relay(1)
    dqs.relay(2)
    query(0)
    query(1)
    tick()
    cqs.relay(1)
    cqs.relay(2)
    for n, dest in ((0, chip ^ 3), (1, chip ^ first)):
        for m in range(2):
            wch_s[n, m] = w_share(dest, m).astype(BF16)
        w_chip(n, first).start()
    for j in (2, 4, 3, 5):
        query(j)
    tick(until=seam)

    gtok[...] = jnp.zeros(gtok.shape, F32)

    def ing_copy(i):
        return pltpu.make_async_copy(ing_s.at[i], ing_o.at[i], out_sem.at[0, i])

    zfin([seam])
    rest = ztot[zrows(seam), :].astype(F32)
    for i in range(count):
        rests[i, 0:tail, :] = rest[tail * i : tail * (i + 1)]
        rests[i, tail:16, :] = jnp.zeros((16 - tail, D), F32)

    def backward(i):
        zfin(chunks_of(d_rows, i))
        base = i * ROWS
        r = pl.ds(base, ROWS)
        a1 = jnp.zeros((8, D), F32)
        a3 = jnp.zeros((8, D), F32)
        for b in range(nblk):
            rb = pl.ds(base + 16 * b, 16)
            if b < nblk - 1:
                e = ztot[pl.ds(i * last + 16 * b, 16), :].astype(F32)
            else:
                e = rests[i]
            xhat = xh2[rb, :]
            a1 = a1 + fold(e * xhat)
            a3 = a3 + fold(e)
            eg = e * gs[1:2, :]
            m1 = jnp.mean(eg, axis=-1, keepdims=True)
            m2 = jnp.mean(eg * xhat, axis=-1, keepdims=True)
            d = dout[rb, :].astype(F32) + rs2[rb, 0:1] * (eg - m1 - xhat * m2)
            dhid[rb, :] = d
            dmix[16 * b : 16 * b + 16, :] = d.astype(BF16)
        acc[1] += a1
        acc[3] += a3
        for c in range(0, D, 256):
            tmp[0:K, :] = dot_nn(toko_t[0:K, 0:ROWS], dmix[:, c : c + 256])
            for b in range(0, K, 16):
                dtok[b : b + 16, c : c + 256] = (
                    tmp[b : b + 16, :] * tgp[i, b : b + 16, c : c + 256]
                ).astype(BF16)
        gtok[0, 0:K, 0:ROWS] += dot_nt(dtok[...], normed[r, :])
        gtok[1, :, 0:ROWS] += dot_nt(th[i], dmix[...])
        for c in range(0, D, 256):
            dnorm[:, c : c + 256] = dot_nn(toki[:, 0:K], dtok[:, c : c + 256])
        a0 = jnp.zeros((8, D), F32)
        a2 = jnp.zeros((8, D), F32)
        for b in range(nblk):
            rb = pl.ds(base + 16 * b, 16)
            e = dnorm[16 * b : 16 * b + 16, :]
            xhat = xh1[rb, :]
            a0 = a0 + fold(e * xhat)
            a2 = a2 + fold(e)
            eg = e * gs[0:1, :]
            m1 = jnp.mean(eg, axis=-1, keepdims=True)
            m2 = jnp.mean(eg * xhat, axis=-1, keepdims=True)
            d = (dhid[rb, :] + rs1[rb, 0:1] * (eg - m1 - xhat * m2)).astype(BF16)
            n = min(16, patches - 16 * b)
            ing_s[i, 16 * b : 16 * b + n, :] = d[0:n]
        acc[0] += a0
        acc[2] += a2
        ing_copy(i).start()
        tick()

    for i in range(count):
        backward(i)
        if i == 0:
            dqs.relay(3)
            cqs.relay(3)
        if i == 1:
            w_chip(0, first).wait_recv()
            for m in range(2):
                wch_s[2, m] = (w_share(chip ^ second, m) + wch_r[0, m].astype(F32)).astype(BF16)
            w_chip(2, second).start()

    for c in range(nc):
        rows = pl.ds(pl.multiple_of((2 * c + 1 - core) * kb, 8), kb)
        for m in range(2):
            tsib_s[c, m] = gtok[m, rows, :]
    t_sib = rcopy(tsib_s, tsib_r, t_sem.at[0, 0], t_sem.at[1, 0], (sib, t))
    t_sib.start()
    vec[...] = jnp.zeros(vec.shape, F32)
    for q in range(6):
        vec[q : q + 1, :] = jnp.sum(acc[q], axis=0, keepdims=True)
    vec[6:7, 0:256] = gtok[1, K : K + 1, :]
    v_sib = rcopy(vec, vsib_r, v_sem.at[0, 0], v_sem.at[1, 0], (sib, t))
    v_sib.start()
    tick()
    v_sib.wait_recv()

    def v_chip(k):
        return rcopy(
            vch.at[chip], vch.at[chip], v_sem.at[0, k], v_sem.at[1, k], (peer(k), t)
        )

    vch[chip] = vec[...] + vsib_r[...]
    for k in range(1, nc):
        v_chip(k).start()
    t_sib.wait_recv()

    def t_chip(k):
        return rcopy(
            tch_s.at[k - 1], tch_r.at[k - 1], t_sem.at[0, k], t_sem.at[1, k], (peer(k), t)
        )

    for k in range(1, nc):
        dest = chip ^ k
        rows = pl.ds(pl.multiple_of((2 * dest + core) * kb, 8), kb)
        for m in range(2):
            tch_s[k - 1, m] = gtok[m, rows, :] + tsib_r[dest, m]
        t_chip(k).start()


    def act_copy(i):
        return pltpu.make_async_copy(act_s.at[i], act_o.at[i], out_sem.at[1, i])

    def act(i):
        tick(chunks_of(o_rows, i)[-1])
        zfin([seam + 1] * (i == 0) + chunks_of(o_rows, i))
        start = o_rows + i * last
        for b in range(0, last, 16):
            ro = slice(start + b, start + b + 16)
            a = xf[i * ROWS + b : i * ROWS + b + 16, :] + ztot[ro, :].astype(F32) + bs[1:2, :]
            act_s[i, b : b + 16, :] = a.astype(BF16)
        a = ztot[zrows(seam + 1), :].astype(F32)[tail * i : tail * (i + 1)] + bs[1:2, :]
        a = a + xf[i * ROWS + last : i * ROWS + patches, :]
        act_s[i, last:patches, :] = a.astype(BF16)
        act_copy(i).start()

    act(0)
    query(6)
    query(7)

    def as_row(values):
        totals = jnp.sum(values, axis=1, keepdims=True)
        at = lax.broadcasted_iota(jnp.int32, (values.shape[0], 128), 0)
        lane = lax.broadcasted_iota(jnp.int32, (values.shape[0], 128), 1)
        return jnp.sum(jnp.where(at == lane, totals, 0.0), axis=0, keepdims=True)

    zsm[t] = jnp.zeros((8, 128), F32)
    zsm[t, 0:1, :] = as_row(sqs[...]) / (2.0 * D * FF)
    for q in range(count - QRY_DEV):
        zsm[t, 1 + q : 2 + q, :] = as_row(infl[q]) * (2.0 * D * FF) ** (-0.5)

    def sm_copy(k):
        return rcopy(
            zsm.at[t], zsm.at[t], s_sem.at[0, k - 1], s_sem.at[1, k - 1], (me, (t + k) % 4)
        )

    for k in (1, 2, 3):
        sm_copy(k).start()

    for m, out in enumerate((gwi_o, gwo_o)):
        out[...] = w_share(chip, m)
    for n in (1, 2):
        w_chip(n, first).wait_recv()
        for m, out in enumerate((gwi_o, gwo_o)):
            out[...] += wch_r[n, m].astype(F32)
    act(1)
    for k in (1, 2, 3):
        sm_copy(k).wait_recv()
    sm_o[...] = (zsm[0] + zsm[1]) + (zsm[2] + zsm[3])
    rows = pl.ds(pl.multiple_of(me * kb, 8), kb)
    for m, out in enumerate((gti_o, gto_o)):
        out[...] = gtok[m, rows, :] + tsib_r[chip, m]
    for k in range(1, nc):
        t_chip(k).wait_recv()
        for m, out in enumerate((gti_o, gto_o)):
            out[...] += tch_r[k - 1, m]
    for k in range(1, nc):
        v_chip(k).wait_recv()
    total = vch[0]
    for c in range(1, nc):
        total = total + vch[c]
    tbo_o[...] = total[:, 0:256]
    vec_o[...] = pltpu.roll(total, (D - me * shard) % D, 1)[:, 0:128]


    act(count - 1)

    params.drain()
    dqs.drain()
    cqs.drain()

    @pl.when(end)
    def _():
        rcopy(zpart, zrx, z_sent.at[0], z_sem.at[0, 0], (me, end_peer)).wait_send()

    @pl.when(mid)
    def _():
        rcopy(zpair, zrxp, z_sent.at[1], z_sem.at[1, 0], (me, mid_peer)).wait_send()
        rcopy(ztot, ztot, z_sent.at[2], z_sem.at[2, 0], (me, mid_end)).wait_send()

    w_sib.wait_send()
    t_sib.wait_send()
    v_sib.wait_send()
    for k in range(1, nc):
        w_chip(k - 1, first).wait_send()
        t_chip(k).wait_send()
        v_chip(k).wait_send()
    for k in (1, 2, 3):
        sm_copy(k).wait_send()
    for i in range(count):
        ing_copy(i).wait()
        act_copy(i).wait()


def finish(shard, ks, patches, count, queries, act, ing, gwi, gwo, gti_h, gto_h, vec_h, tbo_h, sm_h, *refs):
    big, small, refs = refs[:4], refs[4:14], refs[14:]
    held, got, made, sem = refs[:4], refs[4:9], refs[9:19], refs[19]
    pieces = [(n, i) for n in (0, 1) for i in range(count)] + [(2, None), (3, None)]

    def part(ref, i):
        return ref if i is None else ref.at[i]

    loads = [
        pltpu.make_async_copy(a, b, sem.at[0, n])
        for n, (a, b) in enumerate(zip((gti_h, gto_h, vec_h, tbo_h, sm_h), got))
    ]
    moves = []
    for n, i in pieces:
        kept, at = part(held[n], i), len(moves)
        moves.append(
            (
                pltpu.make_async_copy(part((act, ing, gwi, gwo)[n], i), kept, sem.at[1, at]),
                pltpu.make_async_copy(kept, part(big[n], i), sem.at[2, at]),
            )
        )
    for c in loads:
        c.start()
    for load, _ in moves:
        load.start()
    for c in loads:
        c.wait()
    gti, gto, vec, tbo, sm = got
    gains, shifts, gti_o, gto_o, gtb_o, tbo_o, gbi_o, gbo_o, sq_o, infl_o = made
    gains[...] = vec[0:2, 0:shard]
    shifts[...] = vec[2:4, 0:shard]
    gbo_o[...] = vec[4:5, 0:shard]
    gbi_o[...] = vec[5:6, 0:shard]
    gti_o[...] = gti[0:ks, 0:patches]
    gto_o[...] = gto[0:ks, 0:patches]
    tbo_o[...] = tbo[6:7, 0:patches]
    column = gti[0:ks, patches : patches + 1]
    eye = lax.broadcasted_iota(jnp.int32, (ks, ks), 0) == lax.broadcasted_iota(jnp.int32, (ks, ks), 1)
    gtb_o[...] = jnp.sum(jnp.where(eye, column, 0.0), axis=0, keepdims=True)
    sq_o[...] = sm[0:1, 0:count]
    for t in range(infl_o.shape[0]):
        infl_o[t : t + 1, :] = sm[1 + t : 2 + t, 0:queries]
    stores = [pltpu.make_async_copy(a, b, sem.at[3, n]) for n, (a, b) in enumerate(zip(made, small))]
    for c in stores:
        c.start()
    for load, store in moves:
        load.wait()
        store.start()
    for c in stores + [store for _, store in moves]:
        c.wait()


def fused(
    n_dp,
    images,
    cotangent,
    norm_gains,
    norm_shifts,
    tok_in,
    tok_out_t,
    tok_bias_in,
    tok_bias_out,
    w_in,
    bias_in,
    w_out,
    bias_out,
):
    count, patches, width = images.shape
    nc = n_dp // 2
    ks = tok_in.shape[1]
    toks = ks * n_dp
    kb = -(-ks // 16) * 16
    K = n_dp * kb
    KA = K + 16
    KL = -(-KA // 128) * 128
    R = count * ROWS
    zrows, steps = sum(z_sizes(count)), len(z_sizes(count))
    shard = width // n_dp
    hidden = w_in.shape[1]
    anyspace = pl.BlockSpec(memory_space=pl.ANY)
    vm = pl.BlockSpec(memory_space=pltpu.VMEM)
    V = pltpu.VMEM
    dma = lambda *s: pltpu.SemaphoreType.DMA(s)
    scratch = dict(
        gains_r=V(norm_gains.shape, BF16),
        shifts_r=V(norm_shifts.shape, BF16),
        tok_in_r=V((ks, patches), BF16),
        tok_out_r=V((ks, patches), BF16),
        tok_bias_r=V(tok_bias_in.shape, BF16),
        tok_bias_out_r=V(tok_bias_out.shape, BF16),
        bias_in_r=V(bias_in.shape, BF16),
        bias_out_r=V(bias_out.shape, BF16),
        x_raw=V((count, patches, D), BF16),
        d_raw=V((count, patches, D), BF16),
        w_in=V((D, hidden), BF16),
        w_out=V((hidden, D), BF16),
        act_s=V((count, patches, D), BF16),
        ing_s=V((count, patches, D), BF16),
        pb=V((n_dp, 2 * kb + 16, 256), BF16),
        aug=V((ROWS, 128), F32),
        misc=V((16, 256), F32),
        toki_t=V((K, 256), BF16),
        toko_t=V((KA, 256), BF16),
        toki=V((ROWS, KL), BF16),
        toko=V((ROWS, KL), BF16),
        gs=V((16, D), F32),
        bs=V((8, D), F32),
        dout=V((R, D), BF16),
        dhid=V((R, hidden), F32),
        xf=V((R, D), F32),
        xh1=V((R, D), F32),
        rs1=V((R, 128), F32),
        xh2=V((R, D), F32),
        rs2=V((R, 128), F32),
        normed=V((R, D), BF16),
        th=V((count, KA, D), BF16),
        tgp=V((count, K, D), F32),
        chan=V((R, D), BF16),
        hid=V((R, hidden), BF16),
        dpre=V((R, hidden), BF16),
        tmp=V((max(K, 2 * ROWS), 256), F32),
        dq=V((n_dp, ROWS, D), BF16),
        cq=V((n_dp, ROWS, D), BF16),
        hq=V((ROWS, hidden), BF16),
        pq=V((ROWS, hidden), BF16),
        infl=V((count - QRY_DEV, n_dp, 256), F32),
        sqs=V((8, 256), F32),
        dmix=V((ROWS, D), BF16),
        dtok=V((K, D), BF16),
        dnorm=V((ROWS, D), F32),
        tails=V((count, 8, D), F32),
        rests=V((count, 16, D), F32),
        zpart=V((zrows, D), BF16),
        zrx=V((zrows, D), BF16),
        zpair=V((zrows, D), BF16),
        zrxp=V((zrows, D), BF16),
        ztot=V((zrows, D), BF16),
        gw=V((2, D, hidden), F32),
        wsib_s=V((nc, 2, shard, hidden), BF16),
        wsib_r=V((nc, 2, shard, hidden), BF16),
        wch_s=V((nc - 1, 2, shard, hidden), BF16),
        wch_r=V((nc - 1, 2, shard, hidden), BF16),
        gtok=V((2, KA, 256), F32),
        tsib_s=V((nc, 2, kb, 256), F32),
        tsib_r=V((nc, 2, kb, 256), F32),
        tch_s=V((nc - 1, 2, kb, 256), F32),
        tch_r=V((nc - 1, 2, kb, 256), F32),
        acc=V((6, 8, D), F32),
        vec=V((8, D), F32),
        vsib_r=V((8, D), F32),
        vch=V((nc, 8, D), F32),
        zsm=V((4, 8, 128), F32),
        in_sem=dma(12),
        out_sem=dma(2, count),
        pb_sem=dma(8),
        dq_sem=dma(8),
        cq_sem=dma(8),
        z_sem=dma(3, steps),
        z_sent=dma(3),
        w_sem=dma(2, nc),
        t_sem=dma(2, nc),
        v_sem=dma(2, nc),
        s_sem=dma(2, 3),
    )
    outs = [
        (images.shape, BF16, anyspace),
        (images.shape, BF16, anyspace),
        ((shard, hidden), F32, vm),
        ((shard, hidden), F32, vm),
        ((kb, 256), F32, vm),
        ((kb, 256), F32, vm),
        ((8, 128), F32, vm),
        ((8, 256), F32, vm),
        ((8, 128), F32, vm),
    ]
    names = list(scratch)
    n_in, n_out = 12, len(outs)

    def body(*refs):
        mega(n_dp, count, patches, toks, *refs[: n_in + n_out], **dict(zip(names, refs[n_in + n_out :])))

    act, ing, gwi, gwo, gti, gto, vec, tbo, sm = pl.pallas_call(
        body,
        out_shape=[jax.ShapeDtypeStruct(s, d) for s, d, _ in outs],
        in_specs=[anyspace] * 12,
        out_specs=[o[2] for o in outs],
        scratch_shapes=list(scratch.values()),
        compiler_params=pltpu.CompilerParams(
            collective_id=0, has_side_effects=True, vmem_limit_bytes=60 * 2**20
        ),
        name="mixer",
    )(
        images,
        cotangent,
        w_in,
        w_out,
        norm_gains,
        norm_shifts,
        tok_in.T,
        tok_out_t.T,
        tok_bias_in,
        tok_bias_out,
        bias_in,
        bias_out,
    )
    queries, trains = n_dp * QRY_DEV, count - QRY_DEV
    shapes = [
        (images.shape, BF16),
        (images.shape, BF16),
        ((shard, hidden), F32),
        ((shard, hidden), F32),
        ((2, shard), F32),
        ((2, shard), F32),
        ((ks, patches), F32),
        ((ks, patches), F32),
        ((1, ks), F32),
        ((1, patches), F32),
        ((1, shard), F32),
        ((1, shard), F32),
        ((1, count), F32),
        ((trains, queries), F32),
    ]
    smalls = [(o.shape, F32) for o in (gti, gto, vec, tbo, sm)]
    out = pl.pallas_call(
        functools.partial(finish, shard, ks, patches, count, queries),
        out_shape=[jax.ShapeDtypeStruct(s, d) for s, d in shapes],
        in_specs=[anyspace] * 9,
        out_specs=[anyspace] * 14,
        scratch_shapes=[V(s, d) for s, d in shapes[:4] + smalls + shapes[4:]] + [dma(4, 10)],
        name="finish",
    )(act, ing, gwi, gwo, gti, gto, vec, tbo, sm)
    act, ing, gwi, gwo, gains, shifts, gti, gto, gtb, tbo, gbi, gbo, squares, influence = out
    return (
        act,
        ing,
        gains,
        shifts,
        gti.T,
        gto.T,
        gtb,
        tbo.reshape(patches),
        gwi,
        gbi.reshape(shard),
        gwo.T,
        gbo.reshape(shard),
        squares.reshape(count),
        influence.T,
    )


def layer_norm(values, gain, shift):
    center = values - jnp.mean(values, axis=-1, keepdims=True)
    spread = jnp.mean(center * center, axis=-1, keepdims=True)
    return center * lax.rsqrt(spread + 1e-06) * gain + shift


def smooth(values):
    return jax.nn.gelu(values, approximate=True)


def contract(left, right, left_dim, right_dim):
    return lax.dot_general(
        left, right, (((left_dim,), (right_dim,)), ((), ())), preferred_element_type=jnp.float32
    )


def per_device(
    images,
    cotangent,
    norm_gains,
    norm_shifts,
    tok_in,
    tok_out_t,
    tok_bias_in,
    tok_bias_out,
    w_in,
    bias_in,
    w_out,
    bias_out,
):
    gains, shifts, tok_first, tok_second, tok_bias = (
        lax.all_gather(norm_gains, "dp", axis=1, tiled=True),
        lax.all_gather(norm_shifts, "dp", axis=1, tiled=True),
        lax.all_gather(tok_in, "dp", axis=1, tiled=True),
        lax.all_gather(tok_out_t, "dp", axis=1, tiled=True),
        lax.all_gather(tok_bias_in, "dp", axis=1, tiled=True),
    )
    gains = gains.astype(jnp.float32)
    shifts = shifts.astype(jnp.float32)
    count, patches, width = images.shape
    rows = count * patches
    inputs = images.astype(jnp.float32)
    normed_one, first_back = jax.vjp(layer_norm, inputs, gains[0], shifts[0])
    normed_low = normed_one.astype(jnp.bfloat16)
    tok_pre = (
        jnp.einsum("sk,nsd->nkd", tok_first, normed_low, preferred_element_type=jnp.float32)
        + tok_bias[0].astype(jnp.float32)[None, :, None]
    )
    tok_hidden = smooth(tok_pre).astype(jnp.bfloat16)
    tok_mixed = (
        jnp.einsum("sk,nkd->nsd", tok_second, tok_hidden, preferred_element_type=jnp.float32)
        + tok_bias_out.astype(jnp.float32)[None, :, None]
    )
    resid = inputs + tok_mixed
    normed_two, second_back = jax.vjp(layer_norm, resid, gains[1], shifts[1])
    chan_in = normed_two.astype(jnp.bfloat16).reshape(rows, width)
    chan_pre = jnp.dot(chan_in, w_in, preferred_element_type=jnp.float32) + bias_in.astype(
        jnp.float32
    )
    hidden = smooth(chan_pre).astype(jnp.bfloat16)
    partial_out = jnp.dot(hidden, w_out, preferred_element_type=jnp.float32)
    mixed = lax.psum(partial_out, "tensor")
    activations = (
        resid + mixed.reshape(count, patches, width) + bias_out.astype(jnp.float32)
    ).astype(jnp.bfloat16)
    dout_rows = cotangent.reshape(rows, width)
    d_hidden = contract(dout_rows, w_out, 1, 1)
    smooth_value, smooth_back = jax.vjp(smooth, chan_pre)
    d_pre = smooth_back(d_hidden)[0].astype(jnp.bfloat16)
    d_chan_part = contract(d_pre, w_in, 1, 1)
    d_chan = lax.psum(d_chan_part, "tensor")
    d_resid_norm, d_gain_two, d_shift_two = second_back(d_chan.reshape(count, patches, width))
    d_resid = cotangent.astype(jnp.float32) + d_resid_norm
    d_mixed = d_resid.astype(jnp.bfloat16)
    d_tokhid = jnp.einsum("sk,nsd->nkd", tok_second, d_mixed, preferred_element_type=jnp.float32)
    tok_value, tok_back = jax.vjp(smooth, tok_pre)
    d_tokpre = tok_back(d_tokhid)[0].astype(jnp.bfloat16)
    grad_second = jnp.einsum("nsd,nkd->sk", d_mixed, tok_hidden, preferred_element_type=jnp.float32)
    grad_first = jnp.einsum("nsd,nkd->sk", normed_low, d_tokpre, preferred_element_type=jnp.float32)
    grad_tbias = jnp.sum(d_tokpre, axis=(0, 2), dtype=jnp.float32)[None, :]
    grad_tbias_out = jnp.sum(d_mixed, axis=(0, 2), dtype=jnp.float32)
    d_normed = jnp.einsum("sk,nkd->nsd", tok_first, d_tokpre, preferred_element_type=jnp.float32)
    d_input_norm, d_gain_one, d_shift_one = first_back(d_normed)
    input_grad = (d_resid + d_input_norm).astype(jnp.bfloat16)
    grad_win = contract(chan_in, d_pre, 0, 0)
    grad_wout_t = contract(dout_rows, hidden, 0, 0)
    grad_bin = jnp.sum(d_pre, axis=0, dtype=jnp.float32)
    grad_bout = jnp.sum(dout_rows, axis=0, dtype=jnp.float32)
    share_win, share_wout_t, share_bin, share_bout = (
        lax.psum_scatter(grad_win, "dp", scatter_dimension=0, tiled=True),
        lax.psum_scatter(grad_wout_t, "dp", scatter_dimension=0, tiled=True),
        lax.psum_scatter(grad_bin, "dp", scatter_dimension=0, tiled=True),
        lax.psum_scatter(grad_bout, "dp", scatter_dimension=0, tiled=True),
    )
    share_gains, share_shifts, share_first, share_second, share_tbias = (
        lax.psum_scatter(
            jnp.stack([d_gain_one, d_gain_two]), "dp", scatter_dimension=1, tiled=True
        ),
        lax.psum_scatter(
            jnp.stack([d_shift_one, d_shift_two]), "dp", scatter_dimension=1, tiled=True
        ),
        lax.psum_scatter(grad_first, "dp", scatter_dimension=1, tiled=True),
        lax.psum_scatter(grad_second, "dp", scatter_dimension=1, tiled=True),
        lax.psum_scatter(grad_tbias, "dp", scatter_dimension=1, tiled=True),
    )
    total_tbias_out = lax.psum(grad_tbias_out, "dp")
    chan_cube = chan_in.reshape(count, patches, width)
    pre_cube = d_pre.reshape(count, patches, -1)
    hidden_cube = hidden.reshape(count, patches, -1)
    def against(chan, pre, dout, low):
        grams = [
            jnp.einsum("sd,npd->nsp", a, b, preferred_element_type=jnp.float32)
            for a, b in ((chan, chan_cube), (pre, pre_cube), (dout, cotangent), (low, hidden_cube))
        ]
        return jnp.sum(grams[0] * grams[1] + grams[2] * grams[3], axis=(1, 2))

    own = lax.map(lambda a: against(*a), (chan_cube, pre_cube, cotangent, hidden_cube))
    squares = jnp.diagonal(own)
    queries = tuple(
        lax.all_gather(a[:QRY_DEV], "dp", axis=0, tiled=True)
        for a in (chan_cube, pre_cube, cotangent, hidden_cube)
    )
    influence = lax.map(lambda a: against(*a), queries)[:, QRY_DEV:]
    influence, squares = lax.psum((influence, squares), "tensor")
    sqnorms = squares / (2.0 * D * FF)
    influence = influence * (2.0 * D * FF) ** (-0.5)
    return (
        activations,
        input_grad,
        share_gains,
        share_shifts,
        share_first,
        share_second,
        share_tbias,
        total_tbias_out,
        share_win,
        share_bin,
        share_wout_t.T,
        share_bout,
        sqnorms,
        influence,
    )


def solution(mesh):
    placed = (
        P("dp", None, None),
        P("dp", None, None),
        P(None, "dp"),
        P(None, "dp"),
        P(None, "dp"),
        P(None, "dp"),
        P(None, "dp"),
        P(),
        P(None, "tensor"),
        P("tensor"),
        P("tensor", None),
        P(),
    )
    n_dp = mesh.shape["dp"]
    fits = n_dp == 8 and mesh.shape["tensor"] == 4
    device = functools.partial(fused, n_dp) if fits else per_device
    return jax.shard_map(
        device,
        mesh=mesh,
        in_specs=placed,
        out_specs=(
            P("dp", None, None),
            P("dp", None, None),
            P(None, "dp"),
            P(None, "dp"),
            P(None, "dp"),
            P(None, "dp"),
            P(None, "dp"),
            P(),
            P("dp", "tensor"),
            P(("tensor", "dp")),
            P("tensor", "dp"),
            P("dp"),
            P("dp"),
            P(None, "dp"),
        ),
        check_vma=False,
    )
```

```python
import functools

import jax
import jax.numpy as jnp
from jax import lax
from jax.experimental import pallas as pl
from jax.experimental.pallas import tpu as pltpu
from jax.sharding import PartitionSpec as P

D = 768
FF = 3072
QRY_DEV = 1
HIGH = lax.Precision.HIGHEST
MESH = pl.DeviceIdType.MESH
F32 = jnp.float32
BF16 = jnp.bfloat16

ROWS = 208
C1 = 0.7978845608028654
C2 = 0.044715


def dot_nn(a, b):
    return lax.dot_general(a, b, (((1,), (0,)), ((), ())), preferred_element_type=F32)


def dot_nt(a, b):
    return lax.dot_general(a, b, (((1,), (1,)), ((), ())), preferred_element_type=F32)


def dot_tn(a, b):
    return lax.dot_general(a, b, (((0,), (0,)), ((), ())), preferred_element_type=F32)


def gelu_pair(v):
    u = v * v
    th = jnp.tanh(v * (C1 + (C1 * C2) * u))
    hp = 0.5 + 0.5 * th
    value = v * hp
    slope = hp + (0.5 * v) * (1.0 - th * th) * (C1 + (3.0 * C1 * C2) * u)
    return value, slope


def z_sizes(count):
    full = [64] * (3 * count)
    return full + [16, 16] + full


def fold(v):
    out = v[0:8]
    for s in range(8, v.shape[0], 8):
        out = out + v[s : s + 8]
    return out


def mega(
    n_dp,
    count,
    patches,
    toks,
    images,
    cotangent,
    w_in_h,
    w_out_h,
    gains_h,
    shifts_h,
    tok_in_h,
    tok_out_h,
    tok_bias_h,
    tok_bias_out_h,
    bias_in_h,
    bias_out_h,
    act_o,
    ing_o,
    gwi_o,
    gwo_o,
    gti_o,
    gto_o,
    vec_o,
    tbo_o,
    sm_o,
    gwi_k,
    gwo_k,
    gti_k,
    gto_k,
    vec_k,
    tbo_k,
    sm_k,
    gains_r,
    shifts_r,
    tok_in_r,
    tok_out_r,
    tok_bias_r,
    tok_bias_out_r,
    bias_in_r,
    bias_out_r,
    x_raw,
    d_raw,
    w_in,
    w_out,
    act_s,
    ing_s,
    pb,
    aug,
    misc,
    toki_t,
    toko_t,
    toki,
    toko,
    gs,
    bs,
    dout,
    dhid,
    xf,
    xh1,
    rs1,
    xh2,
    rs2,
    normed,
    th,
    tgp,
    chan,
    hid,
    dpre,
    tmp,
    dq,
    cq,
    hq,
    pq,
    infl,
    sqs,
    dmix,
    dtok,
    dnorm,
    tails,
    rests,
    zpart,
    zrx,
    zpair,
    zrxp,
    ztot,
    gw,
    wsib_s,
    wsib_r,
    wch_s,
    wch_r,
    gtok,
    tsib_s,
    tsib_r,
    tch_s,
    tch_r,
    acc,
    vec,
    vsib_r,
    vch,
    zsm,
    in_sem,
    out_sem,
    small_sem,
    pb_sem,
    dq_sem,
    cq_sem,
    z_sem,
    z_sent,
    w_sem,
    t_sem,
    v_sem,
    s_sem,
):
    me = lax.axis_index("dp")
    t = lax.axis_index("tensor")
    core = me % 2
    chip = me // 2
    sib = chip * 2 + 1 - core
    nc = n_dp // 2
    mid = (t == 1) | (t == 2)
    end = (t == 0) | (t == 3)
    end_peer = jnp.where(t < 2, 1, 2)
    mid_end = jnp.where(t < 2, 0, 3)
    mid_peer = 3 - t
    shard = D // n_dp
    ks = toks // n_dp
    kb = -(-ks // 16) * 16
    K = n_dp * kb
    KA = K + 16
    R = count * ROWS
    nblk = ROWS // 16
    last = ROWS - 16
    tail = patches - last

    def peer(k):
        return (chip ^ k) * 2 + core

    def peer_sib(k):
        return (chip ^ k) * 2 + 1 - core

    def rcopy(a, b, ss, rs, dev):
        return pltpu.make_async_remote_copy(
            src_ref=a, dst_ref=b, send_sem=ss, recv_sem=rs, device_id=dev, device_id_type=MESH
        )

    class Gather:
        def __init__(self, buf, sem):
            self.buf, self.sem = buf, sem

        def chip_copy(self, block, k, n):
            b = self.buf.at[block]
            return rcopy(b, b, self.sem.at[0], self.sem.at[1 + n], (peer(k), t))

        def sib_copy(self, k):
            b = self.buf.at[peer(k)]
            return rcopy(b, b, self.sem.at[0], self.sem.at[4 + k], (sib, t))

        def start(self, across=False):
            for k in (1, 2, 3) if across else (1, 2):
                self.chip_copy(me, k, k - 1).start()
            self.sib_copy(0).start()

        def relay(self, k, across=False):
            self.chip_copy(peer(k), k, k - 1).wait_recv()
            if k < 3 and not across:

                @pl.when(core == k - 1)
                def _():
                    self.chip_copy(peer(k), 3 - k, 2).start()

            self.sib_copy(k).start()

        def from_sib(self, k):
            b = self.buf.at[peer_sib(k)]
            rcopy(b, b, self.sem.at[0], self.sem.at[4 + k], (sib, t)).wait_recv()

        def drain(self):
            b = self.buf.at[pl.ds(0, 7)]
            rcopy(b, b, self.sem.at[0], self.sem.at[1], (sib, t)).wait_send()

    params, dqs, cqs = Gather(pb, pb_sem), Gather(dq, dq_sem), Gather(cq, cq_sem)

    barrier = pltpu.get_barrier_semaphore()
    others = [(sib, t)] + [(peer(k), t) for k in range(1, nc)] + [(me, (t + k) % 4) for k in (1, 2, 3)]
    for dev in others:
        pl.semaphore_signal(barrier, inc=1, device_id=dev, device_id_type=MESH)

    pairs = [
        (gains_h, gains_r),
        (shifts_h, shifts_r),
        (tok_in_h, tok_in_r),
        (tok_out_h, tok_out_r),
        (tok_bias_h, tok_bias_r),
        (cotangent, d_raw),
        (w_out_h, w_out),
        (images, x_raw),
        (w_in_h, w_in),
        (tok_bias_out_h, tok_bias_out_r),
        (bias_in_h, bias_in_r),
        (bias_out_h, bias_out_r),
    ]
    loads = [pltpu.make_async_copy(a, b, in_sem.at[n]) for n, (a, b) in enumerate(pairs)]
    for c in loads:
        c.start()

    pb[me] = jnp.zeros(pb.shape[1:], BF16)
    eye = (
        lax.broadcasted_iota(jnp.int32, (kb, 128), 0) == lax.broadcasted_iota(jnp.int32, (kb, 128), 1)
    ).astype(BF16)
    aug[...] = jnp.zeros(aug.shape, F32)
    misc[...] = jnp.zeros(misc.shape, F32)
    for c in loads[:5]:
        c.wait()
    aug[patches : patches + 1, 0:ks] = tok_bias_r[...].astype(F32)
    pb[me, 0:kb, 0:ROWS] = dot_nt(eye, aug[...].astype(BF16)).astype(BF16)
    pb[me, 0:ks, 0:patches] = tok_in_r[...]
    pb[me, kb : kb + ks, 0:patches] = tok_out_r[...]
    misc[0:2, 0:shard] = gains_r[...].astype(F32)
    misc[2:4, 0:shard] = shifts_r[...].astype(F32)
    pb[me, 2 * kb : 2 * kb + 16, :] = misc[...].astype(BF16)

    pl.semaphore_wait(barrier, len(others))
    params.start(across=True)

    loads[5].wait()
    misc[...] = jnp.zeros(misc.shape, F32)
    acc[...] = jnp.zeros(acc.shape, F32)

    def pad_dout(i):
        base = i * ROWS
        dout[pl.ds(base, last), :] = d_raw[i, 0:last, :]
        for c in range(0, D, 256):
            misc[0:tail, :] = d_raw[i, last:patches, c : c + 256].astype(F32)
            dout[pl.ds(base + last, 16), c : c + 256] = misc[...].astype(BF16)
        a = jnp.zeros((8, D), F32)
        for b in range(nblk):
            a = a + fold(dout[pl.ds(base + 16 * b, 16), :].astype(F32))
        acc[4] += a

    for i in range(count):
        pad_dout(i)
    dq[me] = dout[0:ROWS, :]

    loads[6].wait()

    def hidden_grad(i):
        r = pl.ds(i * ROWS, ROWS)
        for c in range(0, D, 256):
            dhid[r, c : c + 256] = dot_nt(dout[r, :], w_out[c : c + 256, :])

    for i in range(count):
        hidden_grad(i)

    loads[7].wait()

    def first_norm(i):
        base = i * ROWS
        xf[pl.ds(base + last, 16), :] = jnp.zeros((16, D), F32)
        xf[pl.ds(base, last), :] = x_raw[i, 0:last, :].astype(F32)
        xf[pl.ds(base + last, tail), :] = x_raw[i, last:patches, :].astype(F32)
        for b in range(nblk):
            r = pl.ds(base + 16 * b, 16)
            v = xf[r, :]
            center = v - jnp.mean(v, axis=-1, keepdims=True)
            inv = lax.rsqrt(jnp.mean(center * center, axis=-1, keepdims=True) + 1e-06)
            xh1[r, :] = center * inv
            rs1[r, :] = jnp.broadcast_to(inv, (16, 128))

    for i in range(count):
        first_norm(i)

    for k in (1, 2, 3):
        params.relay(k, across=True)
    for k in range(nc):
        params.from_sib(k)
    dqs.start()
    for c in loads[8:]:
        c.wait()
    full = jnp.zeros((16, D), F32)
    for d in range(n_dp):
        toki_t[d * kb : (d + 1) * kb, :] = pb[d, 0:kb, :]
        toko_t[d * kb : (d + 1) * kb, :] = pb[d, kb : 2 * kb, :]
        part = pb[d, 2 * kb : 2 * kb + 16, 0:128].astype(F32)
        part = jnp.concatenate([part, jnp.zeros((16, D - 128), F32)], axis=1)
        full = full + (pltpu.roll(part, d * shard, 1) if d else part)
    gs[...] = full
    misc[...] = jnp.zeros(misc.shape, F32)
    misc[0:1, 0:patches] = tok_bias_out_r[...].astype(F32).reshape(1, patches)
    bs[0:1, :] = bias_in_r[...].astype(F32).reshape(1, D)
    bs[1:2, :] = bias_out_r[...].astype(F32).reshape(1, D)
    toko_t[K:KA, :] = misc[...].astype(BF16)
    ri = lax.broadcasted_iota(jnp.int32, (ROWS, ROWS), 0)
    ci = lax.broadcasted_iota(jnp.int32, (ROWS, ROWS), 1)
    eye_rows = ((ri == ci) & (ri < patches)).astype(BF16)
    toki[:, 0:K] = dot_nt(eye_rows, toki_t[:, 0:ROWS]).astype(BF16)
    toko[:, 0:KA] = dot_nt(eye_rows, toko_t[:, 0:ROWS]).astype(BF16)

    chunks = []
    at = 0
    for n in z_sizes(count):
        chunks.append((at, n))
        at += n
    steps = len(chunks)
    seam = [c for c in range(steps) if chunks[c][0] == count * last][0]
    d_rows, o_rows = 0, count * last + 32

    def zrows(c):
        return pl.ds(chunks[c][0], chunks[c][1])

    def chunks_of(start, i):
        return [c for c in range(steps) if start + i * last <= chunks[c][0] < start + (i + 1) * last]

    def up_copy(c, r):
        return rcopy(zpart.at[r], zrx.at[r], z_sent.at[0], z_sem.at[0, c], (me, end_peer))

    def mid_copy(c, r):
        return rcopy(zpair.at[r], zrxp.at[r], z_sent.at[1], z_sem.at[1, c], (me, mid_peer))

    def down_copy(c, r):
        return rcopy(ztot.at[r], ztot.at[r], z_sent.at[2], z_sem.at[2, c], (me, mid_end))

    def start_up(some):
        @pl.when(end)
        def _():
            for c in some:
                up_copy(c, zrows(c)).start()

    def zpair_step(c):
        r = zrows(c)
        up_copy(c, r).wait_recv()
        zpair[r, :] = (zpart[r, :].astype(F32) + zrx[r, :].astype(F32)).astype(BF16)
        mid_copy(c, r).start()

    def ztot_step(c):
        r = zrows(c)
        mid_copy(c, r).wait_recv()
        ztot[r, :] = (zpair[r, :].astype(F32) + zrxp[r, :].astype(F32)).astype(BF16)
        down_copy(c, r).start()

    slots = [[c] for c in range(seam)] + [[seam, seam + 1]] + [[c] for c in range(seam + 2, steps)]
    ticks = iter(range(len(slots) + 2))
    totals = set()

    def tick(until=None):
        if until in totals:
            return
        for n in ticks:
            ups = slots[n] if n < len(slots) else []
            downs = slots[n - 2] if n >= 2 else []
            totals.update(downs)

            @pl.when(mid)
            def _():
                for c in ups:
                    zpair_step(c)
                for c in downs:
                    ztot_step(c)

            if until is None or until in downs:
                return

    def zfin(some):
        @pl.when(end)
        def _():
            for c in some:
                down_copy(c, zrows(c)).wait_recv()

    def pack_tails():
        rows = [tails[i, 0:tail, :] for i in range(count)]
        rows.append(jnp.zeros((16 - count * tail, D), F32))
        return jnp.concatenate(rows, axis=0).astype(BF16)

    def forward(i):
        base = i * ROWS
        r = pl.ds(base, ROWS)
        for b in range(nblk):
            rb = pl.ds(base + 16 * b, 16)
            v = xh1[rb, :] * gs[0:1, :] + gs[2:3, :]
            if 16 * (b + 1) > patches:
                row = lax.broadcasted_iota(jnp.int32, (16, D), 0) + 16 * b
                v = jnp.where(row < patches, v, jnp.where(row == patches, 1.0, 0.0))
            normed[rb, :] = v.astype(BF16)
        th[i, K:KA, :] = (lax.broadcasted_iota(jnp.int32, (16, D), 0) == 0).astype(F32).astype(BF16)
        for c in range(0, D, 256):
            tmp[0:K, :] = dot_nn(toki_t[:, 0:ROWS], normed[r, c : c + 256])
            for b in range(0, K, 16):
                value, slope = gelu_pair(tmp[b : b + 16, :])
                th[i, b : b + 16, c : c + 256] = value.astype(BF16)
                tgp[i, b : b + 16, c : c + 256] = slope
            xf[r, c : c + 256] += dot_nn(toko[:, 0:KA], th[i, :, c : c + 256])
        for b in range(nblk):
            rb = pl.ds(base + 16 * b, 16)
            v = xf[rb, :]
            center = v - jnp.mean(v, axis=-1, keepdims=True)
            inv = lax.rsqrt(jnp.mean(center * center, axis=-1, keepdims=True) + 1e-06)
            xhat = center * inv
            xh2[rb, :] = xhat
            rs2[rb, :] = jnp.broadcast_to(inv, (16, 128))
            chan[rb, :] = (xhat * gs[1:2, :] + gs[3:4, :]).astype(BF16)

        if i == 0:
            cq[me] = chan[0:ROWS, :]
            cqs.start()

        for c in range(0, D, 256):
            tmp[0:ROWS, :] = dot_nn(chan[r, :], w_in[:, c : c + 256])
            a = jnp.zeros((8, 256), F32)
            for b in range(nblk):
                rb = pl.ds(base + 16 * b, 16)
                value, slope = gelu_pair(tmp[16 * b : 16 * b + 16, :] + bs[0:1, c : c + 256])
                hid[rb, c : c + 256] = value.astype(BF16)
                low = (slope * dhid[rb, c : c + 256]).astype(BF16)
                dpre[rb, c : c + 256] = low
                a = a + fold(low.astype(F32))
            acc[5, :, c : c + 256] += a
        for c in range(0, D, 256):
            part = dot_nt(dpre[r, :], w_in[c : c + 256, :])
            zpart[pl.ds(i * last, last), c : c + 256] = part[0:last].astype(BF16)
            tails[i, :, c : c + 256] = part[last : last + 8]
        start_up(chunks_of(d_rows, i))


    for i in range(count):
        forward(i)
    tick()

    zpart[zrows(seam), :] = pack_tails()
    start_up([seam])

    def partial_out(i):
        r = pl.ds(i * ROWS, ROWS)
        ro = pl.ds(o_rows + i * last, last)
        for c in range(0, D, 256):
            part = dot_nn(hid[r, :], w_out[:, c : c + 256])
            zpart[ro, c : c + 256] = part[0:last].astype(BF16)
            tails[i, :, c : c + 256] = part[last : last + 8]

    for i in range(count):
        partial_out(i)
    tick()
    zpart[zrows(seam + 1), :] = pack_tails()
    start_up(range(seam + 1, steps))

    def weight_grad(j):
        cols = pl.ds(j * 256, 256)
        gw[0, cols, :] = dot_tn(chan[:, cols], dpre[...])
        gw[1, cols, :] = dot_tn(dout[:, cols], hid[...])

    for j in range(D // 256):
        weight_grad(j)
    for c in range(nc):
        rows = pl.ds(pl.multiple_of((2 * c + 1 - core) * shard, 8), shard)
        for m in range(2):
            wsib_s[c, m] = gw[m, rows, :].astype(BF16)
    w_sib = rcopy(wsib_s, wsib_r, w_sem.at[0, 0], w_sem.at[1, 0], (sib, t))
    w_sib.start()
    tick()

    sqs[...] = jnp.zeros(sqs.shape, F32)

    def square(i):
        r = pl.ds(i * ROWS, ROWS)
        g1 = dot_nt(chan[r, :], chan[r, :]) * dot_nt(dpre[r, :], dpre[r, :])
        g2 = dot_nt(dout[r, :], dout[r, :]) * dot_nt(hid[r, :], hid[r, :])
        sqs[pl.ds(i, 1), 0:ROWS] = jnp.sum(g1 + g2, axis=0, keepdims=True)

    for i in range(count):
        square(i)
    tick()

    w_sib.wait_recv()

    def w_chip(n, k):
        return rcopy(wch_s.at[n], wch_r.at[n], w_sem.at[0, n + 1], w_sem.at[1, n + 1], (peer(k), t))

    def w_share(dest, m):
        rows = pl.ds(pl.multiple_of((2 * dest + core) * shard, 8), shard)
        return gw[m, rows, :] + wsib_r[dest, m].astype(F32)

    first, second = 1 + core, 2 - core

    infl[...] = jnp.zeros(infl.shape, F32)

    def query(j):
        k = j // 2
        if j == 0:
            slot, cin, din, hid_q, pre_q = me, chan, dout, hid, dpre
        else:
            slot = peer_sib(k) if j % 2 else peer(k)
            if j % 2:
                dqs.from_sib(k)
                cqs.from_sib(k)
            cin, din, hid_q, pre_q = cq.at[slot], dq.at[slot], hq, pq
            for c in range(0, D, 256):
                tmp[0:ROWS, :] = dot_nn(cin[...], w_in[:, c : c + 256])
                tmp[ROWS : 2 * ROWS, :] = dot_nt(din[...], w_out[c : c + 256, :])
                for b in range(0, ROWS, 16):
                    value, slope = gelu_pair(tmp[b : b + 16, :] + bs[0:1, c : c + 256])
                    hq[b : b + 16, c : c + 256] = value.astype(BF16)
                    pq[b : b + 16, c : c + 256] = (slope * tmp[ROWS + b : ROWS + b + 16, :]).astype(BF16)
        for q in range(count - QRY_DEV):
            r = slice((QRY_DEV + q) * ROWS, (QRY_DEV + q + 1) * ROWS)
            g1 = dot_nt(cin[0:ROWS, :], chan[r, :]) * dot_nt(pre_q[0:ROWS, :], dpre[r, :])
            g2 = dot_nt(din[0:ROWS, :], dout[r, :]) * dot_nt(hid_q[0:ROWS, :], hid[r, :])
            infl[q, pl.ds(slot, 1), 0:ROWS] = jnp.sum(g1 + g2, axis=0, keepdims=True)

    dqs.relay(1)
    dqs.relay(2)
    query(0)
    tick()
    query(1)
    tick()
    tick()
    cqs.relay(1)
    cqs.relay(2)
    for n, dest in ((0, chip ^ 3), (1, chip ^ first)):
        for m in range(2):
            wch_s[n, m] = w_share(dest, m).astype(BF16)
        w_chip(n, first).start()
    for j in (2, 4, 3, 5):
        query(j)
        tick()
    tick(until=seam)

    gtok[...] = jnp.zeros(gtok.shape, F32)

    def ing_copy(i):
        return pltpu.make_async_copy(ing_s.at[i], ing_o.at[i], out_sem.at[0, i])

    zfin([seam])
    rest = ztot[zrows(seam), :].astype(F32)
    for i in range(count):
        rests[i, 0:tail, :] = rest[tail * i : tail * (i + 1)]
        rests[i, tail:16, :] = jnp.zeros((16 - tail, D), F32)

    def backward(i):
        zfin(chunks_of(d_rows, i))
        base = i * ROWS
        r = pl.ds(base, ROWS)
        a1 = jnp.zeros((8, D), F32)
        a3 = jnp.zeros((8, D), F32)
        for b in range(nblk):
            rb = pl.ds(base + 16 * b, 16)
            if b < nblk - 1:
                e = ztot[pl.ds(i * last + 16 * b, 16), :].astype(F32)
            else:
                e = rests[i]
            xhat = xh2[rb, :]
            a1 = a1 + fold(e * xhat)
            a3 = a3 + fold(e)
            eg = e * gs[1:2, :]
            m1 = jnp.mean(eg, axis=-1, keepdims=True)
            m2 = jnp.mean(eg * xhat, axis=-1, keepdims=True)
            d = dout[rb, :].astype(F32) + rs2[rb, 0:1] * (eg - m1 - xhat * m2)
            dhid[rb, :] = d
            dmix[16 * b : 16 * b + 16, :] = d.astype(BF16)
        acc[1] += a1
        acc[3] += a3
        for c in range(0, D, 256):
            tmp[0:K, :] = dot_nn(toko_t[0:K, 0:ROWS], dmix[:, c : c + 256])
            for b in range(0, K, 16):
                dtok[b : b + 16, c : c + 256] = (
                    tmp[b : b + 16, :] * tgp[i, b : b + 16, c : c + 256]
                ).astype(BF16)
        gtok[0, 0:K, 0:ROWS] += dot_nt(dtok[...], normed[r, :])
        gtok[1, :, 0:ROWS] += dot_nt(th[i], dmix[...])
        for c in range(0, D, 256):
            dnorm[:, c : c + 256] = dot_nn(toki[:, 0:K], dtok[:, c : c + 256])
        a0 = jnp.zeros((8, D), F32)
        a2 = jnp.zeros((8, D), F32)
        for b in range(nblk):
            rb = pl.ds(base + 16 * b, 16)
            e = dnorm[16 * b : 16 * b + 16, :]
            xhat = xh1[rb, :]
            a0 = a0 + fold(e * xhat)
            a2 = a2 + fold(e)
            eg = e * gs[0:1, :]
            m1 = jnp.mean(eg, axis=-1, keepdims=True)
            m2 = jnp.mean(eg * xhat, axis=-1, keepdims=True)
            d = (dhid[rb, :] + rs1[rb, 0:1] * (eg - m1 - xhat * m2)).astype(BF16)
            n = min(16, patches - 16 * b)
            ing_s[i, 16 * b : 16 * b + n, :] = d[0:n]
        acc[0] += a0
        acc[2] += a2
        ing_copy(i).start()
        tick()

    for i in range(count):
        backward(i)
        if i == 0:
            dqs.relay(3)
            cqs.relay(3)
        if i == 1:
            w_chip(0, first).wait_recv()
            for m in range(2):
                wch_s[2, m] = (w_share(chip ^ second, m) + wch_r[0, m].astype(F32)).astype(BF16)
            w_chip(2, second).start()

    for c in range(nc):
        rows = pl.ds(pl.multiple_of((2 * c + 1 - core) * kb, 8), kb)
        for m in range(2):
            tsib_s[c, m] = gtok[m, rows, :]
    t_sib = rcopy(tsib_s, tsib_r, t_sem.at[0, 0], t_sem.at[1, 0], (sib, t))
    t_sib.start()
    vec[...] = jnp.zeros(vec.shape, F32)
    for q in range(6):
        vec[q : q + 1, :] = jnp.sum(acc[q], axis=0, keepdims=True)
    vec[6:7, 0:256] = gtok[1, K : K + 1, :]
    v_sib = rcopy(vec, vsib_r, v_sem.at[0, 0], v_sem.at[1, 0], (sib, t))
    v_sib.start()
    query(6)
    tick()
    v_sib.wait_recv()

    def v_chip(k):
        return rcopy(
            vch.at[chip], vch.at[chip], v_sem.at[0, k], v_sem.at[1, k], (peer(k), t)
        )

    vch[chip] = vec[...] + vsib_r[...]
    for k in range(1, nc):
        v_chip(k).start()
    t_sib.wait_recv()

    def t_chip(k):
        return rcopy(
            tch_s.at[k - 1], tch_r.at[k - 1], t_sem.at[0, k], t_sem.at[1, k], (peer(k), t)
        )

    for k in range(1, nc):
        dest = chip ^ k
        rows = pl.ds(pl.multiple_of((2 * dest + core) * kb, 8), kb)
        for m in range(2):
            tch_s[k - 1, m] = gtok[m, rows, :] + tsib_r[dest, m]
        t_chip(k).start()
    query(7)

    def as_row(values):
        totals = jnp.sum(values, axis=1, keepdims=True)
        at = lax.broadcasted_iota(jnp.int32, (values.shape[0], 128), 0)
        lane = lax.broadcasted_iota(jnp.int32, (values.shape[0], 128), 1)
        return jnp.sum(jnp.where(at == lane, totals, 0.0), axis=0, keepdims=True)

    zsm[t] = jnp.zeros((8, 128), F32)
    zsm[t, 0:1, :] = as_row(sqs[...]) / (2.0 * D * FF)
    for q in range(count - QRY_DEV):
        zsm[t, 1 + q : 2 + q, :] = as_row(infl[q]) * (2.0 * D * FF) ** (-0.5)

    def sm_copy(k):
        return rcopy(
            zsm.at[t], zsm.at[t], s_sem.at[0, k - 1], s_sem.at[1, k - 1], (me, (t + k) % 4)
        )

    for k in (1, 2, 3):
        sm_copy(k).start()

    tick()

    for m, out in enumerate((gwi_k, gwo_k)):
        out[...] = w_share(chip, m)
    for n in (1, 2):
        w_chip(n, first).wait_recv()
        for m, out in enumerate((gwi_k, gwo_k)):
            out[...] += wch_r[n, m].astype(F32)

    def act_copy(i):
        return pltpu.make_async_copy(act_s.at[i], act_o.at[i], out_sem.at[1, i])

    def act(i):
        tick(chunks_of(o_rows, i)[-1])
        zfin([seam + 1] * (i == 0) + chunks_of(o_rows, i))
        start = o_rows + i * last
        for b in range(0, last, 16):
            ro = slice(start + b, start + b + 16)
            a = xf[i * ROWS + b : i * ROWS + b + 16, :] + ztot[ro, :].astype(F32) + bs[1:2, :]
            act_s[i, b : b + 16, :] = a.astype(BF16)
        a = ztot[zrows(seam + 1), :].astype(F32)[tail * i : tail * (i + 1)] + bs[1:2, :]
        a = a + xf[i * ROWS + last : i * ROWS + patches, :]
        act_s[i, last:patches, :] = a.astype(BF16)
        act_copy(i).start()

    act(0)
    tick()
    act(1)

    for k in (1, 2, 3):
        sm_copy(k).wait_recv()
    sm_k[...] = (zsm[0] + zsm[1]) + (zsm[2] + zsm[3])
    rows = pl.ds(pl.multiple_of(me * kb, 8), kb)
    for m, out in enumerate((gti_k, gto_k)):
        out[...] = gtok[m, rows, :] + tsib_r[chip, m]
    for k in range(1, nc):
        t_chip(k).wait_recv()
        for m, out in enumerate((gti_k, gto_k)):
            out[...] += tch_r[k - 1, m]
    for k in range(1, nc):
        v_chip(k).wait_recv()
    total = vch[0]
    for c in range(1, nc):
        total = total + vch[c]
    tbo_k[...] = total[:, 0:256]
    vec_k[...] = pltpu.roll(total, (D - me * shard) % D, 1)[:, 0:128]
    stores = [(gwi_k, gwi_o), (gwo_k, gwo_o), (gti_k, gti_o), (gto_k, gto_o), (vec_k, vec_o), (tbo_k, tbo_o), (sm_k, sm_o)]
    stores = [pltpu.make_async_copy(a, b, small_sem.at[n]) for n, (a, b) in enumerate(stores)]
    for c in stores:
        c.start()
    act(count - 1)

    params.drain()
    dqs.drain()
    cqs.drain()

    @pl.when(end)
    def _():
        rcopy(zpart, zrx, z_sent.at[0], z_sem.at[0, 0], (me, end_peer)).wait_send()

    @pl.when(mid)
    def _():
        rcopy(zpair, zrxp, z_sent.at[1], z_sem.at[1, 0], (me, mid_peer)).wait_send()
        rcopy(ztot, ztot, z_sent.at[2], z_sem.at[2, 0], (me, mid_end)).wait_send()

    w_sib.wait_send()
    t_sib.wait_send()
    v_sib.wait_send()
    for k in range(1, nc):
        w_chip(k - 1, first).wait_send()
        t_chip(k).wait_send()
        v_chip(k).wait_send()
    for k in (1, 2, 3):
        sm_copy(k).wait_send()
    for c in stores:
        c.wait()
    for i in range(count):
        ing_copy(i).wait()
        act_copy(i).wait()


def finish(shard, ks, patches, count, queries, act, ing, gwi, gwo, gti_h, gto_h, vec_h, tbo_h, sm_h, *refs):
    big, small, refs = refs[:4], refs[4:14], refs[14:]
    held, got, made, sem = refs[:4], refs[4:9], refs[9:19], refs[19]
    pieces = [(n, i) for n in (0, 1) for i in range(count)] + [(2, None), (3, None)]

    def part(ref, i):
        return ref if i is None else ref.at[i]

    loads = [
        pltpu.make_async_copy(a, b, sem.at[0, n])
        for n, (a, b) in enumerate(zip((gti_h, gto_h, vec_h, tbo_h, sm_h), got))
    ]
    moves = []
    for n, i in pieces:
        kept, at = part(held[n], i), len(moves)
        moves.append(
            (
                pltpu.make_async_copy(part((act, ing, gwi, gwo)[n], i), kept, sem.at[1, at]),
                pltpu.make_async_copy(kept, part(big[n], i), sem.at[2, at]),
            )
        )
    for c in loads:
        c.start()
    for load, _ in moves:
        load.start()
    for c in loads:
        c.wait()
    gti, gto, vec, tbo, sm = got
    gains, shifts, gti_o, gto_o, gtb_o, tbo_o, gbi_o, gbo_o, sq_o, infl_o = made
    gains[...] = vec[0:2, 0:shard]
    shifts[...] = vec[2:4, 0:shard]
    gbo_o[...] = vec[4:5, 0:shard]
    gbi_o[...] = vec[5:6, 0:shard]
    gti_o[...] = gti[0:ks, 0:patches]
    gto_o[...] = gto[0:ks, 0:patches]
    tbo_o[...] = tbo[6:7, 0:patches]
    column = gti[0:ks, patches : patches + 1]
    eye = lax.broadcasted_iota(jnp.int32, (ks, ks), 0) == lax.broadcasted_iota(jnp.int32, (ks, ks), 1)
    gtb_o[...] = jnp.sum(jnp.where(eye, column, 0.0), axis=0, keepdims=True)
    sq_o[...] = sm[0:1, 0:count]
    for t in range(infl_o.shape[0]):
        infl_o[t : t + 1, :] = sm[1 + t : 2 + t, 0:queries]
    stores = [pltpu.make_async_copy(a, b, sem.at[3, n]) for n, (a, b) in enumerate(zip(made, small))]
    for c in stores:
        c.start()
    for load, store in moves:
        load.wait()
        store.start()
    for c in stores + [store for _, store in moves]:
        c.wait()


def fused(
    n_dp,
    images,
    cotangent,
    norm_gains,
    norm_shifts,
    tok_in,
    tok_out_t,
    tok_bias_in,
    tok_bias_out,
    w_in,
    bias_in,
    w_out,
    bias_out,
):
    count, patches, width = images.shape
    nc = n_dp // 2
    ks = tok_in.shape[1]
    toks = ks * n_dp
    kb = -(-ks // 16) * 16
    K = n_dp * kb
    KA = K + 16
    KL = -(-KA // 128) * 128
    R = count * ROWS
    zrows, steps = sum(z_sizes(count)), len(z_sizes(count))
    shard = width // n_dp
    hidden = w_in.shape[1]
    anyspace = pl.BlockSpec(memory_space=pl.ANY)
    V = pltpu.VMEM
    dma = lambda *s: pltpu.SemaphoreType.DMA(s)
    scratch = dict(
        gwi_k=V((shard, hidden), F32),
        gwo_k=V((shard, hidden), F32),
        gti_k=V((kb, 256), F32),
        gto_k=V((kb, 256), F32),
        vec_k=V((8, 128), F32),
        tbo_k=V((8, 256), F32),
        sm_k=V((8, 128), F32),
        gains_r=V(norm_gains.shape, BF16),
        shifts_r=V(norm_shifts.shape, BF16),
        tok_in_r=V((ks, patches), BF16),
        tok_out_r=V((ks, patches), BF16),
        tok_bias_r=V(tok_bias_in.shape, BF16),
        tok_bias_out_r=V(tok_bias_out.shape, BF16),
        bias_in_r=V(bias_in.shape, BF16),
        bias_out_r=V(bias_out.shape, BF16),
        x_raw=V((count, patches, D), BF16),
        d_raw=V((count, patches, D), BF16),
        w_in=V((D, hidden), BF16),
        w_out=V((hidden, D), BF16),
        act_s=V((count, patches, D), BF16),
        ing_s=V((count, patches, D), BF16),
        pb=V((n_dp, 2 * kb + 16, 256), BF16),
        aug=V((ROWS, 128), F32),
        misc=V((16, 256), F32),
        toki_t=V((K, 256), BF16),
        toko_t=V((KA, 256), BF16),
        toki=V((ROWS, KL), BF16),
        toko=V((ROWS, KL), BF16),
        gs=V((16, D), F32),
        bs=V((8, D), F32),
        dout=V((R, D), BF16),
        dhid=V((R, hidden), F32),
        xf=V((R, D), F32),
        xh1=V((R, D), F32),
        rs1=V((R, 128), F32),
        xh2=V((R, D), F32),
        rs2=V((R, 128), F32),
        normed=V((R, D), BF16),
        th=V((count, KA, D), BF16),
        tgp=V((count, K, D), F32),
        chan=V((R, D), BF16),
        hid=V((R, hidden), BF16),
        dpre=V((R, hidden), BF16),
        tmp=V((max(K, 2 * ROWS), 256), F32),
        dq=V((n_dp, ROWS, D), BF16),
        cq=V((n_dp, ROWS, D), BF16),
        hq=V((ROWS, hidden), BF16),
        pq=V((ROWS, hidden), BF16),
        infl=V((count - QRY_DEV, n_dp, 256), F32),
        sqs=V((8, 256), F32),
        dmix=V((ROWS, D), BF16),
        dtok=V((K, D), BF16),
        dnorm=V((ROWS, D), F32),
        tails=V((count, 8, D), F32),
        rests=V((count, 16, D), F32),
        zpart=V((zrows, D), BF16),
        zrx=V((zrows, D), BF16),
        zpair=V((zrows, D), BF16),
        zrxp=V((zrows, D), BF16),
        ztot=V((zrows, D), BF16),
        gw=V((2, D, hidden), F32),
        wsib_s=V((nc, 2, shard, hidden), BF16),
        wsib_r=V((nc, 2, shard, hidden), BF16),
        wch_s=V((nc - 1, 2, shard, hidden), BF16),
        wch_r=V((nc - 1, 2, shard, hidden), BF16),
        gtok=V((2, KA, 256), F32),
        tsib_s=V((nc, 2, kb, 256), F32),
        tsib_r=V((nc, 2, kb, 256), F32),
        tch_s=V((nc - 1, 2, kb, 256), F32),
        tch_r=V((nc - 1, 2, kb, 256), F32),
        acc=V((6, 8, D), F32),
        vec=V((8, D), F32),
        vsib_r=V((8, D), F32),
        vch=V((nc, 8, D), F32),
        zsm=V((4, 8, 128), F32),
        in_sem=dma(12),
        out_sem=dma(2, count),
        small_sem=dma(7),
        pb_sem=dma(8),
        dq_sem=dma(8),
        cq_sem=dma(8),
        z_sem=dma(3, steps),
        z_sent=dma(3),
        w_sem=dma(2, nc),
        t_sem=dma(2, nc),
        v_sem=dma(2, nc),
        s_sem=dma(2, 3),
    )
    outs = [
        (images.shape, BF16, anyspace),
        (images.shape, BF16, anyspace),
        ((shard, hidden), F32, anyspace),
        ((shard, hidden), F32, anyspace),
        ((kb, 256), F32, anyspace),
        ((kb, 256), F32, anyspace),
        ((8, 128), F32, anyspace),
        ((8, 256), F32, anyspace),
        ((8, 128), F32, anyspace),
    ]
    names = list(scratch)
    n_in, n_out = 12, len(outs)

    def body(*refs):
        mega(n_dp, count, patches, toks, *refs[: n_in + n_out], **dict(zip(names, refs[n_in + n_out :])))

    act, ing, gwi, gwo, gti, gto, vec, tbo, sm = pl.pallas_call(
        body,
        out_shape=[jax.ShapeDtypeStruct(s, d) for s, d, _ in outs],
        in_specs=[anyspace] * 12,
        out_specs=[o[2] for o in outs],
        scratch_shapes=list(scratch.values()),
        compiler_params=pltpu.CompilerParams(
            collective_id=0, has_side_effects=True, vmem_limit_bytes=60 * 2**20
        ),
        name="mixer",
    )(
        images,
        cotangent,
        w_in,
        w_out,
        norm_gains,
        norm_shifts,
        tok_in.T,
        tok_out_t.T,
        tok_bias_in,
        tok_bias_out,
        bias_in,
        bias_out,
    )
    queries, trains = n_dp * QRY_DEV, count - QRY_DEV
    shapes = [
        (images.shape, BF16),
        (images.shape, BF16),
        ((shard, hidden), F32),
        ((shard, hidden), F32),
        ((2, shard), F32),
        ((2, shard), F32),
        ((ks, patches), F32),
        ((ks, patches), F32),
        ((1, ks), F32),
        ((1, patches), F32),
        ((1, shard), F32),
        ((1, shard), F32),
        ((1, count), F32),
        ((trains, queries), F32),
    ]
    smalls = [(o.shape, F32) for o in (gti, gto, vec, tbo, sm)]
    out = pl.pallas_call(
        functools.partial(finish, shard, ks, patches, count, queries),
        out_shape=[jax.ShapeDtypeStruct(s, d) for s, d in shapes],
        in_specs=[anyspace] * 9,
        out_specs=[anyspace] * 14,
        scratch_shapes=[V(s, d) for s, d in shapes[:4] + smalls + shapes[4:]] + [dma(4, 10)],
        name="finish",
    )(act, ing, gwi, gwo, gti, gto, vec, tbo, sm)
    act, ing, gwi, gwo, gains, shifts, gti, gto, gtb, tbo, gbi, gbo, squares, influence = out
    return (
        act,
        ing,
        gains,
        shifts,
        gti.T,
        gto.T,
        gtb,
        tbo.reshape(patches),
        gwi,
        gbi.reshape(shard),
        gwo.T,
        gbo.reshape(shard),
        squares.reshape(count),
        influence.T,
    )


def layer_norm(values, gain, shift):
    center = values - jnp.mean(values, axis=-1, keepdims=True)
    spread = jnp.mean(center * center, axis=-1, keepdims=True)
    return center * lax.rsqrt(spread + 1e-06) * gain + shift


def smooth(values):
    return jax.nn.gelu(values, approximate=True)


def contract(left, right, left_dim, right_dim):
    return lax.dot_general(
        left, right, (((left_dim,), (right_dim,)), ((), ())), preferred_element_type=jnp.float32
    )


def per_device(
    images,
    cotangent,
    norm_gains,
    norm_shifts,
    tok_in,
    tok_out_t,
    tok_bias_in,
    tok_bias_out,
    w_in,
    bias_in,
    w_out,
    bias_out,
):
    gains, shifts, tok_first, tok_second, tok_bias = (
        lax.all_gather(norm_gains, "dp", axis=1, tiled=True),
        lax.all_gather(norm_shifts, "dp", axis=1, tiled=True),
        lax.all_gather(tok_in, "dp", axis=1, tiled=True),
        lax.all_gather(tok_out_t, "dp", axis=1, tiled=True),
        lax.all_gather(tok_bias_in, "dp", axis=1, tiled=True),
    )
    gains = gains.astype(jnp.float32)
    shifts = shifts.astype(jnp.float32)
    count, patches, width = images.shape
    rows = count * patches
    inputs = images.astype(jnp.float32)
    normed_one, first_back = jax.vjp(layer_norm, inputs, gains[0], shifts[0])
    normed_low = normed_one.astype(jnp.bfloat16)
    tok_pre = (
        jnp.einsum("sk,nsd->nkd", tok_first, normed_low, preferred_element_type=jnp.float32)
        + tok_bias[0].astype(jnp.float32)[None, :, None]
    )
    tok_hidden = smooth(tok_pre).astype(jnp.bfloat16)
    tok_mixed = (
        jnp.einsum("sk,nkd->nsd", tok_second, tok_hidden, preferred_element_type=jnp.float32)
        + tok_bias_out.astype(jnp.float32)[None, :, None]
    )
    resid = inputs + tok_mixed
    normed_two, second_back = jax.vjp(layer_norm, resid, gains[1], shifts[1])
    chan_in = normed_two.astype(jnp.bfloat16).reshape(rows, width)
    chan_pre = jnp.dot(chan_in, w_in, preferred_element_type=jnp.float32) + bias_in.astype(
        jnp.float32
    )
    hidden = smooth(chan_pre).astype(jnp.bfloat16)
    partial_out = jnp.dot(hidden, w_out, preferred_element_type=jnp.float32)
    mixed = lax.psum(partial_out, "tensor")
    activations = (
        resid + mixed.reshape(count, patches, width) + bias_out.astype(jnp.float32)
    ).astype(jnp.bfloat16)
    dout_rows = cotangent.reshape(rows, width)
    d_hidden = contract(dout_rows, w_out, 1, 1)
    smooth_value, smooth_back = jax.vjp(smooth, chan_pre)
    d_pre = smooth_back(d_hidden)[0].astype(jnp.bfloat16)
    d_chan_part = contract(d_pre, w_in, 1, 1)
    d_chan = lax.psum(d_chan_part, "tensor")
    d_resid_norm, d_gain_two, d_shift_two = second_back(d_chan.reshape(count, patches, width))
    d_resid = cotangent.astype(jnp.float32) + d_resid_norm
    d_mixed = d_resid.astype(jnp.bfloat16)
    d_tokhid = jnp.einsum("sk,nsd->nkd", tok_second, d_mixed, preferred_element_type=jnp.float32)
    tok_value, tok_back = jax.vjp(smooth, tok_pre)
    d_tokpre = tok_back(d_tokhid)[0].astype(jnp.bfloat16)
    grad_second = jnp.einsum("nsd,nkd->sk", d_mixed, tok_hidden, preferred_element_type=jnp.float32)
    grad_first = jnp.einsum("nsd,nkd->sk", normed_low, d_tokpre, preferred_element_type=jnp.float32)
    grad_tbias = jnp.sum(d_tokpre, axis=(0, 2), dtype=jnp.float32)[None, :]
    grad_tbias_out = jnp.sum(d_mixed, axis=(0, 2), dtype=jnp.float32)
    d_normed = jnp.einsum("sk,nkd->nsd", tok_first, d_tokpre, preferred_element_type=jnp.float32)
    d_input_norm, d_gain_one, d_shift_one = first_back(d_normed)
    input_grad = (d_resid + d_input_norm).astype(jnp.bfloat16)
    grad_win = contract(chan_in, d_pre, 0, 0)
    grad_wout_t = contract(dout_rows, hidden, 0, 0)
    grad_bin = jnp.sum(d_pre, axis=0, dtype=jnp.float32)
    grad_bout = jnp.sum(dout_rows, axis=0, dtype=jnp.float32)
    share_win, share_wout_t, share_bin, share_bout = (
        lax.psum_scatter(grad_win, "dp", scatter_dimension=0, tiled=True),
        lax.psum_scatter(grad_wout_t, "dp", scatter_dimension=0, tiled=True),
        lax.psum_scatter(grad_bin, "dp", scatter_dimension=0, tiled=True),
        lax.psum_scatter(grad_bout, "dp", scatter_dimension=0, tiled=True),
    )
    share_gains, share_shifts, share_first, share_second, share_tbias = (
        lax.psum_scatter(
            jnp.stack([d_gain_one, d_gain_two]), "dp", scatter_dimension=1, tiled=True
        ),
        lax.psum_scatter(
            jnp.stack([d_shift_one, d_shift_two]), "dp", scatter_dimension=1, tiled=True
        ),
        lax.psum_scatter(grad_first, "dp", scatter_dimension=1, tiled=True),
        lax.psum_scatter(grad_second, "dp", scatter_dimension=1, tiled=True),
        lax.psum_scatter(grad_tbias, "dp", scatter_dimension=1, tiled=True),
    )
    total_tbias_out = lax.psum(grad_tbias_out, "dp")
    chan_cube = chan_in.reshape(count, patches, width)
    pre_cube = d_pre.reshape(count, patches, -1)
    hidden_cube = hidden.reshape(count, patches, -1)
    def against(chan, pre, dout, low):
        grams = [
            jnp.einsum("sd,npd->nsp", a, b, preferred_element_type=jnp.float32)
            for a, b in ((chan, chan_cube), (pre, pre_cube), (dout, cotangent), (low, hidden_cube))
        ]
        return jnp.sum(grams[0] * grams[1] + grams[2] * grams[3], axis=(1, 2))

    own = lax.map(lambda a: against(*a), (chan_cube, pre_cube, cotangent, hidden_cube))
    squares = jnp.diagonal(own)
    queries = tuple(
        lax.all_gather(a[:QRY_DEV], "dp", axis=0, tiled=True)
        for a in (chan_cube, pre_cube, cotangent, hidden_cube)
    )
    influence = lax.map(lambda a: against(*a), queries)[:, QRY_DEV:]
    influence, squares = lax.psum((influence, squares), "tensor")
    sqnorms = squares / (2.0 * D * FF)
    influence = influence * (2.0 * D * FF) ** (-0.5)
    return (
        activations,
        input_grad,
        share_gains,
        share_shifts,
        share_first,
        share_second,
        share_tbias,
        total_tbias_out,
        share_win,
        share_bin,
        share_wout_t.T,
        share_bout,
        sqnorms,
        influence,
    )


def solution(mesh):
    placed = (
        P("dp", None, None),
        P("dp", None, None),
        P(None, "dp"),
        P(None, "dp"),
        P(None, "dp"),
        P(None, "dp"),
        P(None, "dp"),
        P(),
        P(None, "tensor"),
        P("tensor"),
        P("tensor", None),
        P(),
    )
    n_dp = mesh.shape["dp"]
    fits = n_dp == 8 and mesh.shape["tensor"] == 4
    device = functools.partial(fused, n_dp) if fits else per_device
    return jax.shard_map(
        device,
        mesh=mesh,
        in_specs=placed,
        out_specs=(
            P("dp", None, None),
            P("dp", None, None),
            P(None, "dp"),
            P(None, "dp"),
            P(None, "dp"),
            P(None, "dp"),
            P(None, "dp"),
            P(),
            P("dp", "tensor"),
            P(("tensor", "dp")),
            P("tensor", "dp"),
            P("dp"),
            P("dp"),
            P(None, "dp"),
        ),
        check_vma=False,
    )
```

```python
import functools

import jax
import jax.numpy as jnp
from jax import lax
from jax.experimental import pallas as pl
from jax.experimental.pallas import tpu as pltpu
from jax.sharding import PartitionSpec as P

D = 768
FF = 3072
QRY_DEV = 1
HIGH = lax.Precision.HIGHEST
MESH = pl.DeviceIdType.MESH
F32 = jnp.float32
BF16 = jnp.bfloat16

ROWS = 208
C1 = 0.7978845608028654
C2 = 0.044715


def dot_nn(a, b):
    return lax.dot_general(a, b, (((1,), (0,)), ((), ())), preferred_element_type=F32)


def dot_nt(a, b):
    return lax.dot_general(a, b, (((1,), (1,)), ((), ())), preferred_element_type=F32)


def dot_tn(a, b):
    return lax.dot_general(a, b, (((0,), (0,)), ((), ())), preferred_element_type=F32)


def gelu_pair(v):
    u = v * v
    th = jnp.tanh(v * (C1 + (C1 * C2) * u))
    hp = 0.5 + 0.5 * th
    value = v * hp
    slope = hp + (0.5 * v) * (1.0 - th * th) * (C1 + (3.0 * C1 * C2) * u)
    return value, slope


def z_sizes(count):
    full = [64] * (3 * count)
    return full + [16, 16] + full


def fold(v):
    out = v[0:8]
    for s in range(8, v.shape[0], 8):
        out = out + v[s : s + 8]
    return out


def mega(
    n_dp,
    count,
    patches,
    toks,
    images,
    cotangent,
    w_in_h,
    w_out_h,
    gains_h,
    shifts_h,
    tok_in_h,
    tok_out_h,
    tok_bias_h,
    tok_bias_out_h,
    bias_in_h,
    bias_out_h,
    act_o,
    ing_o,
    gwi_o,
    gwo_o,
    gti_o,
    gto_o,
    vec_o,
    tbo_o,
    sm_o,
    gwi_k,
    gwo_k,
    gti_k,
    gto_k,
    vec_k,
    tbo_k,
    sm_k,
    gains_r,
    shifts_r,
    tok_in_r,
    tok_out_r,
    tok_bias_r,
    tok_bias_out_r,
    bias_in_r,
    bias_out_r,
    x_raw,
    d_raw,
    w_in,
    w_out,
    act_s,
    ing_s,
    pb,
    aug,
    misc,
    toki_t,
    toko_t,
    toki,
    toko,
    gs,
    bs,
    dout,
    dhid,
    xf,
    xh1,
    rs1,
    xh2,
    rs2,
    normed,
    th,
    tgp,
    chan,
    hid,
    dpre,
    tmp,
    dq,
    cq,
    hq,
    pq,
    infl,
    sqs,
    dmix,
    dtok,
    dnorm,
    tails,
    rests,
    zpart,
    zrx,
    zpair,
    zrxp,
    ztot,
    gw,
    wsib_s,
    wsib_r,
    wch_s,
    wch_r,
    gtok,
    tsib_s,
    tsib_r,
    tch_s,
    tch_r,
    acc,
    vec,
    vsib_r,
    vch,
    zsm,
    in_sem,
    out_sem,
    small_sem,
    pb_sem,
    dq_sem,
    cq_sem,
    z_sem,
    z_sent,
    w_sem,
    t_sem,
    v_sem,
    s_sem,
):
    me = lax.axis_index("dp")
    t = lax.axis_index("tensor")
    core = me % 2
    chip = me // 2
    sib = chip * 2 + 1 - core
    nc = n_dp // 2
    mid = (t == 1) | (t == 2)
    end = (t == 0) | (t == 3)
    end_peer = jnp.where(t < 2, 1, 2)
    mid_end = jnp.where(t < 2, 0, 3)
    mid_peer = 3 - t
    shard = D // n_dp
    ks = toks // n_dp
    kb = -(-ks // 16) * 16
    K = n_dp * kb
    KA = K + 16
    R = count * ROWS
    nblk = ROWS // 16
    last = ROWS - 16
    tail = patches - last

    def peer(k):
        return (chip ^ k) * 2 + core

    def peer_sib(k):
        return (chip ^ k) * 2 + 1 - core

    def rcopy(a, b, ss, rs, dev):
        return pltpu.make_async_remote_copy(
            src_ref=a, dst_ref=b, send_sem=ss, recv_sem=rs, device_id=dev, device_id_type=MESH
        )

    class Gather:
        def __init__(self, buf, sem):
            self.buf, self.sem = buf, sem

        def chip_copy(self, block, k, n):
            b = self.buf.at[block]
            return rcopy(b, b, self.sem.at[0], self.sem.at[1 + n], (peer(k), t))

        def sib_copy(self, k):
            b = self.buf.at[peer(k)]
            return rcopy(b, b, self.sem.at[0], self.sem.at[4 + k], (sib, t))

        def start(self, across=False):
            for k in (1, 2, 3) if across else (1, 2):
                self.chip_copy(me, k, k - 1).start()
            self.sib_copy(0).start()

        def relay(self, k, across=False):
            self.chip_copy(peer(k), k, k - 1).wait_recv()
            if k < 3 and not across:

                @pl.when(core == k - 1)
                def _():
                    self.chip_copy(peer(k), 3 - k, 2).start()

            self.sib_copy(k).start()

        def from_sib(self, k):
            b = self.buf.at[peer_sib(k)]
            rcopy(b, b, self.sem.at[0], self.sem.at[4 + k], (sib, t)).wait_recv()

        def drain(self):
            b = self.buf.at[pl.ds(0, 7)]
            rcopy(b, b, self.sem.at[0], self.sem.at[1], (sib, t)).wait_send()

    params, dqs, cqs = Gather(pb, pb_sem), Gather(dq, dq_sem), Gather(cq, cq_sem)

    barrier = pltpu.get_barrier_semaphore()
    others = [(sib, t)] + [(peer(k), t) for k in range(1, nc)] + [(me, (t + k) % 4) for k in (1, 2, 3)]
    for dev in others:
        pl.semaphore_signal(barrier, inc=1, device_id=dev, device_id_type=MESH)

    pairs = [
        (gains_h, gains_r),
        (shifts_h, shifts_r),
        (tok_in_h, tok_in_r),
        (tok_out_h, tok_out_r),
        (tok_bias_h, tok_bias_r),
        (cotangent, d_raw),
        (w_out_h, w_out),
        (images, x_raw),
        (w_in_h, w_in),
        (tok_bias_out_h, tok_bias_out_r),
        (bias_in_h, bias_in_r),
        (bias_out_h, bias_out_r),
    ]
    loads = [pltpu.make_async_copy(a, b, in_sem.at[n]) for n, (a, b) in enumerate(pairs)]
    for c in loads:
        c.start()

    pb[me] = jnp.zeros(pb.shape[1:], BF16)
    eye = (
        lax.broadcasted_iota(jnp.int32, (kb, 128), 0) == lax.broadcasted_iota(jnp.int32, (kb, 128), 1)
    ).astype(BF16)
    aug[...] = jnp.zeros(aug.shape, F32)
    misc[...] = jnp.zeros(misc.shape, F32)
    for c in loads[:5]:
        c.wait()
    aug[patches : patches + 1, 0:ks] = tok_bias_r[...].astype(F32)
    pb[me, 0:kb, 0:ROWS] = dot_nt(eye, aug[...].astype(BF16)).astype(BF16)
    pb[me, 0:ks, 0:patches] = tok_in_r[...]
    pb[me, kb : kb + ks, 0:patches] = tok_out_r[...]
    misc[0:2, 0:shard] = gains_r[...].astype(F32)
    misc[2:4, 0:shard] = shifts_r[...].astype(F32)
    pb[me, 2 * kb : 2 * kb + 16, :] = misc[...].astype(BF16)

    pl.semaphore_wait(barrier, len(others))
    params.start(across=True)

    loads[5].wait()
    misc[...] = jnp.zeros(misc.shape, F32)
    acc[...] = jnp.zeros(acc.shape, F32)

    def pad_dout(i):
        base = i * ROWS
        dout[pl.ds(base, last), :] = d_raw[i, 0:last, :]
        for c in range(0, D, 256):
            misc[0:tail, :] = d_raw[i, last:patches, c : c + 256].astype(F32)
            dout[pl.ds(base + last, 16), c : c + 256] = misc[...].astype(BF16)
        a = jnp.zeros((8, D), F32)
        for b in range(nblk):
            a = a + fold(dout[pl.ds(base + 16 * b, 16), :].astype(F32))
        acc[4] += a

    for i in range(count):
        pad_dout(i)
    dq[me] = dout[0:ROWS, :]

    loads[6].wait()

    def hidden_grad(i):
        r = pl.ds(i * ROWS, ROWS)
        for c in range(0, D, 256):
            dhid[r, c : c + 256] = dot_nt(dout[r, :], w_out[c : c + 256, :])

    for i in range(count):
        hidden_grad(i)

    loads[7].wait()

    def first_norm(i):
        base = i * ROWS
        xf[pl.ds(base + last, 16), :] = jnp.zeros((16, D), F32)
        xf[pl.ds(base, last), :] = x_raw[i, 0:last, :].astype(F32)
        xf[pl.ds(base + last, tail), :] = x_raw[i, last:patches, :].astype(F32)
        for b in range(nblk):
            r = pl.ds(base + 16 * b, 16)
            v = xf[r, :]
            center = v - jnp.mean(v, axis=-1, keepdims=True)
            inv = lax.rsqrt(jnp.mean(center * center, axis=-1, keepdims=True) + 1e-06)
            xh1[r, :] = center * inv
            rs1[r, :] = jnp.broadcast_to(inv, (16, 128))

    for i in range(count):
        first_norm(i)

    for k in (1, 2, 3):
        params.relay(k, across=True)
    for k in range(nc):
        params.from_sib(k)
    dqs.start()
    for c in loads[8:]:
        c.wait()
    full = jnp.zeros((16, D), F32)
    for d in range(n_dp):
        toki_t[d * kb : (d + 1) * kb, :] = pb[d, 0:kb, :]
        toko_t[d * kb : (d + 1) * kb, :] = pb[d, kb : 2 * kb, :]
        part = pb[d, 2 * kb : 2 * kb + 16, 0:128].astype(F32)
        part = jnp.concatenate([part, jnp.zeros((16, D - 128), F32)], axis=1)
        full = full + (pltpu.roll(part, d * shard, 1) if d else part)
    gs[...] = full
    misc[...] = jnp.zeros(misc.shape, F32)
    misc[0:1, 0:patches] = tok_bias_out_r[...].astype(F32).reshape(1, patches)
    bs[0:1, :] = bias_in_r[...].astype(F32).reshape(1, D)
    bs[1:2, :] = bias_out_r[...].astype(F32).reshape(1, D)
    toko_t[K:KA, :] = misc[...].astype(BF16)
    ri = lax.broadcasted_iota(jnp.int32, (ROWS, ROWS), 0)
    ci = lax.broadcasted_iota(jnp.int32, (ROWS, ROWS), 1)
    eye_rows = ((ri == ci) & (ri < patches)).astype(BF16)
    toko[:, 0:KA] = dot_nt(eye_rows, toko_t[:, 0:ROWS]).astype(BF16)

    chunks = []
    at = 0
    for n in z_sizes(count):
        chunks.append((at, n))
        at += n
    steps = len(chunks)
    seam = [c for c in range(steps) if chunks[c][0] == count * last][0]
    d_rows, o_rows = 0, count * last + 32

    def zrows(c):
        return pl.ds(chunks[c][0], chunks[c][1])

    def chunks_of(start, i):
        return [c for c in range(steps) if start + i * last <= chunks[c][0] < start + (i + 1) * last]

    def up_copy(c, r):
        return rcopy(zpart.at[r], zrx.at[r], z_sent.at[0], z_sem.at[0, c], (me, end_peer))

    def mid_copy(c, r):
        return rcopy(zpair.at[r], zrxp.at[r], z_sent.at[1], z_sem.at[1, c], (me, mid_peer))

    def down_copy(c, r):
        return rcopy(ztot.at[r], ztot.at[r], z_sent.at[0], z_sem.at[0, c], (me, mid_end))

    def start_up(some):
        @pl.when(end)
        def _():
            for c in some:
                up_copy(c, zrows(c)).start()

    def zpair_step(c):
        r = zrows(c)
        up_copy(c, r).wait_recv()
        zpair[r, :] = (zpart[r, :].astype(F32) + zrx[r, :].astype(F32)).astype(BF16)
        mid_copy(c, r).start()

    def ztot_step(c):
        r = zrows(c)
        mid_copy(c, r).wait_recv()
        ztot[r, :] = (zpair[r, :].astype(F32) + zrxp[r, :].astype(F32)).astype(BF16)
        down_copy(c, r).start()

    slots = [[c] for c in range(seam)] + [[seam, seam + 1]] + [[c] for c in range(seam + 2, steps)]
    ticks = iter(range(len(slots) + 2))
    totals = set()

    def tick(until=None):
        if until in totals:
            return
        for n in ticks:
            ups = slots[n] if n < len(slots) else []
            downs = slots[n - 2] if n >= 2 else []
            totals.update(downs)

            @pl.when(mid)
            def _():
                for c in ups:
                    zpair_step(c)
                for c in downs:
                    ztot_step(c)

            if until is None or until in downs:
                return

    def zfin(some):
        @pl.when(end)
        def _():
            for c in some:
                down_copy(c, zrows(c)).wait_recv()

    def pack_tails():
        rows = [tails[i, 0:tail, :] for i in range(count)]
        rows.append(jnp.zeros((16 - count * tail, D), F32))
        return jnp.concatenate(rows, axis=0).astype(BF16)

    def forward(i):
        base = i * ROWS
        r = pl.ds(base, ROWS)
        for b in range(nblk):
            rb = pl.ds(base + 16 * b, 16)
            v = xh1[rb, :] * gs[0:1, :] + gs[2:3, :]
            if 16 * (b + 1) > patches:
                row = lax.broadcasted_iota(jnp.int32, (16, D), 0) + 16 * b
                v = jnp.where(row < patches, v, jnp.where(row == patches, 1.0, 0.0))
            normed[rb, :] = v.astype(BF16)
        th[i, K:KA, :] = (lax.broadcasted_iota(jnp.int32, (16, D), 0) == 0).astype(F32).astype(BF16)
        for c in range(0, D, 256):
            tmp[0:K, :] = dot_nn(toki_t[:, 0:ROWS], normed[r, c : c + 256])
            for b in range(0, K, 16):
                value, slope = gelu_pair(tmp[b : b + 16, :])
                th[i, b : b + 16, c : c + 256] = value.astype(BF16)
                tgp[i, b : b + 16, c : c + 256] = slope
            xf[r, c : c + 256] += dot_nn(toko[:, 0:KA], th[i, :, c : c + 256])
        for b in range(nblk):
            rb = pl.ds(base + 16 * b, 16)
            v = xf[rb, :]
            center = v - jnp.mean(v, axis=-1, keepdims=True)
            inv = lax.rsqrt(jnp.mean(center * center, axis=-1, keepdims=True) + 1e-06)
            xhat = center * inv
            xh2[rb, :] = xhat
            rs2[rb, :] = jnp.broadcast_to(inv, (16, 128))
            chan[rb, :] = (xhat * gs[1:2, :] + gs[3:4, :]).astype(BF16)

        if i == 0:
            cq[me] = chan[0:ROWS, :]
            cqs.start()

        for c in range(0, D, 256):
            tmp[0:ROWS, :] = dot_nn(chan[r, :], w_in[:, c : c + 256])
            a = jnp.zeros((8, 256), F32)
            for b in range(nblk):
                rb = pl.ds(base + 16 * b, 16)
                value, slope = gelu_pair(tmp[16 * b : 16 * b + 16, :] + bs[0:1, c : c + 256])
                hid[rb, c : c + 256] = value.astype(BF16)
                low = (slope * dhid[rb, c : c + 256]).astype(BF16)
                dpre[rb, c : c + 256] = low
                a = a + fold(low.astype(F32))
            acc[5, :, c : c + 256] += a
        for c in range(0, D, 256):
            part = dot_nt(dpre[r, :], w_in[c : c + 256, :])
            zpart[pl.ds(i * last, last), c : c + 256] = part[0:last].astype(BF16)
            tails[i, :, c : c + 256] = part[last : last + 8]
        start_up(chunks_of(d_rows, i))


    for i in range(count):
        forward(i)
    tick()

    zpart[zrows(seam), :] = pack_tails()
    start_up([seam])

    def partial_out(i):
        r = pl.ds(i * ROWS, ROWS)
        ro = pl.ds(o_rows + i * last, last)
        for c in range(0, D, 256):
            part = dot_nn(hid[r, :], w_out[:, c : c + 256])
            zpart[ro, c : c + 256] = part[0:last].astype(BF16)
            tails[i, :, c : c + 256] = part[last : last + 8]

    for i in range(count):
        partial_out(i)
    tick()
    zpart[zrows(seam + 1), :] = pack_tails()
    start_up(range(seam + 1, steps))

    def weight_grad(j):
        cols = pl.ds(j * 256, 256)
        gw[0, cols, :] = dot_tn(chan[:, cols], dpre[...])
        gw[1, cols, :] = dot_tn(dout[:, cols], hid[...])

    for j in range(D // 256):
        weight_grad(j)
    for c in range(nc):
        rows = pl.ds(pl.multiple_of((2 * c + 1 - core) * shard, 8), shard)
        for m in range(2):
            wsib_s[c, m] = gw[m, rows, :].astype(BF16)
    w_sib = rcopy(wsib_s, wsib_r, w_sem.at[0, 0], w_sem.at[1, 0], (sib, t))
    w_sib.start()
    tick()

    sqs[...] = jnp.zeros(sqs.shape, F32)

    def square(i):
        r = pl.ds(i * ROWS, ROWS)
        g1 = dot_nt(chan[r, :], chan[r, :]) * dot_nt(dpre[r, :], dpre[r, :])
        g2 = dot_nt(dout[r, :], dout[r, :]) * dot_nt(hid[r, :], hid[r, :])
        sqs[pl.ds(i, 1), 0:ROWS] = jnp.sum(g1 + g2, axis=0, keepdims=True)

    for i in range(count):
        square(i)
    tick()

    w_sib.wait_recv()

    def w_chip(n, k):
        return rcopy(wch_s.at[n], wch_r.at[n], w_sem.at[0, n + 1], w_sem.at[1, n + 1], (peer(k), t))

    def w_share(dest, m):
        rows = pl.ds(pl.multiple_of((2 * dest + core) * shard, 8), shard)
        return gw[m, rows, :] + wsib_r[dest, m].astype(F32)

    first, second = 1 + core, 2 - core

    infl[...] = jnp.zeros(infl.shape, F32)

    def query(j):
        k = j // 2
        if j == 0:
            slot, cin, din, hid_q, pre_q = me, chan, dout, hid, dpre
        else:
            slot = peer_sib(k) if j % 2 else peer(k)
            if j % 2:
                dqs.from_sib(k)
                cqs.from_sib(k)
            cin, din, hid_q, pre_q = cq.at[slot], dq.at[slot], hq, pq
            for c in range(0, D, 256):
                tmp[0:ROWS, :] = dot_nn(cin[...], w_in[:, c : c + 256])
                tmp[ROWS : 2 * ROWS, :] = dot_nt(din[...], w_out[c : c + 256, :])
                for b in range(0, ROWS, 16):
                    value, slope = gelu_pair(tmp[b : b + 16, :] + bs[0:1, c : c + 256])
                    hq[b : b + 16, c : c + 256] = value.astype(BF16)
                    pq[b : b + 16, c : c + 256] = (slope * tmp[ROWS + b : ROWS + b + 16, :]).astype(BF16)
        for q in range(count - QRY_DEV):
            r = slice((QRY_DEV + q) * ROWS, (QRY_DEV + q + 1) * ROWS)
            g1 = dot_nt(cin[0:ROWS, :], chan[r, :]) * dot_nt(pre_q[0:ROWS, :], dpre[r, :])
            g2 = dot_nt(din[0:ROWS, :], dout[r, :]) * dot_nt(hid_q[0:ROWS, :], hid[r, :])
            infl[q, pl.ds(slot, 1), 0:ROWS] = jnp.sum(g1 + g2, axis=0, keepdims=True)

    dqs.relay(1)
    dqs.relay(2)
    query(0)
    tick()
    query(1)
    tick()
    tick()
    cqs.relay(1)
    cqs.relay(2)
    for n, dest in ((0, chip ^ 3), (1, chip ^ first)):
        for m in range(2):
            wch_s[n, m] = w_share(dest, m).astype(BF16)
        w_chip(n, first).start()
    for j in (2, 4, 3, 5):
        query(j)
        tick()
    tick(until=seam)

    gtok[...] = jnp.zeros(gtok.shape, F32)
    toki[:, 0:K] = dot_nt(eye_rows, toki_t[:, 0:ROWS]).astype(BF16)

    def ing_copy(i):
        return pltpu.make_async_copy(ing_s.at[i], ing_o.at[i], out_sem.at[0, i])

    zfin([seam])
    rest = ztot[zrows(seam), :].astype(F32)
    for i in range(count):
        rests[i, 0:tail, :] = rest[tail * i : tail * (i + 1)]
        rests[i, tail:16, :] = jnp.zeros((16 - tail, D), F32)

    def backward(i):
        zfin(chunks_of(d_rows, i))
        base = i * ROWS
        r = pl.ds(base, ROWS)
        a1 = jnp.zeros((8, D), F32)
        a3 = jnp.zeros((8, D), F32)
        for b in range(nblk):
            rb = pl.ds(base + 16 * b, 16)
            if b < nblk - 1:
                e = ztot[pl.ds(i * last + 16 * b, 16), :].astype(F32)
            else:
                e = rests[i]
            xhat = xh2[rb, :]
            a1 = a1 + fold(e * xhat)
            a3 = a3 + fold(e)
            eg = e * gs[1:2, :]
            m1 = jnp.mean(eg, axis=-1, keepdims=True)
            m2 = jnp.mean(eg * xhat, axis=-1, keepdims=True)
            d = dout[rb, :].astype(F32) + rs2[rb, 0:1] * (eg - m1 - xhat * m2)
            dhid[rb, :] = d
            dmix[16 * b : 16 * b + 16, :] = d.astype(BF16)
        acc[1] += a1
        acc[3] += a3
        for c in range(0, D, 256):
            tmp[0:K, :] = dot_nn(toko_t[0:K, 0:ROWS], dmix[:, c : c + 256])
            for b in range(0, K, 16):
                dtok[b : b + 16, c : c + 256] = (
                    tmp[b : b + 16, :] * tgp[i, b : b + 16, c : c + 256]
                ).astype(BF16)
        gtok[0, 0:K, 0:ROWS] += dot_nt(dtok[...], normed[r, :])
        gtok[1, :, 0:ROWS] += dot_nt(th[i], dmix[...])
        for c in range(0, D, 256):
            dnorm[:, c : c + 256] = dot_nn(toki[:, 0:K], dtok[:, c : c + 256])
        a0 = jnp.zeros((8, D), F32)
        a2 = jnp.zeros((8, D), F32)
        for b in range(nblk):
            rb = pl.ds(base + 16 * b, 16)
            e = dnorm[16 * b : 16 * b + 16, :]
            xhat = xh1[rb, :]
            a0 = a0 + fold(e * xhat)
            a2 = a2 + fold(e)
            eg = e * gs[0:1, :]
            m1 = jnp.mean(eg, axis=-1, keepdims=True)
            m2 = jnp.mean(eg * xhat, axis=-1, keepdims=True)
            d = (dhid[rb, :] + rs1[rb, 0:1] * (eg - m1 - xhat * m2)).astype(BF16)
            n = min(16, patches - 16 * b)
            ing_s[i, 16 * b : 16 * b + n, :] = d[0:n]
        acc[0] += a0
        acc[2] += a2
        ing_copy(i).start()
        tick()

    for i in range(count):
        backward(i)
        if i == 0:
            dqs.relay(3)
            cqs.relay(3)
        if i == 1:
            w_chip(0, first).wait_recv()
            for m in range(2):
                wch_s[2, m] = (w_share(chip ^ second, m) + wch_r[0, m].astype(F32)).astype(BF16)
            w_chip(2, second).start()

    for c in range(nc):
        rows = pl.ds(pl.multiple_of((2 * c + 1 - core) * kb, 8), kb)
        for m in range(2):
            tsib_s[c, m] = gtok[m, rows, :]
    t_sib = rcopy(tsib_s, tsib_r, t_sem.at[0, 0], t_sem.at[1, 0], (sib, t))
    t_sib.start()
    vec[...] = jnp.zeros(vec.shape, F32)
    for q in range(6):
        vec[q : q + 1, :] = jnp.sum(acc[q], axis=0, keepdims=True)
    vec[6:7, 0:256] = gtok[1, K : K + 1, :]
    v_sib = rcopy(vec, vsib_r, v_sem.at[0, 0], v_sem.at[1, 0], (sib, t))
    v_sib.start()
    query(6)
    tick()
    v_sib.wait_recv()

    def v_chip(k):
        return rcopy(
            vch.at[chip], vch.at[chip], v_sem.at[0, k], v_sem.at[1, k], (peer(k), t)
        )

    vch[chip] = vec[...] + vsib_r[...]
    for k in range(1, nc):
        v_chip(k).start()
    t_sib.wait_recv()

    def t_chip(k):
        return rcopy(
            tch_s.at[k - 1], tch_r.at[k - 1], t_sem.at[0, k], t_sem.at[1, k], (peer(k), t)
        )

    for k in range(1, nc):
        dest = chip ^ k
        rows = pl.ds(pl.multiple_of((2 * dest + core) * kb, 8), kb)
        for m in range(2):
            tch_s[k - 1, m] = gtok[m, rows, :] + tsib_r[dest, m]
        t_chip(k).start()
    query(7)

    def as_row(values):
        totals = jnp.sum(values, axis=1, keepdims=True)
        at = lax.broadcasted_iota(jnp.int32, (values.shape[0], 128), 0)
        lane = lax.broadcasted_iota(jnp.int32, (values.shape[0], 128), 1)
        return jnp.sum(jnp.where(at == lane, totals, 0.0), axis=0, keepdims=True)

    zsm[t] = jnp.zeros((8, 128), F32)
    zsm[t, 0:1, :] = as_row(sqs[...]) / (2.0 * D * FF)
    for q in range(count - QRY_DEV):
        zsm[t, 1 + q : 2 + q, :] = as_row(infl[q]) * (2.0 * D * FF) ** (-0.5)

    def sm_copy(k):
        return rcopy(
            zsm.at[t], zsm.at[t], s_sem.at[0, k - 1], s_sem.at[1, k - 1], (me, (t + k) % 4)
        )

    for k in (1, 2, 3):
        sm_copy(k).start()

    tick()

    for m, out in enumerate((gwi_k, gwo_k)):
        out[...] = w_share(chip, m)
    for n in (1, 2):
        w_chip(n, first).wait_recv()
        for m, out in enumerate((gwi_k, gwo_k)):
            out[...] += wch_r[n, m].astype(F32)

    def act_copy(i):
        return pltpu.make_async_copy(act_s.at[i], act_o.at[i], out_sem.at[1, i])

    def act_rows(i, lo, hi):
        for b in range(lo, hi, 16):
            ro = slice(o_rows + i * last + b, o_rows + i * last + b + 16)
            a = xf[i * ROWS + b : i * ROWS + b + 16, :] + ztot[ro, :].astype(F32) + bs[1:2, :]
            act_s[i, b : b + 16, :] = a.astype(BF16)

    def act(i):
        *before, final = chunks_of(o_rows, i)
        cut = chunks[final][0] - o_rows - i * last
        tick(before[-1])
        zfin([seam + 1] * (i == 0) + before)
        act_rows(i, 0, cut)
        a = ztot[zrows(seam + 1), :].astype(F32)[tail * i : tail * (i + 1)] + bs[1:2, :]
        a = a + xf[i * ROWS + last : i * ROWS + patches, :]
        act_s[i, last:patches, :] = a.astype(BF16)
        tick(final)
        zfin([final])
        act_rows(i, cut, last)
        act_copy(i).start()

    act(0)
    tick()
    act(1)
    tick()

    for k in (1, 2, 3):
        sm_copy(k).wait_recv()
    sm_k[...] = (zsm[0] + zsm[1]) + (zsm[2] + zsm[3])
    rows = pl.ds(pl.multiple_of(me * kb, 8), kb)
    for m, out in enumerate((gti_k, gto_k)):
        out[...] = gtok[m, rows, :] + tsib_r[chip, m]
    for k in range(1, nc):
        t_chip(k).wait_recv()
        for m, out in enumerate((gti_k, gto_k)):
            out[...] += tch_r[k - 1, m]
    for k in range(1, nc):
        v_chip(k).wait_recv()
    total = vch[0]
    for c in range(1, nc):
        total = total + vch[c]
    tbo_k[...] = total[:, 0:256]
    vec_k[...] = pltpu.roll(total, (D - me * shard) % D, 1)[:, 0:128]
    stores = [(gwi_k, gwi_o), (gwo_k, gwo_o), (gti_k, gti_o), (gto_k, gto_o), (vec_k, vec_o), (tbo_k, tbo_o), (sm_k, sm_o)]
    stores = [pltpu.make_async_copy(a, b, small_sem.at[n]) for n, (a, b) in enumerate(stores)]
    for c in stores:
        c.start()
    act(count - 1)

    params.drain()
    dqs.drain()
    cqs.drain()

    @pl.when(end)
    def _():
        rcopy(zpart, zrx, z_sent.at[0], z_sem.at[0, 0], (me, end_peer)).wait_send()

    @pl.when(mid)
    def _():
        rcopy(zpair, zrxp, z_sent.at[1], z_sem.at[1, 0], (me, mid_peer)).wait_send()
        rcopy(ztot, ztot, z_sent.at[0], z_sem.at[0, 0], (me, mid_end)).wait_send()

    w_sib.wait_send()
    t_sib.wait_send()
    v_sib.wait_send()
    for k in range(1, nc):
        w_chip(k - 1, first).wait_send()
        t_chip(k).wait_send()
        v_chip(k).wait_send()
    for k in (1, 2, 3):
        sm_copy(k).wait_send()
    for c in stores:
        c.wait()
    for i in range(count):
        ing_copy(i).wait()
        act_copy(i).wait()


def finish(shard, ks, patches, count, queries, act, ing, gwi, gwo, gti_h, gto_h, vec_h, tbo_h, sm_h, *refs):
    big, small, refs = refs[:4], refs[4:14], refs[14:]
    held, got, made, sem = refs[:4], refs[4:9], refs[9:19], refs[19]
    pieces = [(n, i) for n in (0, 1) for i in range(count)] + [(2, None), (3, None)]

    def part(ref, i):
        return ref if i is None else ref.at[i]

    loads = [
        pltpu.make_async_copy(a, b, sem.at[0, n])
        for n, (a, b) in enumerate(zip((gti_h, gto_h, vec_h, tbo_h, sm_h), got))
    ]
    moves = []
    for n, i in pieces:
        kept, at = part(held[n], i), len(moves)
        moves.append(
            (
                pltpu.make_async_copy(part((act, ing, gwi, gwo)[n], i), kept, sem.at[1, at]),
                pltpu.make_async_copy(kept, part(big[n], i), sem.at[2, at]),
            )
        )
    for c in loads:
        c.start()
    for load, _ in moves:
        load.start()
    for c in loads:
        c.wait()
    gti, gto, vec, tbo, sm = got
    gains, shifts, gti_o, gto_o, gtb_o, tbo_o, gbi_o, gbo_o, sq_o, infl_o = made
    gains[...] = vec[0:2, 0:shard]
    shifts[...] = vec[2:4, 0:shard]
    gbo_o[...] = vec[4:5, 0:shard]
    gbi_o[...] = vec[5:6, 0:shard]
    gti_o[...] = gti[0:ks, 0:patches]
    gto_o[...] = gto[0:ks, 0:patches]
    tbo_o[...] = tbo[6:7, 0:patches]
    column = gti[0:ks, patches : patches + 1]
    eye = lax.broadcasted_iota(jnp.int32, (ks, ks), 0) == lax.broadcasted_iota(jnp.int32, (ks, ks), 1)
    gtb_o[...] = jnp.sum(jnp.where(eye, column, 0.0), axis=0, keepdims=True)
    sq_o[...] = sm[0:1, 0:count]
    for t in range(infl_o.shape[0]):
        infl_o[t : t + 1, :] = sm[1 + t : 2 + t, 0:queries]
    stores = [pltpu.make_async_copy(a, b, sem.at[3, n]) for n, (a, b) in enumerate(zip(made, small))]
    for c in stores:
        c.start()
    for load, store in moves:
        load.wait()
        store.start()
    for c in stores + [store for _, store in moves]:
        c.wait()


def fused(
    n_dp,
    images,
    cotangent,
    norm_gains,
    norm_shifts,
    tok_in,
    tok_out_t,
    tok_bias_in,
    tok_bias_out,
    w_in,
    bias_in,
    w_out,
    bias_out,
):
    count, patches, width = images.shape
    nc = n_dp // 2
    ks = tok_in.shape[1]
    toks = ks * n_dp
    kb = -(-ks // 16) * 16
    K = n_dp * kb
    KA = K + 16
    KL = -(-KA // 128) * 128
    R = count * ROWS
    zrows, steps = sum(z_sizes(count)), len(z_sizes(count))
    shard = width // n_dp
    hidden = w_in.shape[1]
    anyspace = pl.BlockSpec(memory_space=pl.ANY)
    V = pltpu.VMEM
    dma = lambda *s: pltpu.SemaphoreType.DMA(s)
    scratch = dict(
        gwi_k=V((shard, hidden), F32),
        gwo_k=V((shard, hidden), F32),
        gti_k=V((kb, 256), F32),
        gto_k=V((kb, 256), F32),
        vec_k=V((8, 128), F32),
        tbo_k=V((8, 256), F32),
        sm_k=V((8, 128), F32),
        gains_r=V(norm_gains.shape, BF16),
        shifts_r=V(norm_shifts.shape, BF16),
        tok_in_r=V((ks, patches), BF16),
        tok_out_r=V((ks, patches), BF16),
        tok_bias_r=V(tok_bias_in.shape, BF16),
        tok_bias_out_r=V(tok_bias_out.shape, BF16),
        bias_in_r=V(bias_in.shape, BF16),
        bias_out_r=V(bias_out.shape, BF16),
        x_raw=V((count, patches, D), BF16),
        d_raw=V((count, patches, D), BF16),
        w_in=V((D, hidden), BF16),
        w_out=V((hidden, D), BF16),
        act_s=V((count, patches, D), BF16),
        ing_s=V((count, patches, D), BF16),
        pb=V((n_dp, 2 * kb + 16, 256), BF16),
        aug=V((ROWS, 128), F32),
        misc=V((16, 256), F32),
        toki_t=V((K, 256), BF16),
        toko_t=V((KA, 256), BF16),
        toki=V((ROWS, KL), BF16),
        toko=V((ROWS, KL), BF16),
        gs=V((16, D), F32),
        bs=V((8, D), F32),
        dout=V((R, D), BF16),
        dhid=V((R, hidden), F32),
        xf=V((R, D), F32),
        xh1=V((R, D), F32),
        rs1=V((R, 128), F32),
        xh2=V((R, D), F32),
        rs2=V((R, 128), F32),
        normed=V((R, D), BF16),
        th=V((count, KA, D), BF16),
        tgp=V((count, K, D), F32),
        chan=V((R, D), BF16),
        hid=V((R, hidden), BF16),
        dpre=V((R, hidden), BF16),
        tmp=V((max(K, 2 * ROWS), 256), F32),
        dq=V((n_dp, ROWS, D), BF16),
        cq=V((n_dp, ROWS, D), BF16),
        hq=V((ROWS, hidden), BF16),
        pq=V((ROWS, hidden), BF16),
        infl=V((count - QRY_DEV, n_dp, 256), F32),
        sqs=V((8, 256), F32),
        dmix=V((ROWS, D), BF16),
        dtok=V((K, D), BF16),
        dnorm=V((ROWS, D), F32),
        tails=V((count, 8, D), F32),
        rests=V((count, 16, D), F32),
        zpart=V((zrows, D), BF16),
        zrx=V((zrows, D), BF16),
        zpair=V((zrows, D), BF16),
        zrxp=V((zrows, D), BF16),
        ztot=V((zrows, D), BF16),
        gw=V((2, D, hidden), F32),
        wsib_s=V((nc, 2, shard, hidden), BF16),
        wsib_r=V((nc, 2, shard, hidden), BF16),
        wch_s=V((nc - 1, 2, shard, hidden), BF16),
        wch_r=V((nc - 1, 2, shard, hidden), BF16),
        gtok=V((2, KA, 256), F32),
        tsib_s=V((nc, 2, kb, 256), F32),
        tsib_r=V((nc, 2, kb, 256), F32),
        tch_s=V((nc - 1, 2, kb, 256), F32),
        tch_r=V((nc - 1, 2, kb, 256), F32),
        acc=V((6, 8, D), F32),
        vec=V((8, D), F32),
        vsib_r=V((8, D), F32),
        vch=V((nc, 8, D), F32),
        zsm=V((4, 8, 128), F32),
        in_sem=dma(12),
        out_sem=dma(2, count),
        small_sem=dma(7),
        pb_sem=dma(8),
        dq_sem=dma(8),
        cq_sem=dma(8),
        z_sem=dma(2, steps),
        z_sent=dma(2),
        w_sem=dma(2, nc),
        t_sem=dma(2, nc),
        v_sem=dma(2, nc),
        s_sem=dma(2, 3),
    )
    outs = [
        (images.shape, BF16, anyspace),
        (images.shape, BF16, anyspace),
        ((shard, hidden), F32, anyspace),
        ((shard, hidden), F32, anyspace),
        ((kb, 256), F32, anyspace),
        ((kb, 256), F32, anyspace),
        ((8, 128), F32, anyspace),
        ((8, 256), F32, anyspace),
        ((8, 128), F32, anyspace),
    ]
    names = list(scratch)
    n_in, n_out = 12, len(outs)

    def body(*refs):
        mega(n_dp, count, patches, toks, *refs[: n_in + n_out], **dict(zip(names, refs[n_in + n_out :])))

    act, ing, gwi, gwo, gti, gto, vec, tbo, sm = pl.pallas_call(
        body,
        out_shape=[jax.ShapeDtypeStruct(s, d) for s, d, _ in outs],
        in_specs=[anyspace] * 12,
        out_specs=[o[2] for o in outs],
        scratch_shapes=list(scratch.values()),
        compiler_params=pltpu.CompilerParams(
            collective_id=0, has_side_effects=True, vmem_limit_bytes=60 * 2**20
        ),
        name="mixer",
    )(
        images,
        cotangent,
        w_in,
        w_out,
        norm_gains,
        norm_shifts,
        tok_in.T,
        tok_out_t.T,
        tok_bias_in,
        tok_bias_out,
        bias_in,
        bias_out,
    )
    queries, trains = n_dp * QRY_DEV, count - QRY_DEV
    shapes = [
        (images.shape, BF16),
        (images.shape, BF16),
        ((shard, hidden), F32),
        ((shard, hidden), F32),
        ((2, shard), F32),
        ((2, shard), F32),
        ((ks, patches), F32),
        ((ks, patches), F32),
        ((1, ks), F32),
        ((1, patches), F32),
        ((1, shard), F32),
        ((1, shard), F32),
        ((1, count), F32),
        ((trains, queries), F32),
    ]
    smalls = [(o.shape, F32) for o in (gti, gto, vec, tbo, sm)]
    out = pl.pallas_call(
        functools.partial(finish, shard, ks, patches, count, queries),
        out_shape=[jax.ShapeDtypeStruct(s, d) for s, d in shapes],
        in_specs=[anyspace] * 9,
        out_specs=[anyspace] * 14,
        scratch_shapes=[V(s, d) for s, d in shapes[:4] + smalls + shapes[4:]] + [dma(4, 10)],
        name="finish",
    )(act, ing, gwi, gwo, gti, gto, vec, tbo, sm)
    act, ing, gwi, gwo, gains, shifts, gti, gto, gtb, tbo, gbi, gbo, squares, influence = out
    return (
        act,
        ing,
        gains,
        shifts,
        gti.T,
        gto.T,
        gtb,
        tbo.reshape(patches),
        gwi,
        gbi.reshape(shard),
        gwo.T,
        gbo.reshape(shard),
        squares.reshape(count),
        influence.T,
    )


def layer_norm(values, gain, shift):
    center = values - jnp.mean(values, axis=-1, keepdims=True)
    spread = jnp.mean(center * center, axis=-1, keepdims=True)
    return center * lax.rsqrt(spread + 1e-06) * gain + shift


def smooth(values):
    return jax.nn.gelu(values, approximate=True)


def contract(left, right, left_dim, right_dim):
    return lax.dot_general(
        left, right, (((left_dim,), (right_dim,)), ((), ())), preferred_element_type=jnp.float32
    )


def per_device(
    images,
    cotangent,
    norm_gains,
    norm_shifts,
    tok_in,
    tok_out_t,
    tok_bias_in,
    tok_bias_out,
    w_in,
    bias_in,
    w_out,
    bias_out,
):
    gains, shifts, tok_first, tok_second, tok_bias = (
        lax.all_gather(norm_gains, "dp", axis=1, tiled=True),
        lax.all_gather(norm_shifts, "dp", axis=1, tiled=True),
        lax.all_gather(tok_in, "dp", axis=1, tiled=True),
        lax.all_gather(tok_out_t, "dp", axis=1, tiled=True),
        lax.all_gather(tok_bias_in, "dp", axis=1, tiled=True),
    )
    gains = gains.astype(jnp.float32)
    shifts = shifts.astype(jnp.float32)
    count, patches, width = images.shape
    rows = count * patches
    inputs = images.astype(jnp.float32)
    normed_one, first_back = jax.vjp(layer_norm, inputs, gains[0], shifts[0])
    normed_low = normed_one.astype(jnp.bfloat16)
    tok_pre = (
        jnp.einsum("sk,nsd->nkd", tok_first, normed_low, preferred_element_type=jnp.float32)
        + tok_bias[0].astype(jnp.float32)[None, :, None]
    )
    tok_hidden = smooth(tok_pre).astype(jnp.bfloat16)
    tok_mixed = (
        jnp.einsum("sk,nkd->nsd", tok_second, tok_hidden, preferred_element_type=jnp.float32)
        + tok_bias_out.astype(jnp.float32)[None, :, None]
    )
    resid = inputs + tok_mixed
    normed_two, second_back = jax.vjp(layer_norm, resid, gains[1], shifts[1])
    chan_in = normed_two.astype(jnp.bfloat16).reshape(rows, width)
    chan_pre = jnp.dot(chan_in, w_in, preferred_element_type=jnp.float32) + bias_in.astype(
        jnp.float32
    )
    hidden = smooth(chan_pre).astype(jnp.bfloat16)
    partial_out = jnp.dot(hidden, w_out, preferred_element_type=jnp.float32)
    mixed = lax.psum(partial_out, "tensor")
    activations = (
        resid + mixed.reshape(count, patches, width) + bias_out.astype(jnp.float32)
    ).astype(jnp.bfloat16)
    dout_rows = cotangent.reshape(rows, width)
    d_hidden = contract(dout_rows, w_out, 1, 1)
    smooth_value, smooth_back = jax.vjp(smooth, chan_pre)
    d_pre = smooth_back(d_hidden)[0].astype(jnp.bfloat16)
    d_chan_part = contract(d_pre, w_in, 1, 1)
    d_chan = lax.psum(d_chan_part, "tensor")
    d_resid_norm, d_gain_two, d_shift_two = second_back(d_chan.reshape(count, patches, width))
    d_resid = cotangent.astype(jnp.float32) + d_resid_norm
    d_mixed = d_resid.astype(jnp.bfloat16)
    d_tokhid = jnp.einsum("sk,nsd->nkd", tok_second, d_mixed, preferred_element_type=jnp.float32)
    tok_value, tok_back = jax.vjp(smooth, tok_pre)
    d_tokpre = tok_back(d_tokhid)[0].astype(jnp.bfloat16)
    grad_second = jnp.einsum("nsd,nkd->sk", d_mixed, tok_hidden, preferred_element_type=jnp.float32)
    grad_first = jnp.einsum("nsd,nkd->sk", normed_low, d_tokpre, preferred_element_type=jnp.float32)
    grad_tbias = jnp.sum(d_tokpre, axis=(0, 2), dtype=jnp.float32)[None, :]
    grad_tbias_out = jnp.sum(d_mixed, axis=(0, 2), dtype=jnp.float32)
    d_normed = jnp.einsum("sk,nkd->nsd", tok_first, d_tokpre, preferred_element_type=jnp.float32)
    d_input_norm, d_gain_one, d_shift_one = first_back(d_normed)
    input_grad = (d_resid + d_input_norm).astype(jnp.bfloat16)
    grad_win = contract(chan_in, d_pre, 0, 0)
    grad_wout_t = contract(dout_rows, hidden, 0, 0)
    grad_bin = jnp.sum(d_pre, axis=0, dtype=jnp.float32)
    grad_bout = jnp.sum(dout_rows, axis=0, dtype=jnp.float32)
    share_win, share_wout_t, share_bin, share_bout = (
        lax.psum_scatter(grad_win, "dp", scatter_dimension=0, tiled=True),
        lax.psum_scatter(grad_wout_t, "dp", scatter_dimension=0, tiled=True),
        lax.psum_scatter(grad_bin, "dp", scatter_dimension=0, tiled=True),
        lax.psum_scatter(grad_bout, "dp", scatter_dimension=0, tiled=True),
    )
    share_gains, share_shifts, share_first, share_second, share_tbias = (
        lax.psum_scatter(
            jnp.stack([d_gain_one, d_gain_two]), "dp", scatter_dimension=1, tiled=True
        ),
        lax.psum_scatter(
            jnp.stack([d_shift_one, d_shift_two]), "dp", scatter_dimension=1, tiled=True
        ),
        lax.psum_scatter(grad_first, "dp", scatter_dimension=1, tiled=True),
        lax.psum_scatter(grad_second, "dp", scatter_dimension=1, tiled=True),
        lax.psum_scatter(grad_tbias, "dp", scatter_dimension=1, tiled=True),
    )
    total_tbias_out = lax.psum(grad_tbias_out, "dp")
    chan_cube = chan_in.reshape(count, patches, width)
    pre_cube = d_pre.reshape(count, patches, -1)
    hidden_cube = hidden.reshape(count, patches, -1)
    def against(chan, pre, dout, low):
        grams = [
            jnp.einsum("sd,npd->nsp", a, b, preferred_element_type=jnp.float32)
            for a, b in ((chan, chan_cube), (pre, pre_cube), (dout, cotangent), (low, hidden_cube))
        ]
        return jnp.sum(grams[0] * grams[1] + grams[2] * grams[3], axis=(1, 2))

    own = lax.map(lambda a: against(*a), (chan_cube, pre_cube, cotangent, hidden_cube))
    squares = jnp.diagonal(own)
    queries = tuple(
        lax.all_gather(a[:QRY_DEV], "dp", axis=0, tiled=True)
        for a in (chan_cube, pre_cube, cotangent, hidden_cube)
    )
    influence = lax.map(lambda a: against(*a), queries)[:, QRY_DEV:]
    influence, squares = lax.psum((influence, squares), "tensor")
    sqnorms = squares / (2.0 * D * FF)
    influence = influence * (2.0 * D * FF) ** (-0.5)
    return (
        activations,
        input_grad,
        share_gains,
        share_shifts,
        share_first,
        share_second,
        share_tbias,
        total_tbias_out,
        share_win,
        share_bin,
        share_wout_t.T,
        share_bout,
        sqnorms,
        influence,
    )


def solution(mesh):
    placed = (
        P("dp", None, None),
        P("dp", None, None),
        P(None, "dp"),
        P(None, "dp"),
        P(None, "dp"),
        P(None, "dp"),
        P(None, "dp"),
        P(),
        P(None, "tensor"),
        P("tensor"),
        P("tensor", None),
        P(),
    )
    n_dp = mesh.shape["dp"]
    fits = n_dp == 8 and mesh.shape["tensor"] == 4
    device = functools.partial(fused, n_dp) if fits else per_device
    return jax.shard_map(
        device,
        mesh=mesh,
        in_specs=placed,
        out_specs=(
            P("dp", None, None),
            P("dp", None, None),
            P(None, "dp"),
            P(None, "dp"),
            P(None, "dp"),
            P(None, "dp"),
            P(None, "dp"),
            P(),
            P("dp", "tensor"),
            P(("tensor", "dp")),
            P("tensor", "dp"),
            P("dp"),
            P("dp"),
            P(None, "dp"),
        ),
        check_vma=False,
    )
```

```python
import functools

import jax
import jax.numpy as jnp
from jax import lax
from jax.experimental import pallas as pl
from jax.experimental.pallas import tpu as pltpu
from jax.sharding import PartitionSpec as P

D = 768
FF = 3072
QRY_DEV = 1
HIGH = lax.Precision.HIGHEST
MESH = pl.DeviceIdType.MESH
F32 = jnp.float32
BF16 = jnp.bfloat16

ROWS = 208
C1 = 0.7978845608028654
C2 = 0.044715


def dot_nn(a, b):
    return lax.dot_general(a, b, (((1,), (0,)), ((), ())), preferred_element_type=F32)


def dot_nt(a, b):
    return lax.dot_general(a, b, (((1,), (1,)), ((), ())), preferred_element_type=F32)


def dot_tn(a, b):
    return lax.dot_general(a, b, (((0,), (0,)), ((), ())), preferred_element_type=F32)


def gelu_pair(v):
    u = v * v
    th = jnp.tanh(v * (C1 + (C1 * C2) * u))
    hp = 0.5 + 0.5 * th
    value = v * hp
    slope = hp + (0.5 * v) * (1.0 - th * th) * (C1 + (3.0 * C1 * C2) * u)
    return value, slope


def z_sizes(count):
    full = [64] * (3 * count)
    return full + [16, 16] + full


def fold(v):
    out = v[0:8]
    for s in range(8, v.shape[0], 8):
        out = out + v[s : s + 8]
    return out


def mega(
    n_dp,
    count,
    patches,
    toks,
    images,
    cotangent,
    w_in_h,
    w_out_h,
    gains_h,
    shifts_h,
    tok_in_h,
    tok_out_h,
    tok_bias_h,
    tok_bias_out_h,
    bias_in_h,
    bias_out_h,
    act_o,
    ing_o,
    gwi_o,
    gwo_o,
    gti_o,
    gto_o,
    vec_o,
    tbo_o,
    sm_o,
    gwi_k,
    gwo_k,
    gti_k,
    gto_k,
    vec_k,
    tbo_k,
    sm_k,
    gains_r,
    shifts_r,
    tok_in_r,
    tok_out_r,
    tok_bias_r,
    tok_bias_out_r,
    bias_in_r,
    bias_out_r,
    x_raw,
    d_raw,
    w_in,
    w_out,
    act_s,
    ing_s,
    pb,
    aug,
    misc,
    toki_t,
    toko_t,
    toki,
    toko,
    gs,
    bs,
    dout,
    dhid,
    xf,
    xh1,
    rs1,
    xh2,
    rs2,
    normed,
    th,
    tgp,
    chan,
    hid,
    dpre,
    tmp,
    dq,
    cq,
    hq,
    pq,
    infl,
    sqs,
    dmix,
    dtok,
    dnorm,
    tails,
    rests,
    zpart,
    zrx,
    zpair,
    zrxp,
    ztot,
    gw,
    wsib_s,
    wsib_r,
    wch_s,
    wch_r,
    gtok,
    tsib_s,
    tsib_r,
    tch_s,
    tch_r,
    acc,
    vec,
    vsib_r,
    vch,
    zsm,
    in_sem,
    out_sem,
    small_sem,
    pb_sem,
    dq_sem,
    cq_sem,
    z_sem,
    z_sent,
    w_sem,
    t_sem,
    v_sem,
    s_sem,
):
    me = lax.axis_index("dp")
    t = lax.axis_index("tensor")
    core = me % 2
    chip = me // 2
    sib = chip * 2 + 1 - core
    nc = n_dp // 2
    mid = (t == 1) | (t == 2)
    end = (t == 0) | (t == 3)
    end_peer = jnp.where(t < 2, 1, 2)
    mid_end = jnp.where(t < 2, 0, 3)
    mid_peer = 3 - t
    shard = D // n_dp
    ks = toks // n_dp
    kb = -(-ks // 16) * 16
    K = n_dp * kb
    KA = K + 16
    R = count * ROWS
    nblk = ROWS // 16
    last = ROWS - 16
    tail = patches - last

    def peer(k):
        return (chip ^ k) * 2 + core

    def peer_sib(k):
        return (chip ^ k) * 2 + 1 - core

    def rcopy(a, b, ss, rs, dev):
        return pltpu.make_async_remote_copy(
            src_ref=a, dst_ref=b, send_sem=ss, recv_sem=rs, device_id=dev, device_id_type=MESH
        )

    class Gather:
        def __init__(self, buf, sem):
            self.buf, self.sem = buf, sem

        def chip_copy(self, block, k, n):
            b = self.buf.at[block]
            return rcopy(b, b, self.sem.at[0], self.sem.at[1 + n], (peer(k), t))

        def sib_copy(self, k):
            b = self.buf.at[peer(k)]
            return rcopy(b, b, self.sem.at[0], self.sem.at[4 + k], (sib, t))

        def start(self, across=False):
            for k in (1, 2, 3) if across else (1, 2):
                self.chip_copy(me, k, k - 1).start()
            self.sib_copy(0).start()

        def relay(self, k, across=False):
            self.chip_copy(peer(k), k, k - 1).wait_recv()
            if k < 3 and not across:

                @pl.when(core == k - 1)
                def _():
                    self.chip_copy(peer(k), 3 - k, 2).start()

            self.sib_copy(k).start()

        def from_sib(self, k):
            b = self.buf.at[peer_sib(k)]
            rcopy(b, b, self.sem.at[0], self.sem.at[4 + k], (sib, t)).wait_recv()

        def drain(self):
            b = self.buf.at[pl.ds(0, 7)]
            rcopy(b, b, self.sem.at[0], self.sem.at[1], (sib, t)).wait_send()

    params, dqs, cqs = Gather(pb, pb_sem), Gather(dq, dq_sem), Gather(cq, cq_sem)

    barrier = pltpu.get_barrier_semaphore()
    others = [(sib, t)] + [(peer(k), t) for k in range(1, nc)] + [(me, (t + k) % 4) for k in (1, 2, 3)]
    for dev in others:
        pl.semaphore_signal(barrier, inc=1, device_id=dev, device_id_type=MESH)

    pairs = [
        (gains_h, gains_r),
        (shifts_h, shifts_r),
        (tok_in_h, tok_in_r),
        (tok_out_h, tok_out_r),
        (tok_bias_h, tok_bias_r),
        (cotangent, d_raw),
        (w_out_h, w_out),
        (images, x_raw),
        (w_in_h, w_in),
        (tok_bias_out_h, tok_bias_out_r),
        (bias_in_h, bias_in_r),
        (bias_out_h, bias_out_r),
    ]
    loads = [pltpu.make_async_copy(a, b, in_sem.at[n]) for n, (a, b) in enumerate(pairs)]
    for c in loads:
        c.start()

    pb[me] = jnp.zeros(pb.shape[1:], BF16)
    eye = (
        lax.broadcasted_iota(jnp.int32, (kb, 128), 0) == lax.broadcasted_iota(jnp.int32, (kb, 128), 1)
    ).astype(BF16)
    aug[...] = jnp.zeros(aug.shape, F32)
    misc[...] = jnp.zeros(misc.shape, F32)
    for c in loads[:5]:
        c.wait()
    aug[patches : patches + 1, 0:ks] = tok_bias_r[...].astype(F32)
    pb[me, 0:kb, 0:ROWS] = dot_nt(eye, aug[...].astype(BF16)).astype(BF16)
    pb[me, 0:ks, 0:patches] = tok_in_r[...]
    pb[me, kb : kb + ks, 0:patches] = tok_out_r[...]
    misc[0:2, 0:shard] = gains_r[...].astype(F32)
    misc[2:4, 0:shard] = shifts_r[...].astype(F32)
    pb[me, 2 * kb : 2 * kb + 16, :] = misc[...].astype(BF16)

    pl.semaphore_wait(barrier, len(others))
    params.start(across=True)

    loads[5].wait()
    misc[...] = jnp.zeros(misc.shape, F32)
    acc[...] = jnp.zeros(acc.shape, F32)

    def pad_dout(i):
        base = i * ROWS
        dout[pl.ds(base, last), :] = d_raw[i, 0:last, :]
        for c in range(0, D, 256):
            misc[0:tail, :] = d_raw[i, last:patches, c : c + 256].astype(F32)
            dout[pl.ds(base + last, 16), c : c + 256] = misc[...].astype(BF16)
        a = jnp.zeros((8, D), F32)
        for b in range(nblk):
            a = a + fold(dout[pl.ds(base + 16 * b, 16), :].astype(F32))
        acc[4] += a

    for i in range(count):
        pad_dout(i)
    dq[me] = dout[0:ROWS, :]

    loads[6].wait()

    def hidden_grad(i):
        r = pl.ds(i * ROWS, ROWS)
        for c in range(0, D, 256):
            dhid[r, c : c + 256] = dot_nt(dout[r, :], w_out[c : c + 256, :])

    for i in range(count):
        hidden_grad(i)

    loads[7].wait()

    def first_norm(i):
        base = i * ROWS
        xf[pl.ds(base + last, 16), :] = jnp.zeros((16, D), F32)
        xf[pl.ds(base, last), :] = x_raw[i, 0:last, :].astype(F32)
        xf[pl.ds(base + last, tail), :] = x_raw[i, last:patches, :].astype(F32)
        for b in range(nblk):
            r = pl.ds(base + 16 * b, 16)
            v = xf[r, :]
            center = v - jnp.mean(v, axis=-1, keepdims=True)
            inv = lax.rsqrt(jnp.mean(center * center, axis=-1, keepdims=True) + 1e-06)
            xh1[r, :] = center * inv
            rs1[r, :] = jnp.broadcast_to(inv, (16, 128))

    for i in range(count):
        first_norm(i)

    for k in (1, 2, 3):
        params.relay(k, across=True)
    for k in range(nc):
        params.from_sib(k)
    dqs.start()
    for c in loads[8:]:
        c.wait()
    full = jnp.zeros((16, D), F32)
    for d in range(n_dp):
        toki_t[d * kb : (d + 1) * kb, :] = pb[d, 0:kb, :]
        toko_t[d * kb : (d + 1) * kb, :] = pb[d, kb : 2 * kb, :]
        part = pb[d, 2 * kb : 2 * kb + 16, 0:128].astype(F32)
        part = jnp.concatenate([part, jnp.zeros((16, D - 128), F32)], axis=1)
        full = full + (pltpu.roll(part, d * shard, 1) if d else part)
    gs[...] = full
    misc[...] = jnp.zeros(misc.shape, F32)
    misc[0:1, 0:patches] = tok_bias_out_r[...].astype(F32).reshape(1, patches)
    bs[0:1, :] = bias_in_r[...].astype(F32).reshape(1, D)
    bs[1:2, :] = bias_out_r[...].astype(F32).reshape(1, D)
    toko_t[K:KA, :] = misc[...].astype(BF16)
    ri = lax.broadcasted_iota(jnp.int32, (ROWS, ROWS), 0)
    ci = lax.broadcasted_iota(jnp.int32, (ROWS, ROWS), 1)
    eye_rows = ((ri == ci) & (ri < patches)).astype(BF16)
    toko[:, 0:KA] = dot_nt(eye_rows, toko_t[:, 0:ROWS]).astype(BF16)

    chunks = []
    at = 0
    for n in z_sizes(count):
        chunks.append((at, n))
        at += n
    steps = len(chunks)
    seam = [c for c in range(steps) if chunks[c][0] == count * last][0]
    d_rows, o_rows = 0, count * last + 32

    def zrows(c):
        return pl.ds(chunks[c][0], chunks[c][1])

    def chunks_of(start, i):
        return [c for c in range(steps) if start + i * last <= chunks[c][0] < start + (i + 1) * last]

    def up_copy(c, r):
        return rcopy(zpart.at[r], zrx.at[r], z_sent.at[0], z_sem.at[0, c], (me, end_peer))

    def mid_copy(c, r):
        return rcopy(zpair.at[r], zrxp.at[r], z_sent.at[1], z_sem.at[1, c], (me, mid_peer))

    def down_copy(c, r):
        return rcopy(ztot.at[r], ztot.at[r], z_sent.at[0], z_sem.at[0, c], (me, mid_end))

    def start_up(some):
        @pl.when(end)
        def _():
            for c in some:
                up_copy(c, zrows(c)).start()

    def zpair_step(c):
        r = zrows(c)
        up_copy(c, r).wait_recv()
        zpair[r, :] = (zpart[r, :].astype(F32) + zrx[r, :].astype(F32)).astype(BF16)
        mid_copy(c, r).start()

    def ztot_step(c):
        r = zrows(c)
        mid_copy(c, r).wait_recv()
        ztot[r, :] = (zpair[r, :].astype(F32) + zrxp[r, :].astype(F32)).astype(BF16)
        down_copy(c, r).start()

    slots = [[c] for c in range(seam)] + [[seam, seam + 1]] + [[c] for c in range(seam + 2, steps)]
    ticks = iter(range(len(slots) + 2))
    totals = set()

    def tick(until=None):
        if until in totals:
            return
        for n in ticks:
            ups = slots[n] if n < len(slots) else []
            downs = slots[n - 2] if n >= 2 else []
            totals.update(downs)

            @pl.when(mid)
            def _():
                for c in ups:
                    zpair_step(c)
                for c in downs:
                    ztot_step(c)

            if until is None or until in downs:
                return

    def zfin(some):
        @pl.when(end)
        def _():
            for c in some:
                down_copy(c, zrows(c)).wait_recv()

    def pack_tails():
        rows = [tails[i, 0:tail, :] for i in range(count)]
        rows.append(jnp.zeros((16 - count * tail, D), F32))
        return jnp.concatenate(rows, axis=0).astype(BF16)

    def forward(i):
        base = i * ROWS
        r = pl.ds(base, ROWS)
        for b in range(nblk):
            rb = pl.ds(base + 16 * b, 16)
            v = xh1[rb, :] * gs[0:1, :] + gs[2:3, :]
            if 16 * (b + 1) > patches:
                row = lax.broadcasted_iota(jnp.int32, (16, D), 0) + 16 * b
                v = jnp.where(row < patches, v, jnp.where(row == patches, 1.0, 0.0))
            normed[rb, :] = v.astype(BF16)
        th[i, K:KA, :] = (lax.broadcasted_iota(jnp.int32, (16, D), 0) == 0).astype(F32).astype(BF16)
        for c in range(0, D, 256):
            tmp[0:K, :] = dot_nn(toki_t[:, 0:ROWS], normed[r, c : c + 256])
            for b in range(0, K, 16):
                value, slope = gelu_pair(tmp[b : b + 16, :])
                th[i, b : b + 16, c : c + 256] = value.astype(BF16)
                tgp[i, b : b + 16, c : c + 256] = slope
            xf[r, c : c + 256] += dot_nn(toko[:, 0:KA], th[i, :, c : c + 256])
        for b in range(nblk):
            rb = pl.ds(base + 16 * b, 16)
            v = xf[rb, :]
            center = v - jnp.mean(v, axis=-1, keepdims=True)
            inv = lax.rsqrt(jnp.mean(center * center, axis=-1, keepdims=True) + 1e-06)
            xhat = center * inv
            xh2[rb, :] = xhat
            rs2[rb, :] = jnp.broadcast_to(inv, (16, 128))
            chan[rb, :] = (xhat * gs[1:2, :] + gs[3:4, :]).astype(BF16)

        if i == 0:
            cq[me] = chan[0:ROWS, :]
            cqs.start()

        for c in range(0, D, 256):
            tmp[0:ROWS, :] = dot_nn(chan[r, :], w_in[:, c : c + 256])
            a = jnp.zeros((8, 256), F32)
            for b in range(nblk):
                rb = pl.ds(base + 16 * b, 16)
                value, slope = gelu_pair(tmp[16 * b : 16 * b + 16, :] + bs[0:1, c : c + 256])
                hid[rb, c : c + 256] = value.astype(BF16)
                low = (slope * dhid[rb, c : c + 256]).astype(BF16)
                dpre[rb, c : c + 256] = low
                a = a + fold(low.astype(F32))
            acc[5, :, c : c + 256] += a
        for c in range(0, D, 256):
            part = dot_nt(dpre[r, :], w_in[c : c + 256, :])
            zpart[pl.ds(i * last, last), c : c + 256] = part[0:last].astype(BF16)
            tails[i, :, c : c + 256] = part[last : last + 8]
        start_up(chunks_of(d_rows, i))


    for i in range(count):
        forward(i)
    tick()

    zpart[zrows(seam), :] = pack_tails()
    start_up([seam])

    def partial_out(i):
        r = pl.ds(i * ROWS, ROWS)
        ro = pl.ds(o_rows + i * last, last)
        for c in range(0, D, 256):
            part = dot_nn(hid[r, :], w_out[:, c : c + 256])
            zpart[ro, c : c + 256] = part[0:last].astype(BF16)
            tails[i, :, c : c + 256] = part[last : last + 8]

    for i in range(count):
        partial_out(i)
    tick()
    zpart[zrows(seam + 1), :] = pack_tails()
    start_up(range(seam + 1, steps))

    def weight_grad(j):
        cols = pl.ds(j * 256, 256)
        gw[0, cols, :] = dot_tn(chan[:, cols], dpre[...])
        gw[1, cols, :] = dot_tn(dout[:, cols], hid[...])

    for j in range(D // 256):
        weight_grad(j)
    for c in range(nc):
        rows = pl.ds(pl.multiple_of((2 * c + 1 - core) * shard, 8), shard)
        for m in range(2):
            wsib_s[c, m] = gw[m, rows, :].astype(BF16)
    w_sib = rcopy(wsib_s, wsib_r, w_sem.at[0, 0], w_sem.at[1, 0], (sib, t))
    w_sib.start()
    tick()

    sqs[...] = jnp.zeros(sqs.shape, F32)

    def square(i):
        r = pl.ds(i * ROWS, ROWS)
        g1 = dot_nt(chan[r, :], chan[r, :]) * dot_nt(dpre[r, :], dpre[r, :])
        g2 = dot_nt(dout[r, :], dout[r, :]) * dot_nt(hid[r, :], hid[r, :])
        sqs[pl.ds(i, 1), 0:ROWS] = jnp.sum(g1 + g2, axis=0, keepdims=True)

    for i in range(count):
        square(i)
    tick()

    w_sib.wait_recv()

    def w_chip(n, k):
        return rcopy(wch_s.at[n], wch_r.at[n], w_sem.at[0, n + 1], w_sem.at[1, n + 1], (peer(k), t))

    def w_share(dest, m):
        rows = pl.ds(pl.multiple_of((2 * dest + core) * shard, 8), shard)
        return gw[m, rows, :] + wsib_r[dest, m].astype(F32)

    first, second = 1 + core, 2 - core

    infl[...] = jnp.zeros(infl.shape, F32)

    def query(j):
        k = j // 2
        if j == 0:
            slot, cin, din, hid_q, pre_q = me, chan, dout, hid, dpre
        else:
            slot = peer_sib(k) if j % 2 else peer(k)
            if j % 2:
                dqs.from_sib(k)
                cqs.from_sib(k)
            cin, din, hid_q, pre_q = cq.at[slot], dq.at[slot], hq, pq
            for c in range(0, D, 256):
                tmp[0:ROWS, :] = dot_nn(cin[...], w_in[:, c : c + 256])
                tmp[ROWS : 2 * ROWS, :] = dot_nt(din[...], w_out[c : c + 256, :])
                for b in range(0, ROWS, 16):
                    value, slope = gelu_pair(tmp[b : b + 16, :] + bs[0:1, c : c + 256])
                    hq[b : b + 16, c : c + 256] = value.astype(BF16)
                    pq[b : b + 16, c : c + 256] = (slope * tmp[ROWS + b : ROWS + b + 16, :]).astype(BF16)
        for q in range(count - QRY_DEV):
            r = slice((QRY_DEV + q) * ROWS, (QRY_DEV + q + 1) * ROWS)
            g1 = dot_nt(cin[0:ROWS, :], chan[r, :]) * dot_nt(pre_q[0:ROWS, :], dpre[r, :])
            g2 = dot_nt(din[0:ROWS, :], dout[r, :]) * dot_nt(hid_q[0:ROWS, :], hid[r, :])
            infl[q, pl.ds(slot, 1), 0:ROWS] = jnp.sum(g1 + g2, axis=0, keepdims=True)

    dqs.relay(1)
    dqs.relay(2)
    query(0)
    tick()
    query(1)
    tick()
    tick()
    cqs.relay(1)
    cqs.relay(2)
    for n, dest in ((0, chip ^ 3), (1, chip ^ first)):
        for m in range(2):
            wch_s[n, m] = w_share(dest, m).astype(BF16)
        w_chip(n, first).start()
    for j in (2, 4, 3, 5):
        query(j)
        tick()
    tick(until=seam)

    gtok[...] = jnp.zeros(gtok.shape, F32)
    toki[:, 0:K] = dot_nt(eye_rows, toki_t[:, 0:ROWS]).astype(BF16)

    def ing_copy(i):
        return pltpu.make_async_copy(ing_s.at[i], ing_o.at[i], out_sem.at[0])

    zfin([seam])
    rest = ztot[zrows(seam), :].astype(F32)
    for i in range(count):
        rests[i, 0:tail, :] = rest[tail * i : tail * (i + 1)]
        rests[i, tail:16, :] = jnp.zeros((16 - tail, D), F32)

    def backward(i):
        zfin(chunks_of(d_rows, i))
        base = i * ROWS
        r = pl.ds(base, ROWS)
        a1 = jnp.zeros((8, D), F32)
        a3 = jnp.zeros((8, D), F32)
        for b in range(nblk):
            rb = pl.ds(base + 16 * b, 16)
            if b < nblk - 1:
                e = ztot[pl.ds(i * last + 16 * b, 16), :].astype(F32)
            else:
                e = rests[i]
            xhat = xh2[rb, :]
            a1 = a1 + fold(e * xhat)
            a3 = a3 + fold(e)
            eg = e * gs[1:2, :]
            m1 = jnp.mean(eg, axis=-1, keepdims=True)
            m2 = jnp.mean(eg * xhat, axis=-1, keepdims=True)
            d = dout[rb, :].astype(F32) + rs2[rb, 0:1] * (eg - m1 - xhat * m2)
            dhid[rb, :] = d
            dmix[16 * b : 16 * b + 16, :] = d.astype(BF16)
        acc[1] += a1
        acc[3] += a3
        for c in range(0, D, 256):
            tmp[0:K, :] = dot_nn(toko_t[0:K, 0:ROWS], dmix[:, c : c + 256])
            for b in range(0, K, 16):
                dtok[b : b + 16, c : c + 256] = (
                    tmp[b : b + 16, :] * tgp[i, b : b + 16, c : c + 256]
                ).astype(BF16)
        gtok[0, 0:K, 0:ROWS] += dot_nt(dtok[...], normed[r, :])
        gtok[1, :, 0:ROWS] += dot_nt(th[i], dmix[...])
        for c in range(0, D, 256):
            dnorm[:, c : c + 256] = dot_nn(toki[:, 0:K], dtok[:, c : c + 256])
        a0 = jnp.zeros((8, D), F32)
        a2 = jnp.zeros((8, D), F32)
        for b in range(nblk):
            rb = pl.ds(base + 16 * b, 16)
            e = dnorm[16 * b : 16 * b + 16, :]
            xhat = xh1[rb, :]
            a0 = a0 + fold(e * xhat)
            a2 = a2 + fold(e)
            eg = e * gs[0:1, :]
            m1 = jnp.mean(eg, axis=-1, keepdims=True)
            m2 = jnp.mean(eg * xhat, axis=-1, keepdims=True)
            d = (dhid[rb, :] + rs1[rb, 0:1] * (eg - m1 - xhat * m2)).astype(BF16)
            n = min(16, patches - 16 * b)
            ing_s[i, 16 * b : 16 * b + n, :] = d[0:n]
        acc[0] += a0
        acc[2] += a2
        ing_copy(i).start()
        tick()

    for i in range(count):
        backward(i)
        if i == 0:
            dqs.relay(3)
            cqs.relay(3)
        if i == 1:
            w_chip(0, first).wait_recv()
            for m in range(2):
                wch_s[2, m] = (w_share(chip ^ second, m) + wch_r[0, m].astype(F32)).astype(BF16)
            w_chip(2, second).start()

    for c in range(nc):
        rows = pl.ds(pl.multiple_of((2 * c + 1 - core) * kb, 8), kb)
        for m in range(2):
            tsib_s[c, m] = gtok[m, rows, :]
    t_sib = rcopy(tsib_s, tsib_r, t_sem.at[0, 0], t_sem.at[1, 0], (sib, t))
    t_sib.start()
    vec[...] = jnp.zeros(vec.shape, F32)
    for q in range(6):
        vec[q : q + 1, :] = jnp.sum(acc[q], axis=0, keepdims=True)
    vec[6:7, 0:256] = gtok[1, K : K + 1, :]
    v_sib = rcopy(vec, vsib_r, v_sem.at[0, 0], v_sem.at[1, 0], (sib, t))
    v_sib.start()
    query(6)
    tick()
    v_sib.wait_recv()

    def v_chip(k):
        return rcopy(
            vch.at[chip], vch.at[chip], v_sem.at[0, k], v_sem.at[1, k], (peer(k), t)
        )

    vch[chip] = vec[...] + vsib_r[...]
    for k in range(1, nc):
        v_chip(k).start()
    t_sib.wait_recv()

    def t_chip(k):
        return rcopy(
            tch_s.at[k - 1], tch_r.at[k - 1], t_sem.at[0, k], t_sem.at[1, k], (peer(k), t)
        )

    for k in range(1, nc):
        dest = chip ^ k
        rows = pl.ds(pl.multiple_of((2 * dest + core) * kb, 8), kb)
        for m in range(2):
            tch_s[k - 1, m] = gtok[m, rows, :] + tsib_r[dest, m]
        t_chip(k).start()
    query(7)

    def as_row(values):
        totals = jnp.sum(values, axis=1, keepdims=True)
        at = lax.broadcasted_iota(jnp.int32, (values.shape[0], 128), 0)
        lane = lax.broadcasted_iota(jnp.int32, (values.shape[0], 128), 1)
        return jnp.sum(jnp.where(at == lane, totals, 0.0), axis=0, keepdims=True)

    zsm[t] = jnp.zeros((8, 128), F32)
    zsm[t, 0:1, :] = as_row(sqs[...]) / (2.0 * D * FF)
    for q in range(count - QRY_DEV):
        zsm[t, 1 + q : 2 + q, :] = as_row(infl[q]) * (2.0 * D * FF) ** (-0.5)

    def sm_copy(k):
        return rcopy(
            zsm.at[t], zsm.at[t], s_sem.at[0], s_sem.at[k], (me, (t + k) % 4)
        )

    for k in (1, 2, 3):
        sm_copy(k).start()

    tick()

    for m, out in enumerate((gwi_k, gwo_k)):
        out[...] = w_share(chip, m)
    for n in (1, 2):
        w_chip(n, first).wait_recv()
        for m, out in enumerate((gwi_k, gwo_k)):
            out[...] += wch_r[n, m].astype(F32)

    def act_copy(i):
        return pltpu.make_async_copy(act_s.at[i], act_o.at[i], out_sem.at[1])

    def act_rows(i, lo, hi):
        for b in range(lo, hi, 16):
            ro = slice(o_rows + i * last + b, o_rows + i * last + b + 16)
            a = xf[i * ROWS + b : i * ROWS + b + 16, :] + ztot[ro, :].astype(F32) + bs[1:2, :]
            act_s[i, b : b + 16, :] = a.astype(BF16)

    def act(i):
        *before, final = chunks_of(o_rows, i)
        cut = chunks[final][0] - o_rows - i * last
        tick(before[-1])
        zfin([seam + 1] * (i == 0) + before)
        act_rows(i, 0, cut)
        a = ztot[zrows(seam + 1), :].astype(F32)[tail * i : tail * (i + 1)] + bs[1:2, :]
        a = a + xf[i * ROWS + last : i * ROWS + patches, :]
        act_s[i, last:patches, :] = a.astype(BF16)
        tick(final)
        zfin([final])
        act_rows(i, cut, last)
        act_copy(i).start()

    act(0)
    tick()
    act(1)
    tick()

    for k in (1, 2, 3):
        sm_copy(k).wait_recv()
    sm_k[...] = (zsm[0] + zsm[1]) + (zsm[2] + zsm[3])
    rows = pl.ds(pl.multiple_of(me * kb, 8), kb)
    for m, out in enumerate((gti_k, gto_k)):
        out[...] = gtok[m, rows, :] + tsib_r[chip, m]
    for k in range(1, nc):
        t_chip(k).wait_recv()
        for m, out in enumerate((gti_k, gto_k)):
            out[...] += tch_r[k - 1, m]
    for k in range(1, nc):
        v_chip(k).wait_recv()
    total = vch[0]
    for c in range(1, nc):
        total = total + vch[c]
    tbo_k[...] = total[:, 0:256]
    vec_k[...] = pltpu.roll(total, (D - me * shard) % D, 1)[:, 0:128]
    stores = [(gwi_k, gwi_o), (gwo_k, gwo_o), (gti_k, gti_o), (gto_k, gto_o), (vec_k, vec_o), (tbo_k, tbo_o), (sm_k, sm_o)]
    stores = [pltpu.make_async_copy(a, b, small_sem.at[n]) for n, (a, b) in enumerate(stores)]
    for c in stores:
        c.start()
    act(count - 1)

    params.drain()
    dqs.drain()
    cqs.drain()

    @pl.when(end)
    def _():
        rcopy(zpart, zrx, z_sent.at[0], z_sem.at[0, 0], (me, end_peer)).wait_send()

    @pl.when(mid)
    def _():
        rcopy(zpair, zrxp, z_sent.at[1], z_sem.at[1, 0], (me, mid_peer)).wait_send()
        rcopy(ztot, ztot, z_sent.at[0], z_sem.at[0, 0], (me, mid_end)).wait_send()

    w_sib.wait_send()
    t_sib.wait_send()
    v_sib.wait_send()
    for k in range(1, nc):
        w_chip(k - 1, first).wait_send()
        t_chip(k).wait_send()
        v_chip(k).wait_send()
    z3 = zsm.at[pl.ds(0, 3)]
    rcopy(z3, z3, s_sem.at[0], s_sem.at[1], (me, (t + 1) % 4)).wait_send()
    for c in stores:
        c.wait()
    pltpu.make_async_copy(ing_s, ing_o, out_sem.at[0]).wait()
    pltpu.make_async_copy(act_s, act_o, out_sem.at[1]).wait()


def finish(shard, ks, patches, count, queries, act, ing, gwi, gwo, gti_h, gto_h, vec_h, tbo_h, sm_h, *refs):
    big, small, refs = refs[:4], refs[4:14], refs[14:]
    held, got, made = refs[:4], refs[4:9], refs[9:19]
    got_sem, load_sem, store_sem, made_sem = refs[19:23]
    pieces = [(n, i) for n in (0, 1) for i in range(count)] + [(2, None), (3, None)]

    def part(ref, i):
        return ref if i is None else ref.at[i]

    loads = [
        pltpu.make_async_copy(a, b, got_sem.at[n])
        for n, (a, b) in enumerate(zip((gti_h, gto_h, vec_h, tbo_h, sm_h), got))
    ]
    moves = []
    for n, i in pieces:
        kept, at = part(held[n], i), len(moves)
        moves.append(
            (
                pltpu.make_async_copy(part((act, ing, gwi, gwo)[n], i), kept, load_sem.at[at]),
                pltpu.make_async_copy(kept, part(big[n], i), store_sem.at[n]),
            )
        )
    for c in loads:
        c.start()
    for load, _ in moves:
        load.start()
    for c in loads:
        c.wait()
    gti, gto, vec, tbo, sm = got
    gains, shifts, gti_o, gto_o, gtb_o, tbo_o, gbi_o, gbo_o, sq_o, infl_o = made
    gains[...] = vec[0:2, 0:shard]
    shifts[...] = vec[2:4, 0:shard]
    gbo_o[...] = vec[4:5, 0:shard]
    gbi_o[...] = vec[5:6, 0:shard]
    gti_o[...] = gti[0:ks, 0:patches]
    gto_o[...] = gto[0:ks, 0:patches]
    tbo_o[...] = tbo[6:7, 0:patches]
    column = gti[0:ks, patches : patches + 1]
    eye = lax.broadcasted_iota(jnp.int32, (ks, ks), 0) == lax.broadcasted_iota(jnp.int32, (ks, ks), 1)
    gtb_o[...] = jnp.sum(jnp.where(eye, column, 0.0), axis=0, keepdims=True)
    sq_o[...] = sm[0:1, 0:count]
    for t in range(infl_o.shape[0]):
        infl_o[t : t + 1, :] = sm[1 + t : 2 + t, 0:queries]
    stores = [pltpu.make_async_copy(a, b, made_sem.at[n]) for n, (a, b) in enumerate(zip(made, small))]
    for c in stores:
        c.start()
    for load, store in moves:
        load.wait()
        store.start()
    for c in stores:
        c.wait()
    for n in range(4):
        pltpu.make_async_copy(held[n], big[n], store_sem.at[n]).wait()


def fused(
    n_dp,
    images,
    cotangent,
    norm_gains,
    norm_shifts,
    tok_in,
    tok_out_t,
    tok_bias_in,
    tok_bias_out,
    w_in,
    bias_in,
    w_out,
    bias_out,
):
    count, patches, width = images.shape
    nc = n_dp // 2
    ks = tok_in.shape[1]
    toks = ks * n_dp
    kb = -(-ks // 16) * 16
    K = n_dp * kb
    KA = K + 16
    KL = -(-KA // 128) * 128
    R = count * ROWS
    zrows, steps = sum(z_sizes(count)), len(z_sizes(count))
    shard = width // n_dp
    hidden = w_in.shape[1]
    anyspace = pl.BlockSpec(memory_space=pl.ANY)
    V = pltpu.VMEM
    dma = lambda *s: pltpu.SemaphoreType.DMA(s)
    scratch = dict(
        gwi_k=V((shard, hidden), F32),
        gwo_k=V((shard, hidden), F32),
        gti_k=V((kb, 256), F32),
        gto_k=V((kb, 256), F32),
        vec_k=V((8, 128), F32),
        tbo_k=V((8, 256), F32),
        sm_k=V((8, 128), F32),
        gains_r=V(norm_gains.shape, BF16),
        shifts_r=V(norm_shifts.shape, BF16),
        tok_in_r=V((ks, patches), BF16),
        tok_out_r=V((ks, patches), BF16),
        tok_bias_r=V(tok_bias_in.shape, BF16),
        tok_bias_out_r=V(tok_bias_out.shape, BF16),
        bias_in_r=V(bias_in.shape, BF16),
        bias_out_r=V(bias_out.shape, BF16),
        x_raw=V((count, patches, D), BF16),
        d_raw=V((count, patches, D), BF16),
        w_in=V((D, hidden), BF16),
        w_out=V((hidden, D), BF16),
        act_s=V((count, patches, D), BF16),
        ing_s=V((count, patches, D), BF16),
        pb=V((n_dp, 2 * kb + 16, 256), BF16),
        aug=V((ROWS, 128), F32),
        misc=V((16, 256), F32),
        toki_t=V((K, 256), BF16),
        toko_t=V((KA, 256), BF16),
        toki=V((ROWS, KL), BF16),
        toko=V((ROWS, KL), BF16),
        gs=V((16, D), F32),
        bs=V((8, D), F32),
        dout=V((R, D), BF16),
        dhid=V((R, hidden), F32),
        xf=V((R, D), F32),
        xh1=V((R, D), F32),
        rs1=V((R, 128), F32),
        xh2=V((R, D), F32),
        rs2=V((R, 128), F32),
        normed=V((R, D), BF16),
        th=V((count, KA, D), BF16),
        tgp=V((count, K, D), F32),
        chan=V((R, D), BF16),
        hid=V((R, hidden), BF16),
        dpre=V((R, hidden), BF16),
        tmp=V((max(K, 2 * ROWS), 256), F32),
        dq=V((n_dp, ROWS, D), BF16),
        cq=V((n_dp, ROWS, D), BF16),
        hq=V((ROWS, hidden), BF16),
        pq=V((ROWS, hidden), BF16),
        infl=V((count - QRY_DEV, n_dp, 256), F32),
        sqs=V((8, 256), F32),
        dmix=V((ROWS, D), BF16),
        dtok=V((K, D), BF16),
        dnorm=V((ROWS, D), F32),
        tails=V((count, 8, D), F32),
        rests=V((count, 16, D), F32),
        zpart=V((zrows, D), BF16),
        zrx=V((zrows, D), BF16),
        zpair=V((zrows, D), BF16),
        zrxp=V((zrows, D), BF16),
        ztot=V((zrows, D), BF16),
        gw=V((2, D, hidden), F32),
        wsib_s=V((nc, 2, shard, hidden), BF16),
        wsib_r=V((nc, 2, shard, hidden), BF16),
        wch_s=V((nc - 1, 2, shard, hidden), BF16),
        wch_r=V((nc - 1, 2, shard, hidden), BF16),
        gtok=V((2, KA, 256), F32),
        tsib_s=V((nc, 2, kb, 256), F32),
        tsib_r=V((nc, 2, kb, 256), F32),
        tch_s=V((nc - 1, 2, kb, 256), F32),
        tch_r=V((nc - 1, 2, kb, 256), F32),
        acc=V((6, 8, D), F32),
        vec=V((8, D), F32),
        vsib_r=V((8, D), F32),
        vch=V((nc, 8, D), F32),
        zsm=V((4, 8, 128), F32),
        in_sem=dma(12),
        out_sem=dma(2),
        small_sem=dma(7),
        pb_sem=dma(8),
        dq_sem=dma(8),
        cq_sem=dma(8),
        z_sem=dma(2, steps),
        z_sent=dma(2),
        w_sem=dma(2, nc),
        t_sem=dma(2, nc),
        v_sem=dma(2, nc),
        s_sem=dma(4),
    )
    outs = [
        (images.shape, BF16, anyspace),
        (images.shape, BF16, anyspace),
        ((shard, hidden), F32, anyspace),
        ((shard, hidden), F32, anyspace),
        ((kb, 256), F32, anyspace),
        ((kb, 256), F32, anyspace),
        ((8, 128), F32, anyspace),
        ((8, 256), F32, anyspace),
        ((8, 128), F32, anyspace),
    ]
    names = list(scratch)
    n_in, n_out = 12, len(outs)

    def body(*refs):
        mega(n_dp, count, patches, toks, *refs[: n_in + n_out], **dict(zip(names, refs[n_in + n_out :])))

    act, ing, gwi, gwo, gti, gto, vec, tbo, sm = pl.pallas_call(
        body,
        out_shape=[jax.ShapeDtypeStruct(s, d) for s, d, _ in outs],
        in_specs=[anyspace] * 12,
        out_specs=[o[2] for o in outs],
        scratch_shapes=list(scratch.values()),
        compiler_params=pltpu.CompilerParams(
            collective_id=0, has_side_effects=True, vmem_limit_bytes=60 * 2**20
        ),
        name="mixer",
    )(
        images,
        cotangent,
        w_in,
        w_out,
        norm_gains,
        norm_shifts,
        tok_in.T,
        tok_out_t.T,
        tok_bias_in,
        tok_bias_out,
        bias_in,
        bias_out,
    )
    queries, trains = n_dp * QRY_DEV, count - QRY_DEV
    shapes = [
        (images.shape, BF16),
        (images.shape, BF16),
        ((shard, hidden), F32),
        ((shard, hidden), F32),
        ((2, shard), F32),
        ((2, shard), F32),
        ((ks, patches), F32),
        ((ks, patches), F32),
        ((1, ks), F32),
        ((1, patches), F32),
        ((1, shard), F32),
        ((1, shard), F32),
        ((1, count), F32),
        ((trains, queries), F32),
    ]
    smalls = [(o.shape, F32) for o in (gti, gto, vec, tbo, sm)]
    out = pl.pallas_call(
        functools.partial(finish, shard, ks, patches, count, queries),
        out_shape=[jax.ShapeDtypeStruct(s, d) for s, d in shapes],
        in_specs=[anyspace] * 9,
        out_specs=[anyspace] * 14,
        scratch_shapes=[V(s, d) for s, d in shapes[:4] + smalls + shapes[4:]] + [dma(5), dma(2 * count + 2), dma(4), dma(10)],
        name="finish",
    )(act, ing, gwi, gwo, gti, gto, vec, tbo, sm)
    act, ing, gwi, gwo, gains, shifts, gti, gto, gtb, tbo, gbi, gbo, squares, influence = out
    return (
        act,
        ing,
        gains,
        shifts,
        gti.T,
        gto.T,
        gtb,
        tbo.reshape(patches),
        gwi,
        gbi.reshape(shard),
        gwo.T,
        gbo.reshape(shard),
        squares.reshape(count),
        influence.T,
    )


def layer_norm(values, gain, shift):
    center = values - jnp.mean(values, axis=-1, keepdims=True)
    spread = jnp.mean(center * center, axis=-1, keepdims=True)
    return center * lax.rsqrt(spread + 1e-06) * gain + shift


def smooth(values):
    return jax.nn.gelu(values, approximate=True)


def contract(left, right, left_dim, right_dim):
    return lax.dot_general(
        left, right, (((left_dim,), (right_dim,)), ((), ())), preferred_element_type=jnp.float32
    )


def per_device(
    images,
    cotangent,
    norm_gains,
    norm_shifts,
    tok_in,
    tok_out_t,
    tok_bias_in,
    tok_bias_out,
    w_in,
    bias_in,
    w_out,
    bias_out,
):
    gains, shifts, tok_first, tok_second, tok_bias = (
        lax.all_gather(norm_gains, "dp", axis=1, tiled=True),
        lax.all_gather(norm_shifts, "dp", axis=1, tiled=True),
        lax.all_gather(tok_in, "dp", axis=1, tiled=True),
        lax.all_gather(tok_out_t, "dp", axis=1, tiled=True),
        lax.all_gather(tok_bias_in, "dp", axis=1, tiled=True),
    )
    gains = gains.astype(jnp.float32)
    shifts = shifts.astype(jnp.float32)
    count, patches, width = images.shape
    rows = count * patches
    inputs = images.astype(jnp.float32)
    normed_one, first_back = jax.vjp(layer_norm, inputs, gains[0], shifts[0])
    normed_low = normed_one.astype(jnp.bfloat16)
    tok_pre = (
        jnp.einsum("sk,nsd->nkd", tok_first, normed_low, preferred_element_type=jnp.float32)
        + tok_bias[0].astype(jnp.float32)[None, :, None]
    )
    tok_hidden = smooth(tok_pre).astype(jnp.bfloat16)
    tok_mixed = (
        jnp.einsum("sk,nkd->nsd", tok_second, tok_hidden, preferred_element_type=jnp.float32)
        + tok_bias_out.astype(jnp.float32)[None, :, None]
    )
    resid = inputs + tok_mixed
    normed_two, second_back = jax.vjp(layer_norm, resid, gains[1], shifts[1])
    chan_in = normed_two.astype(jnp.bfloat16).reshape(rows, width)
    chan_pre = jnp.dot(chan_in, w_in, preferred_element_type=jnp.float32) + bias_in.astype(
        jnp.float32
    )
    hidden = smooth(chan_pre).astype(jnp.bfloat16)
    partial_out = jnp.dot(hidden, w_out, preferred_element_type=jnp.float32)
    mixed = lax.psum(partial_out, "tensor")
    activations = (
        resid + mixed.reshape(count, patches, width) + bias_out.astype(jnp.float32)
    ).astype(jnp.bfloat16)
    dout_rows = cotangent.reshape(rows, width)
    d_hidden = contract(dout_rows, w_out, 1, 1)
    smooth_value, smooth_back = jax.vjp(smooth, chan_pre)
    d_pre = smooth_back(d_hidden)[0].astype(jnp.bfloat16)
    d_chan_part = contract(d_pre, w_in, 1, 1)
    d_chan = lax.psum(d_chan_part, "tensor")
    d_resid_norm, d_gain_two, d_shift_two = second_back(d_chan.reshape(count, patches, width))
    d_resid = cotangent.astype(jnp.float32) + d_resid_norm
    d_mixed = d_resid.astype(jnp.bfloat16)
    d_tokhid = jnp.einsum("sk,nsd->nkd", tok_second, d_mixed, preferred_element_type=jnp.float32)
    tok_value, tok_back = jax.vjp(smooth, tok_pre)
    d_tokpre = tok_back(d_tokhid)[0].astype(jnp.bfloat16)
    grad_second = jnp.einsum("nsd,nkd->sk", d_mixed, tok_hidden, preferred_element_type=jnp.float32)
    grad_first = jnp.einsum("nsd,nkd->sk", normed_low, d_tokpre, preferred_element_type=jnp.float32)
    grad_tbias = jnp.sum(d_tokpre, axis=(0, 2), dtype=jnp.float32)[None, :]
    grad_tbias_out = jnp.sum(d_mixed, axis=(0, 2), dtype=jnp.float32)
    d_normed = jnp.einsum("sk,nkd->nsd", tok_first, d_tokpre, preferred_element_type=jnp.float32)
    d_input_norm, d_gain_one, d_shift_one = first_back(d_normed)
    input_grad = (d_resid + d_input_norm).astype(jnp.bfloat16)
    grad_win = contract(chan_in, d_pre, 0, 0)
    grad_wout_t = contract(dout_rows, hidden, 0, 0)
    grad_bin = jnp.sum(d_pre, axis=0, dtype=jnp.float32)
    grad_bout = jnp.sum(dout_rows, axis=0, dtype=jnp.float32)
    share_win, share_wout_t, share_bin, share_bout = (
        lax.psum_scatter(grad_win, "dp", scatter_dimension=0, tiled=True),
        lax.psum_scatter(grad_wout_t, "dp", scatter_dimension=0, tiled=True),
        lax.psum_scatter(grad_bin, "dp", scatter_dimension=0, tiled=True),
        lax.psum_scatter(grad_bout, "dp", scatter_dimension=0, tiled=True),
    )
    share_gains, share_shifts, share_first, share_second, share_tbias = (
        lax.psum_scatter(
            jnp.stack([d_gain_one, d_gain_two]), "dp", scatter_dimension=1, tiled=True
        ),
        lax.psum_scatter(
            jnp.stack([d_shift_one, d_shift_two]), "dp", scatter_dimension=1, tiled=True
        ),
        lax.psum_scatter(grad_first, "dp", scatter_dimension=1, tiled=True),
        lax.psum_scatter(grad_second, "dp", scatter_dimension=1, tiled=True),
        lax.psum_scatter(grad_tbias, "dp", scatter_dimension=1, tiled=True),
    )
    total_tbias_out = lax.psum(grad_tbias_out, "dp")
    chan_cube = chan_in.reshape(count, patches, width)
    pre_cube = d_pre.reshape(count, patches, -1)
    hidden_cube = hidden.reshape(count, patches, -1)
    def against(chan, pre, dout, low):
        grams = [
            jnp.einsum("sd,npd->nsp", a, b, preferred_element_type=jnp.float32)
            for a, b in ((chan, chan_cube), (pre, pre_cube), (dout, cotangent), (low, hidden_cube))
        ]
        return jnp.sum(grams[0] * grams[1] + grams[2] * grams[3], axis=(1, 2))

    own = lax.map(lambda a: against(*a), (chan_cube, pre_cube, cotangent, hidden_cube))
    squares = jnp.diagonal(own)
    queries = tuple(
        lax.all_gather(a[:QRY_DEV], "dp", axis=0, tiled=True)
        for a in (chan_cube, pre_cube, cotangent, hidden_cube)
    )
    influence = lax.map(lambda a: against(*a), queries)[:, QRY_DEV:]
    influence, squares = lax.psum((influence, squares), "tensor")
    sqnorms = squares / (2.0 * D * FF)
    influence = influence * (2.0 * D * FF) ** (-0.5)
    return (
        activations,
        input_grad,
        share_gains,
        share_shifts,
        share_first,
        share_second,
        share_tbias,
        total_tbias_out,
        share_win,
        share_bin,
        share_wout_t.T,
        share_bout,
        sqnorms,
        influence,
    )


def solution(mesh):
    placed = (
        P("dp", None, None),
        P("dp", None, None),
        P(None, "dp"),
        P(None, "dp"),
        P(None, "dp"),
        P(None, "dp"),
        P(None, "dp"),
        P(),
        P(None, "tensor"),
        P("tensor"),
        P("tensor", None),
        P(),
    )
    n_dp = mesh.shape["dp"]
    fits = n_dp == 8 and mesh.shape["tensor"] == 4
    device = functools.partial(fused, n_dp) if fits else per_device
    return jax.shard_map(
        device,
        mesh=mesh,
        in_specs=placed,
        out_specs=(
            P("dp", None, None),
            P("dp", None, None),
            P(None, "dp"),
            P(None, "dp"),
            P(None, "dp"),
            P(None, "dp"),
            P(None, "dp"),
            P(),
            P("dp", "tensor"),
            P(("tensor", "dp")),
            P("tensor", "dp"),
            P("dp"),
            P("dp"),
            P(None, "dp"),
        ),
        check_vma=False,
    )
```
